128 devices in a mesh: ha: 8 (over z, core), wa: 16 (over y, x).
Axes of the slice: x: 4, y: 4, z: 4, core: 2. Of those that a mesh axis runs over, the one named last changes fastest.
Arguments:
- frames_in: bfloat16 [1, 240, 640, 128], P(None, 'ha', 'wa'), may hold values from -6 to 6
- cache_in: bfloat16 [2, 240, 640, 128], P(None, 'ha', 'wa'), may hold values from -6 to 6
- cache_mid: bfloat16 [2, 240, 640, 128], P(None, 'ha', 'wa'), may hold values from -6 to 6
- w_first: bfloat16 [3, 3, 3, 128, 128], replicated, may hold values from -0.109375 to 0.109375
- w_second: bfloat16 [3, 3, 3, 128, 128], replicated, may hold values from -0.109375 to 0.109375
- scale_first: float32 [1, 128], replicated, may hold values from -0.5 to 0.5
- shift_first: float32 [1, 128], replicated, may hold values from -3 to 3
- scale_second: float32 [1, 128], replicated, may hold values from -0.5 to 0.5
- shift_second: float32 [1, 128], replicated, may hold values from -3 to 3
- cotangent: bfloat16 [1, 240, 640, 128], P(None, 'ha', 'wa'), may hold values from -6 to 6
Outputs:
- grad_input: bfloat16 [1, 240, 640, 128], P(None, 'ha', 'wa')
- grad_first: float32 [3, 3, 3, 128, 128], replicated
- grad_second: float32 [3, 3, 3, 128, 128], replicated
The draws below stay inside these ranges and needn't reach their ends.
All inputs are finite; a program needn't handle non-finite values.
Results may differ from the reference program's by a relative error of at most 0.0058.
Values may be sent and summed in bfloat16 or wider, within the bound.
No kernel may reach another device: no remote copies, remote signals or barrier semaphores. Data moves between devices by JAX's collectives and lax.ppermute only.
A program may use at most 128 MiB of HBM per device.

```python
import jax
import jax.numpy as jnp

C = 128
F = 1
CACHE = 2
H = 240
W = 640


def block_scale(rng, shape, shards, low, top_value):
    factor_of, own = 1.0, jax.random.fold_in(rng, 6)
    for axis_at, shards_of in shards:
        draws = jnp.exp(jax.random.uniform(jax.random.fold_in(own, axis_at), (shards_of,), jnp.float32, low / len(shards), top_value / len(shards)))
        factor_of = factor_of * jnp.repeat(draws, shape[axis_at] // shards_of).reshape([-1 if axis == axis_at else 1 for axis in range(len(shape))])
    return factor_of


def noise(rng, dims, scale, reach, split=(), held_as=jnp.bfloat16):
    drawn = jax.random.normal(rng, dims, jnp.float32) * scale
    if len(split) > 0:
        drawn = block_scale(rng, dims, split, -0.22, 0.18) * drawn
    return jnp.clip(drawn, min=-reach, max=reach).astype(held_as)


def setup_inputs(seed: int = 0) -> dict:
    keys = jax.random.split(jax.random.key(seed), 11)
    frames_in = noise(keys[0], (F, H, W, C), 1.0, 6.0, ((1, 8), (2, 16)))
    cache_in = noise(keys[1], (CACHE, H, W, C), 1.0, 6.0, ((1, 8), (2, 16)))
    cache_mid = noise(keys[2], (CACHE, H, W, C), 1.0, 6.0, ((1, 8), (2, 16)))
    w_first = noise(keys[3], (3, 3, 3, C, C), (27 * C) ** -0.5, 0.109375)
    w_second = noise(keys[4], (3, 3, 3, C, C), (27 * C) ** -0.5, 0.109375)
    scale_first = jnp.clip(jax.random.uniform(keys[5], (F, C), jnp.float32, -0.5, 0.5), -0.5, 0.5)
    shift_first = noise(keys[6], (F, C), 0.5, 3.0, (), jnp.float32)
    scale_second = jnp.clip(jax.random.uniform(keys[7], (F, C), jnp.float32, -0.5, 0.5), -0.5, 0.5)
    shift_second = noise(keys[8], (F, C), 0.5, 3.0, (), jnp.float32)
    cotangent = noise(keys[9], (F, H, W, C), 1.0, 6.0, ((1, 8), (2, 16)))
    return dict(frames_in=frames_in, cache_in=cache_in, cache_mid=cache_mid, w_first=w_first, w_second=w_second, scale_first=scale_first, shift_first=shift_first, scale_second=scale_second, shift_second=shift_second, cotangent=cotangent)


def convolve(padded, kernel, frames, rows, cols):
    chans = padded.shape[-1]
    total = jnp.zeros((frames * rows * cols, kernel.shape[-1]), jnp.float32)
    for depth in range(3):
        for vert in range(3):
            block = jnp.concatenate([padded[depth:depth + frames, vert:vert + rows, horiz:horiz + cols, :] for horiz in range(3)], axis=-1)
            block = block.reshape(frames * rows * cols, 3 * chans)
            total = total + jnp.dot(block, kernel[depth, vert].reshape(3 * chans, kernel.shape[-1]), preferred_element_type=jnp.float32)
    return total.reshape(frames, rows, cols, kernel.shape[-1])

def kernel_grad(padded, grad_out, frames, rows, cols):
    chans = padded.shape[-1]
    flat_grad = grad_out.reshape(frames * rows * cols, grad_out.shape[-1])
    pieces = []
    for depth in range(3):
        for vert in range(3):
            block = jnp.concatenate([padded[depth:depth + frames, vert:vert + rows, horiz:horiz + cols, :] for horiz in range(3)], axis=-1)
            block = block.reshape(frames * rows * cols, 3 * chans)
            pieces.append(jax.lax.dot_general(block, flat_grad, (((0,), (0,)), ((), ())), preferred_element_type=jnp.float32).reshape(3, chans, chans))
    return jnp.stack(pieces).reshape(3, 3, 3, chans, chans)

def flipped(kernel):
    return jnp.swapaxes(kernel[::-1, ::-1, ::-1], 3, 4)

def silu_slope(value):
    sig = jax.nn.sigmoid(value)
    return sig * (1.0 + value * (1.0 - sig))

def pad_space(field):
    return jnp.pad(field, ((0, 0), (1, 1), (1, 1), (0, 0)))

def reference(frames_in, cache_in, cache_mid, w_first, w_second, scale_first, shift_first, scale_second, shift_second, cotangent):
    frames, rows, cols, chans = frames_in.shape
    factor = 1.0 / (frames * rows * cols) ** 0.5
    padded_in = pad_space(jnp.concatenate([cache_in, frames_in], axis=0))
    m_one = convolve(padded_in, w_first, frames, rows, cols) * (1.0 + scale_first[:, None, None, :]) + shift_first[:, None, None, :]
    a_one = jax.nn.silu(m_one).astype(jnp.bfloat16)
    padded_mid = pad_space(jnp.concatenate([cache_mid, a_one], axis=0))
    m_two = convolve(padded_mid, w_second, frames, rows, cols) * (1.0 + scale_second[:, None, None, :]) + shift_second[:, None, None, :]
    d_two = (cotangent.astype(jnp.float32) * silu_slope(m_two) * (1.0 + scale_second[:, None, None, :])).astype(jnp.bfloat16)
    grad_second = kernel_grad(padded_mid, d_two, frames, rows, cols) * factor
    tail = jnp.zeros((2, rows, cols, chans), jnp.bfloat16)
    g_one = convolve(pad_space(jnp.concatenate([d_two, tail], axis=0)), flipped(w_second), frames, rows, cols)
    d_one = (g_one * silu_slope(m_one) * (1.0 + scale_first[:, None, None, :])).astype(jnp.bfloat16)
    grad_first = kernel_grad(padded_in, d_one, frames, rows, cols) * factor
    grad_input = convolve(pad_space(jnp.concatenate([d_one, tail], axis=0)), flipped(w_first), frames, rows, cols).astype(jnp.bfloat16)
    return (grad_input, grad_first, grad_second)
```

```python
import jax
import jax.numpy as jnp
from jax import lax
from jax.experimental import pallas as pl
from jax.experimental.pallas import tpu as pltpu
from jax.sharding import PartitionSpec as P

BF = jnp.bfloat16
F32 = jnp.float32
RIM = 4
BOTH = ("ha", "wa")


def shift(axis, step):
    count = lax.axis_size(axis)
    return [(i, i + step) for i in range(count) if 0 <= i + step < count]


def slope(value):
    sig = jax.nn.sigmoid(value)
    return sig * (1.0 + value * (1.0 - sig))


def chain_kernel(
    rows, cols, wide, low, high, w_one, w_two, sc_one, sh_one, sc_two, sh_two,
    gin, grads, field, wv_one, wv_two, slope_one, a_one, d_two, d_one, moved, sems,
):
    full, lanes = cols + 2 * RIM, field.shape[-1]
    tall = rows + 2 * RIM
    copies = [
        pltpu.make_async_copy(wide, field.at[:, RIM : RIM + rows], sems.at[0]),
        pltpu.make_async_copy(low, field.at[:, 0:RIM], sems.at[1]),
        pltpu.make_async_copy(high, field.at[:, RIM + rows : tall], sems.at[2]),
        pltpu.make_async_copy(w_one, wv_one, sems.at[3]),
        pltpu.make_async_copy(w_two, wv_two, sems.at[4]),
    ]
    for copy in copies:
        copy.start()
    for copy in copies[:4]:
        copy.wait()

    ha, wa = lax.axis_index("ha"), lax.axis_index("wa")
    image_rows, image_cols = rows * lax.axis_size("ha"), cols * lax.axis_size("wa")
    col = lax.broadcasted_iota(jnp.int32, (1, full, lanes), 1)
    own_col = col < cols
    place = jnp.where(col < cols + RIM, col, col - full) + wa * cols
    col_in = (place >= 0) & (place < image_cols)

    def in_image(start, count):
        row = lax.broadcasted_iota(jnp.int32, (count, full, lanes), 0) + (start - RIM) + ha * rows
        return (row >= 0) & (row < image_rows) & col_in

    def roll(value, step):
        return pltpu.roll(value, step % full, 1)

    def forward(piece, weight, start, count):
        lhs = jnp.concatenate(
            [piece(a, start - 1 + b, count) for a in range(3) for b in range(3)], axis=1
        )
        rhs = jnp.concatenate(
            [
                jnp.concatenate([weight[a, b, c] for c in range(3)], axis=1)
                for a in range(3)
                for b in range(3)
            ],
            axis=0,
        )
        out = jnp.dot(lhs, rhs, preferred_element_type=F32).reshape(count, full, 3 * lanes)
        return (
            roll(out[..., :lanes], 1)
            + out[..., lanes : 2 * lanes]
            + roll(out[..., 2 * lanes :], -1)
        )

    def backward(piece, weight, start, count):
        lhs = jnp.concatenate([piece(start + 1 - b, count) for b in range(3)], axis=1)
        rhs = jnp.concatenate(
            [jnp.concatenate([weight[2, b, c] for b in range(3)], axis=1) for c in range(3)],
            axis=0,
        )
        out = lax.dot_general(
            lhs, rhs, (((1,), (1,)), ((), ())), preferred_element_type=F32
        ).reshape(count, full, 3 * lanes)
        return (
            roll(out[..., :lanes], -1)
            + out[..., lanes : 2 * lanes]
            + roll(out[..., 2 * lanes :], 1)
        )

    def flat(value):
        return value.reshape(-1, lanes)

    def gradient(which, source):
        lhs = jnp.concatenate([source(a) for a in range(3)], axis=1)
        for b in range(3):
            rhs = moved[2 - b : 2 - b + rows + 2].reshape(-1, 3 * lanes)
            out = lax.dot_general(
                lhs, rhs, (((0,), (0,)), ((), ())), preferred_element_type=F32
            )
            for a in range(3):
                for c in range(3):
                    at = (((which * 3 + a) * 3 + b) * 3 + c) * lanes
                    grads[at : at + lanes, :] = out[
                        a * lanes : (a + 1) * lanes, c * lanes : (c + 1) * lanes
                    ].astype(BF)

    def spread(value, start, count):
        kept = jnp.where(own_col, value, 0.0)
        at = start - 2
        moved[at : at + count, :, :lanes] = roll(kept, -1).astype(BF)
        moved[at : at + count, :, lanes : 2 * lanes] = kept.astype(BF)
        moved[at : at + count, :, 2 * lanes :] = roll(kept, 1).astype(BF)

    zero_rows = jnp.zeros((2, full, 3 * lanes), BF)
    moved[0:2] = zero_rows
    moved[rows + 2 : rows + 4] = zero_rows

    gain_one = (1.0 + sc_one[...]).reshape(1, 1, lanes)
    gain_two = (1.0 + sc_two[...]).reshape(1, 1, lanes)
    bias_one = sh_one[...].reshape(1, 1, lanes)
    bias_two = sh_two[...].reshape(1, 1, lanes)
    step = (tall - 2) // 3
    for start in range(1, tall - 1, step):
        count = min(step, tall - 1 - start)
        m_one = (
            forward(lambda a, r, n: flat(field[a, r : r + n]), wv_one, start, count) * gain_one
            + bias_one
        )
        sig = jax.nn.sigmoid(m_one)
        inside = in_image(start, count)
        a_one[start : start + count] = jnp.where(inside, m_one * sig, 0.0).astype(BF)
        slope_one[start : start + count] = jnp.where(
            inside, sig * (1.0 + m_one * (1.0 - sig)) * gain_one, 0.0
        )

    copies[4].wait()

    def mid(a, r, n):
        return flat(a_one[r : r + n] if a == 2 else field[3 + a, r : r + n])

    step = (tall - 4) // 2
    for start in range(2, tall - 2, step):
        count = min(step, tall - 2 - start)
        m_two = forward(mid, wv_two, start, count) * gain_two + bias_two
        value = field[5, start : start + count].astype(F32) * slope(m_two) * gain_two
        d_two[start : start + count] = value.astype(BF)
        low_at, high_at = max(start, RIM), min(start + count, RIM + rows)
        spread(value[low_at - start : high_at - start], low_at, high_at - low_at)

    gradient(1, lambda a: mid(a, 3, rows + 2))

    step = (tall - 6) // 2
    for start in range(3, tall - 3, step):
        count = min(step, tall - 3 - start)
        value = (
            backward(lambda r, n: flat(d_two[r : r + n]), wv_two, start, count)
            * slope_one[start : start + count]
        )
        d_one[start : start + count] = value.astype(BF)
        low_at, high_at = max(start, RIM), min(start + count, RIM + rows)
        spread(value[low_at - start : high_at - start], low_at, high_at - low_at)

    gradient(0, lambda a: flat(field[a, 3 : 3 + rows + 2]))

    step = rows // 2
    for start in range(RIM, RIM + rows, step):
        count = min(step, RIM + rows - start)
        value = backward(lambda r, n: flat(d_one[r : r + n]), wv_one, start, count)
        gin[0, start - RIM : start - RIM + count] = value[:, :cols].astype(BF)

    used = 54 * lanes
    if grads.shape[0] > used:
        grads[used:, :] = jnp.zeros((grads.shape[0] - used, lanes), BF)


def per_device(
    frames_in, cache_in, cache_mid, w_first, w_second,
    scale_first, shift_first, scale_second, shift_second, cotangent,
):
    _, rows, cols, chans = frames_in.shape
    devices = lax.axis_size("ha") * lax.axis_size("wa")
    factor = 1.0 / (rows * cols * devices) ** 0.5
    own = jnp.concatenate([cache_in, frames_in, cache_mid, cotangent], axis=0)
    from_left = lax.ppermute(own[:, :, cols - RIM :], "wa", shift("wa", 1))
    from_right = lax.ppermute(own[:, :, :RIM], "wa", shift("wa", -1))
    wide = jnp.concatenate([own, from_right, from_left], axis=2)
    low = lax.ppermute(wide[:, rows - RIM :], "ha", shift("ha", 1))
    high = lax.ppermute(wide[:, :RIM], "ha", shift("ha", -1))

    full, tall = cols + 2 * RIM, rows + 2 * RIM
    total = 2 * 27 * chans
    share = -(-total // (8 * devices)) * 8
    anywhere = pl.BlockSpec(memory_space=pl.ANY)
    inner = pl.BlockSpec(memory_space=pltpu.VMEM)

    def body(*refs):
        chain_kernel(rows, cols, *refs)

    grad_input, grads = pl.pallas_call(
        body,
        out_shape=(
            jax.ShapeDtypeStruct((1, rows, cols, chans), BF),
            jax.ShapeDtypeStruct((share * devices, chans), BF),
        ),
        in_specs=[anywhere] * 5 + [inner] * 4,
        out_specs=(inner, inner),
        scratch_shapes=[
            pltpu.VMEM((6, tall, full, chans), BF),
            pltpu.VMEM((3, 3, 3, chans, chans), BF),
            pltpu.VMEM((3, 3, 3, chans, chans), BF),
            pltpu.VMEM((tall, full, chans), F32),
            pltpu.VMEM((tall, full, chans), BF),
            pltpu.VMEM((tall, full, chans), BF),
            pltpu.VMEM((tall, full, chans), BF),
            pltpu.VMEM((rows + 4, full, 3 * chans), BF),
            pltpu.SemaphoreType.DMA((5,)),
        ],
        compiler_params=pltpu.CompilerParams(vmem_limit_bytes=56 * 1024 * 1024),
        name="chain",
    )(wide, low, high, w_first, w_second, scale_first, shift_first, scale_second, shift_second)

    parts = lax.all_to_all(grads.reshape(devices, share, chans), BOTH, 0, 0, tiled=True)
    mine = (jnp.sum(parts.astype(F32), axis=0) * factor).astype(BF)
    every = lax.all_to_all(
        jnp.broadcast_to(mine[None], (devices, share, chans)), BOTH, 0, 0, tiled=True
    )
    every = every.reshape(share * devices, chans)
    half = total // 2
    shape = (3, 3, 3, chans, chans)
    grad_first = every[:half].astype(F32).reshape(shape)
    grad_second = every[half:total].astype(F32).reshape(shape)
    return (grad_input, grad_first, grad_second)


def solution(mesh):
    tiled = P(None, "ha", "wa", None)
    return jax.shard_map(
        per_device,
        mesh=mesh,
        in_specs=(tiled, tiled, tiled, P(), P(), P(), P(), P(), P(), tiled),
        out_specs=(tiled, P(), P()),
        check_vma=False,
    )
```

```python
import jax
import jax.numpy as jnp
from jax import lax
from jax.experimental import pallas as pl
from jax.experimental.pallas import tpu as pltpu
from jax.sharding import PartitionSpec as P

BF = jnp.bfloat16
F32 = jnp.float32
RIM = 4
BOTH = ("ha", "wa")


def swaps(axis):
    count = lax.axis_size(axis)
    first = [(i, i ^ 1) for i in range(count)]
    second = [(i, i + 1 if i % 2 else i - 1) for i in range(1, count - 1)]
    return first, second


def trade(axis, head, tail):
    odd = lax.axis_index(axis) % 2 == 1
    first, second = swaps(axis)
    near = lax.ppermute(jnp.where(odd, head, tail), axis, first)
    far = lax.ppermute(jnp.where(odd, tail, head), axis, second)
    return near, far


def slope(value):
    sig = jax.nn.sigmoid(value)
    return sig * (1.0 + value * (1.0 - sig))


def chain_kernel(
    rows, cols, cache_in, frames_in, cache_mid, cot, row_near, row_far, col_near, col_far,
    w_one, w_two, sc_one, sh_one, sc_two, sh_two,
    gin, keep, send, field, slope_one, a_one, d_two, d_one, moved, grads, sems,
):
    full, lanes = cols + 2 * RIM, field.shape[-1]
    tall = rows + 2 * RIM
    ha, wa = lax.axis_index("ha"), lax.axis_index("wa")
    odd_row, odd_col = ha % 2 == 1, wa % 2 == 1
    core = ha % 2

    def pick(odd, one, other):
        return jnp.where(odd, one.astype(F32), other.astype(F32))

    def assemble(frame, top, block, at):
        count, high = block.shape[:2]
        size = count * high * RIM
        near, far = col_near[at : at + size], col_far[at : at + size]
        left = pick(odd_col, near, far).reshape(-1, 2 * RIM, lanes)
        right = pick(odd_col, far, near).reshape(-1, 2 * RIM, lanes)
        lower = lax.broadcasted_iota(jnp.int32, left.shape, 1) < RIM
        rim = jnp.stack(
            [
                jnp.where(lower, right, pltpu.roll(left, RIM, 1)),
                jnp.where(lower, pltpu.roll(right, RIM, 1), left),
            ],
            axis=1,
        ).reshape(count, high, 2 * RIM, lanes)
        field[frame : frame + count, top : top + high] = jnp.concatenate(
            [block, rim], axis=2
        ).astype(BF)

    own_strip, corner = rows * RIM, RIM * RIM
    for frame, source in ((0, cache_in), (2, frames_in), (3, cache_mid), (5, cot)):
        assemble(frame, RIM, source[...].astype(F32), frame * own_strip)
    near_at, far_at = 6 * own_strip, 6 * (own_strip + corner)
    near_block, far_block = row_near[...].astype(F32), row_far[...].astype(F32)

    @pl.when(odd_row)
    def _():
        assemble(0, 0, near_block, near_at)
        assemble(0, RIM + rows, far_block, far_at)

    @pl.when(jnp.logical_not(odd_row))
    def _():
        assemble(0, 0, far_block, far_at)
        assemble(0, RIM + rows, near_block, near_at)

    image_rows, image_cols = rows * lax.axis_size("ha"), cols * lax.axis_size("wa")
    col = lax.broadcasted_iota(jnp.int32, (1, full, lanes), 1)
    own_col = col < cols
    place = jnp.where(col < cols + RIM, col, col - full) + wa * cols
    col_in = (place >= 0) & (place < image_cols)

    def in_image(start, count):
        row = lax.broadcasted_iota(jnp.int32, (count, full, lanes), 0) + (start - RIM) + ha * rows
        return (row >= 0) & (row < image_rows) & col_in

    def roll(value, step):
        return pltpu.roll(value, step % full, 1)

    def forward(piece, weight, start, count):
        lhs = jnp.concatenate(
            [piece(a, start - 1 + b, count) for a in range(3) for b in range(3)], axis=1
        )
        rhs = jnp.concatenate(
            [
                jnp.concatenate([weight[a, b, c] for c in range(3)], axis=1)
                for a in range(3)
                for b in range(3)
            ],
            axis=0,
        )
        out = jnp.dot(lhs, rhs, preferred_element_type=F32).reshape(count, full, 3 * lanes)
        return (
            roll(out[..., :lanes], 1)
            + out[..., lanes : 2 * lanes]
            + roll(out[..., 2 * lanes :], -1)
        )

    def backward(piece, weight, start, count):
        lhs = jnp.concatenate([piece(start + 1 - b, count) for b in range(3)], axis=1)
        rhs = jnp.concatenate(
            [jnp.concatenate([weight[2, b, c] for b in range(3)], axis=1) for c in range(3)],
            axis=0,
        )
        out = lax.dot_general(
            lhs, rhs, (((1,), (1,)), ((), ())), preferred_element_type=F32
        ).reshape(count, full, 3 * lanes)
        return (
            roll(out[..., :lanes], -1)
            + out[..., lanes : 2 * lanes]
            + roll(out[..., 2 * lanes :], 1)
        )

    def flat(value):
        return value.reshape(-1, lanes)

    def gradient(which, source):
        lhs = jnp.concatenate([source(a) for a in range(3)], axis=1)
        for b in range(3):
            rhs = moved[2 - b : 2 - b + rows + 2].reshape(-1, 3 * lanes)
            out = lax.dot_general(
                lhs, rhs, (((0,), (0,)), ((), ())), preferred_element_type=F32
            )
            for a in range(3):
                for c in range(3):
                    at = ((a * 3 + b) * 3 + c) * lanes
                    grads[which, at : at + lanes, :] = out[
                        a * lanes : (a + 1) * lanes, c * lanes : (c + 1) * lanes
                    ].astype(BF)

    def spread(value, start, count):
        kept = jnp.where(own_col, value, 0.0)
        at = start - 2
        moved[at : at + count, :, :lanes] = roll(kept, -1).astype(BF)
        moved[at : at + count, :, lanes : 2 * lanes] = kept.astype(BF)
        moved[at : at + count, :, 2 * lanes :] = roll(kept, 1).astype(BF)

    zero_rows = jnp.zeros((2, full, 3 * lanes), BF)
    moved[0:2] = zero_rows
    moved[rows + 2 : rows + 4] = zero_rows
    used = 27 * lanes
    if grads.shape[1] > used:
        grads[:, used:, :] = jnp.zeros((2, grads.shape[1] - used, lanes), BF)

    gain_one = (1.0 + sc_one[...]).reshape(1, 1, lanes)
    gain_two = (1.0 + sc_two[...]).reshape(1, 1, lanes)
    bias_one = sh_one[...].reshape(1, 1, lanes)
    bias_two = sh_two[...].reshape(1, 1, lanes)
    step = (tall - 2) // 3
    for start in range(1, tall - 1, step):
        count = min(step, tall - 1 - start)
        m_one = (
            forward(lambda a, r, n: flat(field[a, r : r + n]), w_one, start, count) * gain_one
            + bias_one
        )
        sig = jax.nn.sigmoid(m_one)
        inside = in_image(start, count)
        a_one[start : start + count] = jnp.where(inside, m_one * sig, 0.0).astype(BF)
        slope_one[start : start + count] = jnp.where(
            inside, sig * (1.0 + m_one * (1.0 - sig)) * gain_one, 0.0
        )

    def mid(a, r, n):
        return flat(a_one[r : r + n] if a == 2 else field[3 + a, r : r + n])

    step = (tall - 4) // 2
    for start in range(2, tall - 2, step):
        count = min(step, tall - 2 - start)
        m_two = forward(mid, w_two, start, count) * gain_two + bias_two
        value = field[5, start : start + count].astype(F32) * slope(m_two) * gain_two
        d_two[start : start + count] = value.astype(BF)
        low_at, high_at = max(start, RIM), min(start + count, RIM + rows)
        spread(value[low_at - start : high_at - start], low_at, high_at - low_at)

    gradient(1, lambda a: mid(a, 3, rows + 2))

    step = (tall - 6) // 2
    for start in range(3, tall - 3, step):
        count = min(step, tall - 3 - start)
        value = (
            backward(lambda r, n: flat(d_two[r : r + n]), w_two, start, count)
            * slope_one[start : start + count]
        )
        d_one[start : start + count] = value.astype(BF)
        low_at, high_at = max(start, RIM), min(start + count, RIM + rows)
        spread(value[low_at - start : high_at - start], low_at, high_at - low_at)

    gradient(0, lambda a: flat(field[a, 3 : 3 + rows + 2]))
    out_copies = [
        pltpu.make_async_copy(grads.at[core], keep, sems.at[0]),
        pltpu.make_async_copy(grads.at[1 - core], send, sems.at[1]),
    ]
    for copy in out_copies:
        copy.start()

    step = rows // 2
    for start in range(RIM, RIM + rows, step):
        count = min(step, RIM + rows - start)
        value = backward(lambda r, n: flat(d_one[r : r + n]), w_one, start, count)
        gin[0, start - RIM : start - RIM + count] = value[:, :cols].astype(BF)

    for copy in out_copies:
        copy.wait()


def per_device(
    frames_in, cache_in, cache_mid, w_first, w_second,
    scale_first, shift_first, scale_second, shift_second, cotangent,
):
    _, rows, cols, chans = frames_in.shape
    devices = lax.axis_size("ha") * lax.axis_size("wa")
    factor = 1.0 / (rows * cols * devices) ** 0.5
    fields = [cache_in, frames_in, cache_mid, cotangent]

    def edges(cut):
        return jnp.concatenate([cut(field) for field in fields], axis=0)

    row_near, row_far = trade(
        "ha", edges(lambda v: v[:, :RIM]), edges(lambda v: v[:, rows - RIM :])
    )

    def strip(cut):
        pieces = [edges(cut), cut(row_near), cut(row_far)]
        return jnp.concatenate([piece.reshape(-1, chans) for piece in pieces], axis=0)

    col_near, col_far = trade(
        "wa", strip(lambda v: v[:, :, :RIM]), strip(lambda v: v[:, :, cols - RIM :])
    )

    full, tall = cols + 2 * RIM, rows + 2 * RIM
    chips = devices // 2
    total = 27 * chans
    share = -(-total // (8 * chips)) * 8
    anywhere = pl.BlockSpec(memory_space=pl.ANY)
    inner = pl.BlockSpec(memory_space=pltpu.VMEM)

    def body(*refs):
        chain_kernel(rows, cols, *refs)

    grad_input, keep, send = pl.pallas_call(
        body,
        out_shape=(
            jax.ShapeDtypeStruct((1, rows, cols, chans), BF),
            jax.ShapeDtypeStruct((share * chips, chans), BF),
            jax.ShapeDtypeStruct((share * chips, chans), BF),
        ),
        in_specs=[inner] * 14,
        out_specs=(inner, anywhere, anywhere),
        scratch_shapes=[
            pltpu.VMEM((6, tall, full, chans), BF),
            pltpu.VMEM((tall, full, chans), F32),
            pltpu.VMEM((tall, full, chans), BF),
            pltpu.VMEM((tall, full, chans), BF),
            pltpu.VMEM((tall, full, chans), BF),
            pltpu.VMEM((rows + 4, full, 3 * chans), BF),
            pltpu.VMEM((2, share * chips, chans), BF),
            pltpu.SemaphoreType.DMA((2,)),
        ],
        compiler_params=pltpu.CompilerParams(vmem_limit_bytes=40 * 1024 * 1024),
        name="chain",
    )(
        cache_in, frames_in, cache_mid, cotangent, row_near, row_far, col_near, col_far,
        w_first, w_second, scale_first, shift_first, scale_second, shift_second,
    )

    pairs, _ = swaps("ha")
    chip_sum = (keep.astype(F32) + lax.ppermute(send, "ha", pairs).astype(F32)).astype(BF)
    cores = [[c for c in range(devices) if (c // lax.axis_size("wa")) % 2 == k] for k in range(2)]

    def spread_out(value):
        return lax.all_to_all(
            value.reshape(chips, share, chans), BOTH, 0, 0, axis_index_groups=cores, tiled=True
        )

    mine = (jnp.sum(spread_out(chip_sum).astype(F32), axis=0) * factor).astype(BF)
    one = spread_out(jnp.broadcast_to(mine[None], (chips, share, chans))).reshape(-1, chans)
    other = lax.ppermute(one, "ha", pairs)
    even = lax.axis_index("ha") % 2 == 0
    shape = (3, 3, 3, chans, chans)
    one, other = one[:total].astype(F32), other[:total].astype(F32)
    grad_first = jnp.where(even, one, other).reshape(shape)
    grad_second = jnp.where(even, other, one).reshape(shape)
    return (grad_input, grad_first, grad_second)


def solution(mesh):
    tiled = P(None, "ha", "wa", None)
    return jax.shard_map(
        per_device,
        mesh=mesh,
        in_specs=(tiled, tiled, tiled, P(), P(), P(), P(), P(), P(), tiled),
        out_specs=(tiled, P(), P()),
        check_vma=False,
    )
```

```python
import jax
import jax.numpy as jnp
from jax import lax
from jax.experimental import pallas as pl
from jax.experimental.pallas import tpu as pltpu
from jax.sharding import PartitionSpec as P

BF = jnp.bfloat16
F32 = jnp.float32
RIM = 4
BOTH = ("ha", "wa")


def swaps(axis):
    count = lax.axis_size(axis)
    first = [(i, i ^ 1) for i in range(count)]
    second = [(i, i + 1 if i % 2 else i - 1) for i in range(1, count - 1)]
    return first, second


def trade(axis, near, far):
    first, second = swaps(axis)
    return lax.ppermute(near, axis, first), lax.ppermute(far, axis, second)


def slope(value):
    sig = jax.nn.sigmoid(value)
    return sig * (1.0 + value * (1.0 - sig))


def chain_kernel(
    rows, cols, cache_in, frames_in, cache_mid, cot, row_near, row_far, col_near, col_far,
    corner_near, corner_far, ahead_one, ahead_two, back_one, back_two, affine,
    gin, keep, send, field, slope_one, a_one, d_two, d_one, moved, grads, sems,
):
    full, lanes = cols + 2 * RIM, field.shape[-1]
    tall = rows + 2 * RIM
    ha, wa = lax.axis_index("ha"), lax.axis_index("wa")
    odd_row, odd_col = ha % 2 == 1, wa % 2 == 1
    core = ha % 2

    def pick(odd, one, other):
        return jnp.where(odd, one.astype(F32), other.astype(F32))

    def assemble(top, blocks, near, far):
        high = blocks[0].shape[0]
        left = pick(odd_col, near, far).reshape(high, 3, 2 * RIM, lanes)
        right = pick(odd_col, far, near).reshape(high, 3, 2 * RIM, lanes)
        lower = lax.broadcasted_iota(jnp.int32, (high, 2 * RIM, lanes), 1) < RIM
        for frame, block in enumerate(blocks):
            one, other = right[:, frame // 2], left[:, frame // 2]
            if frame % 2 == 0:
                rim = jnp.where(lower, one, pltpu.roll(other, RIM, 1))
            else:
                rim = jnp.where(lower, pltpu.roll(one, RIM, 1), other)
            field[frame, top : top + high] = jnp.concatenate([block, rim], axis=1).astype(BF)

    sources = (
        (cache_in, 0), (cache_in, 1), (frames_in, 0), (cache_mid, 0), (cache_mid, 1), (cot, 0)
    )
    assemble(RIM, [ref[i].astype(F32) for ref, i in sources], col_near[...], col_far[...])

    def assemble_rim(top, block, corners):
        half = corners.shape[0] // 2
        assemble(
            top, [block[i].astype(F32) for i in range(6)], corners[:half], corners[half:]
        )

    @pl.when(odd_row)
    def _():
        assemble_rim(0, row_near, corner_near)
        assemble_rim(RIM + rows, row_far, corner_far)

    @pl.when(jnp.logical_not(odd_row))
    def _():
        assemble_rim(0, row_far, corner_far)
        assemble_rim(RIM + rows, row_near, corner_near)

    image_rows, image_cols = rows * lax.axis_size("ha"), cols * lax.axis_size("wa")
    col = lax.broadcasted_iota(jnp.int32, (1, full, lanes), 1)
    own_col = col < cols
    place = jnp.where(col < cols + RIM, col, col - full) + wa * cols
    col_in = (place >= 0) & (place < image_cols)

    def in_image(start, count):
        row = lax.broadcasted_iota(jnp.int32, (count, full, lanes), 0) + (start - RIM) + ha * rows
        return (row >= 0) & (row < image_rows) & col_in

    def roll(value, step):
        return pltpu.roll(value, step % full, 1)

    def forward(piece, weight, start, count):
        lhs = jnp.concatenate(
            [piece(a, start - 1 + b, count) for a in range(3) for b in range(3)], axis=1
        )
        out = jnp.dot(lhs, weight[...], preferred_element_type=F32).reshape(count, full, 3 * lanes)
        return (
            roll(out[..., :lanes], 1)
            + out[..., lanes : 2 * lanes]
            + roll(out[..., 2 * lanes :], -1)
        )

    def backward(piece, weight, start, count):
        lhs = jnp.concatenate([piece(start + 1 - b, count) for b in range(3)], axis=1)
        out = lax.dot_general(
            lhs, weight[...], (((1,), (1,)), ((), ())), preferred_element_type=F32
        ).reshape(count, full, 3 * lanes)
        return (
            roll(out[..., :lanes], -1)
            + out[..., lanes : 2 * lanes]
            + roll(out[..., 2 * lanes :], 1)
        )

    def flat(value):
        return value.reshape(-1, lanes)

    def gradient(which, source):
        lhs = jnp.concatenate([source(a) for a in range(3)], axis=1)
        for b in range(3):
            rhs = moved[2 - b : 2 - b + rows + 2].reshape(-1, 3 * lanes)
            out = lax.dot_general(
                lhs, rhs, (((0,), (0,)), ((), ())), preferred_element_type=F32
            )
            for a in range(3):
                for c in range(3):
                    at = ((a * 3 + b) * 3 + c) * lanes
                    grads[which, at : at + lanes, :] = out[
                        a * lanes : (a + 1) * lanes, c * lanes : (c + 1) * lanes
                    ].astype(BF)

    def spread(value, start, count):
        kept = jnp.where(own_col, value, 0.0)
        at = start - 2
        moved[at : at + count, :, :lanes] = roll(kept, -1).astype(BF)
        moved[at : at + count, :, lanes : 2 * lanes] = kept.astype(BF)
        moved[at : at + count, :, 2 * lanes :] = roll(kept, 1).astype(BF)

    zero_rows = jnp.zeros((2, full, 3 * lanes), BF)
    moved[0:2] = zero_rows
    moved[rows + 2 : rows + 4] = zero_rows
    used = 27 * lanes
    if grads.shape[1] > used:
        grads[:, used:, :] = jnp.zeros((2, grads.shape[1] - used, lanes), BF)

    gain_one, bias_one, gain_two, bias_two = (
        affine[i : i + 1, :].reshape(1, 1, lanes) for i in range(4)
    )
    step = (tall - 2) // 3
    for start in range(1, tall - 1, step):
        count = min(step, tall - 1 - start)
        m_one = (
            forward(lambda a, r, n: flat(field[a, r : r + n]), ahead_one, start, count) * gain_one
            + bias_one
        )
        sig = jax.nn.sigmoid(m_one)
        inside = in_image(start, count)
        a_one[start : start + count] = jnp.where(inside, m_one * sig, 0.0).astype(BF)
        slope_one[start : start + count] = jnp.where(
            inside, sig * (1.0 + m_one * (1.0 - sig)) * gain_one, 0.0
        )

    def mid(a, r, n):
        return flat(a_one[r : r + n] if a == 2 else field[3 + a, r : r + n])

    step = (tall - 4) // 2
    for start in range(2, tall - 2, step):
        count = min(step, tall - 2 - start)
        m_two = forward(mid, ahead_two, start, count) * gain_two + bias_two
        value = field[5, start : start + count].astype(F32) * slope(m_two) * gain_two
        d_two[start : start + count] = value.astype(BF)
        low_at, high_at = max(start, RIM), min(start + count, RIM + rows)
        spread(value[low_at - start : high_at - start], low_at, high_at - low_at)

    gradient(1, lambda a: mid(a, 3, rows + 2))

    step = (tall - 6) // 2
    for start in range(3, tall - 3, step):
        count = min(step, tall - 3 - start)
        value = (
            backward(lambda r, n: flat(d_two[r : r + n]), back_two, start, count)
            * slope_one[start : start + count]
        )
        d_one[start : start + count] = value.astype(BF)
        low_at, high_at = max(start, RIM), min(start + count, RIM + rows)
        spread(value[low_at - start : high_at - start], low_at, high_at - low_at)

    gradient(0, lambda a: flat(field[a, 3 : 3 + rows + 2]))
    out_copies = [
        pltpu.make_async_copy(grads.at[core], keep, sems.at[0]),
        pltpu.make_async_copy(grads.at[1 - core], send, sems.at[1]),
    ]
    for copy in out_copies:
        copy.start()

    step = rows // 2
    for start in range(RIM, RIM + rows, step):
        count = min(step, RIM + rows - start)
        value = backward(lambda r, n: flat(d_one[r : r + n]), back_one, start, count)
        gin[0, start - RIM : start - RIM + count] = value[:, :cols].astype(BF)

    for copy in out_copies:
        copy.wait()


def pack_kernel(rows, cols, cache_in, frames_in, cache_mid, cot, row_near, row_far, col_near, col_far):
    odd_row, odd_col = lax.axis_index("ha") % 2 == 1, lax.axis_index("wa") % 2 == 1
    sources = (
        (cache_in, 0), (cache_in, 1), (frames_in, 0), (cache_mid, 0), (cache_mid, 1), (cot, 0)
    )
    last = rows - RIM
    near_at, far_at = jnp.where(odd_row, 0, last), jnp.where(odd_row, last, 0)
    for frame, (ref, i) in enumerate(sources):
        row_near[frame] = ref[i, pl.ds(near_at, RIM)]
        row_far[frame] = ref[i, pl.ds(far_at, RIM)]
    lanes = col_near.shape[-1]
    lower = lax.broadcasted_iota(jnp.int32, (rows, 2 * RIM, lanes), 1) < RIM

    def edges(frame):
        ref, i = sources[frame]
        value = ref[i].astype(F32)
        return value[:, : 2 * RIM], pltpu.roll(value[:, cols - 2 * RIM :], RIM, 1)

    near, far = [], []
    for pair in range(3):
        (head, tail), (head_b, tail_b) = edges(2 * pair), edges(2 * pair + 1)
        heads = jnp.where(lower, head, pltpu.roll(head_b, RIM, 1))
        tails = jnp.where(lower, tail, pltpu.roll(tail_b, RIM, 1))
        near.append(jnp.where(odd_col, heads, tails))
        far.append(jnp.where(odd_col, tails, heads))
    col_near[...] = jnp.stack(near, axis=1).reshape(-1, lanes).astype(BF)
    col_far[...] = jnp.stack(far, axis=1).reshape(-1, lanes).astype(BF)


def ready_kernel(w_one, w_two, sc_one, sh_one, sc_two, sh_two, ahead_one, ahead_two, back_one, back_two, affine):
    lanes = affine.shape[-1]
    for weight, ahead, back in ((w_one, ahead_one, back_one), (w_two, ahead_two, back_two)):
        for a in range(3):
            for b in range(3):
                for c in range(3):
                    at = (a * 3 + b) * lanes
                    ahead[at : at + lanes, c * lanes : (c + 1) * lanes] = weight[a, b, c]
        for b in range(3):
            for c in range(3):
                back[c * lanes : (c + 1) * lanes, b * lanes : (b + 1) * lanes] = weight[2, b, c]
    affine[...] = jnp.concatenate(
        [1.0 + sc_one[...], sh_one[...], 1.0 + sc_two[...], sh_two[...]] * 2, axis=0
    )


def per_device(
    frames_in, cache_in, cache_mid, w_first, w_second,
    scale_first, shift_first, scale_second, shift_second, cotangent,
):
    _, rows, cols, chans = frames_in.shape
    devices = lax.axis_size("ha") * lax.axis_size("wa")
    factor = 1.0 / (rows * cols * devices) ** 0.5
    inner = pl.BlockSpec(memory_space=pltpu.VMEM)
    anywhere = pl.BlockSpec(memory_space=pl.ANY)

    def pack(*refs):
        pack_kernel(rows, cols, *refs)

    rim_rows = jax.ShapeDtypeStruct((6, RIM, cols, chans), BF)
    rim_cols = jax.ShapeDtypeStruct((6 * rows * RIM, chans), BF)
    row_near, row_far, col_near, col_far = pl.pallas_call(
        pack,
        out_shape=(rim_rows, rim_rows, rim_cols, rim_cols),
        in_specs=[inner] * 4,
        out_specs=(inner,) * 4,
        compiler_params=pltpu.CompilerParams(vmem_limit_bytes=16 * 1024 * 1024),
        name="pack",
    )(cache_in, frames_in, cache_mid, cotangent)
    ahead = jax.ShapeDtypeStruct((9 * chans, 3 * chans), BF)
    back = jax.ShapeDtypeStruct((3 * chans, 3 * chans), BF)
    ready = pl.pallas_call(
        ready_kernel,
        out_shape=(ahead, ahead, back, back, jax.ShapeDtypeStruct((8, chans), F32)),
        in_specs=[inner] * 6,
        out_specs=(inner,) * 5,
        cost_estimate=pl.CostEstimate(
            flops=2 * 10**9, bytes_accessed=8 * 10**6, transcendentals=0
        ),
        compiler_params=pltpu.CompilerParams(vmem_limit_bytes=16 * 1024 * 1024),
        name="ready",
    )(w_first, w_second, scale_first, shift_first, scale_second, shift_second)
    row_near, row_far = trade("ha", row_near, row_far)
    col_near, col_far = trade("wa", col_near, col_far)
    size = 6 * RIM * RIM
    head = jnp.concatenate([col_near[:size], col_far[:size]], axis=0)
    tail = jnp.concatenate([col_near[-size:], col_far[-size:]], axis=0)
    odd = lax.axis_index("ha") % 2 == 1
    corner_near, corner_far = trade(
        "ha", jnp.where(odd, head, tail), jnp.where(odd, tail, head)
    )

    full, tall = cols + 2 * RIM, rows + 2 * RIM
    chips = devices // 2
    total = 27 * chans
    share = -(-total // (8 * chips)) * 8

    def body(*refs):
        chain_kernel(rows, cols, *refs)

    grad_input, keep, send = pl.pallas_call(
        body,
        out_shape=(
            jax.ShapeDtypeStruct((1, rows, cols, chans), BF),
            jax.ShapeDtypeStruct((share * chips, chans), BF),
            jax.ShapeDtypeStruct((share * chips, chans), BF),
        ),
        in_specs=[inner] * 15,
        out_specs=(inner, anywhere, anywhere),
        scratch_shapes=[
            pltpu.VMEM((6, tall, full, chans), BF),
            pltpu.VMEM((tall, full, chans), F32),
            pltpu.VMEM((tall, full, chans), BF),
            pltpu.VMEM((tall, full, chans), BF),
            pltpu.VMEM((tall, full, chans), BF),
            pltpu.VMEM((rows + 4, full, 3 * chans), BF),
            pltpu.VMEM((2, share * chips, chans), BF),
            pltpu.SemaphoreType.DMA((2,)),
        ],
        compiler_params=pltpu.CompilerParams(vmem_limit_bytes=40 * 1024 * 1024),
        name="chain",
    )(
        cache_in, frames_in, cache_mid, cotangent, row_near, row_far, col_near, col_far,
        corner_near, corner_far, *ready,
    )

    pairs, _ = swaps("ha")
    chip_sum = (keep.astype(F32) + lax.ppermute(send, "ha", pairs).astype(F32)).astype(BF)
    cores = [[c for c in range(devices) if (c // lax.axis_size("wa")) % 2 == k] for k in range(2)]

    def spread_out(value):
        return lax.all_to_all(
            value.reshape(chips, share, chans), BOTH, 0, 0, axis_index_groups=cores, tiled=True
        )

    mine = (jnp.sum(spread_out(chip_sum).astype(F32), axis=0) * factor).astype(BF)
    one = spread_out(jnp.broadcast_to(mine[None], (chips, share, chans))).reshape(-1, chans)
    other = lax.ppermute(one, "ha", pairs)
    even = lax.axis_index("ha") % 2 == 0
    shape = (3, 3, 3, chans, chans)
    one, other = one[:total].astype(F32), other[:total].astype(F32)
    grad_first = jnp.where(even, one, other).reshape(shape)
    grad_second = jnp.where(even, other, one).reshape(shape)
    return (grad_input, grad_first, grad_second)


def solution(mesh):
    tiled = P(None, "ha", "wa", None)
    return jax.shard_map(
        per_device,
        mesh=mesh,
        in_specs=(tiled, tiled, tiled, P(), P(), P(), P(), P(), P(), tiled),
        out_specs=(tiled, P(), P()),
        check_vma=False,
    )
```

```python
import jax
import jax.numpy as jnp
from jax import lax
from jax.experimental import pallas as pl
from jax.experimental.pallas import tpu as pltpu
from jax.sharding import PartitionSpec as P

BF = jnp.bfloat16
F32 = jnp.float32
RIM = 4
BOTH = ("ha", "wa")


def swaps(axis):
    count = lax.axis_size(axis)
    first = [(i, i ^ 1) for i in range(count)]
    second = [(i, i + 1 if i % 2 else i - 1) for i in range(1, count - 1)]
    return first, second


def trade(axis, near, far):
    first, second = swaps(axis)
    return lax.ppermute(near, axis, first), lax.ppermute(far, axis, second)


def is_odd(axis):
    return lax.axis_index(axis) % 2 == 1


def slope(value):
    sig = jax.nn.sigmoid(value)
    return sig * (1.0 + value * (1.0 - sig))


def flat(value):
    return value.reshape(-1, value.shape[-1])


def turn(value, step):
    return pltpu.roll(value, step % value.shape[1], 1)


def join(block, near, far):
    high, _, lanes = block[0].shape
    odd = is_odd("wa")
    near, far = near.astype(F32), far.astype(F32)
    left = jnp.where(odd, near, far).reshape(high, 3, 2 * RIM, lanes)
    right = jnp.where(odd, far, near).reshape(high, 3, 2 * RIM, lanes)
    lower = lax.broadcasted_iota(jnp.int32, (high, 2 * RIM, lanes), 1) < RIM
    frames = []
    for frame in range(6):
        one, other = right[:, frame // 2], left[:, frame // 2]
        if frame % 2 == 0:
            rim = jnp.where(lower, one, pltpu.roll(other, RIM, 1))
        else:
            rim = jnp.where(lower, pltpu.roll(one, RIM, 1), other)
        frames.append(jnp.concatenate([block[frame].astype(F32), rim], axis=1).astype(BF))
    return frames


class Rows:
    def __init__(self, *pieces):
        self.pieces = pieces

    def get(self, start, count):
        out = []
        for first, ref, size in self.pieces:
            low, high = max(start, first), min(start + count, first + size)
            if low < high:
                out.append(ref[low - first : high - first])
        return out[0] if len(out) == 1 else jnp.concatenate(out, axis=0)


class Frame:
    def __init__(self, ref, index):
        self.ref, self.index = ref, index

    def __getitem__(self, key):
        return self.ref[self.index, key]


def forward(frames, weight, blocks):
    lhs = jnp.concatenate(
        [
            jnp.concatenate(
                [flat(frames[a].get(start - 1 + b, count)) for start, count in blocks], axis=0
            )
            for a in range(3)
            for b in range(3)
        ],
        axis=1,
    )
    out = jnp.dot(lhs, weight[...], preferred_element_type=F32)
    return gather_columns(out, 1)


def backward(field, weight, start, count):
    lhs = jnp.concatenate([flat(field.get(start + 1 - b, count)) for b in range(3)], axis=1)
    out = lax.dot_general(lhs, weight[...], (((1,), (1,)), ((), ())), preferred_element_type=F32)
    return gather_columns(out, -1)


def gather_columns(out, step):
    lanes = out.shape[-1] // 3
    out = out.reshape(-1, FULL[0], 3 * lanes)
    return (
        turn(out[..., :lanes], step)
        + out[..., lanes : 2 * lanes]
        + turn(out[..., 2 * lanes :], -step)
    )


FULL = [0]


def in_image(rows, cols, lanes, blocks):
    full = cols + 2 * RIM
    image_rows, image_cols = rows * lax.axis_size("ha"), cols * lax.axis_size("wa")
    col = lax.broadcasted_iota(jnp.int32, (1, full, lanes), 1)
    place = jnp.where(col < cols + RIM, col, col - full) + lax.axis_index("wa") * cols
    col_in = (place >= 0) & (place < image_cols)
    out = []
    for start, count in blocks:
        row = lax.broadcasted_iota(jnp.int32, (count, full, lanes), 0)
        row = row + (start - RIM) + lax.axis_index("ha") * rows
        out.append((row >= 0) & (row < image_rows) & col_in)
    return jnp.concatenate(out, axis=0) if len(out) > 1 else out[0]


def first_layer(rows, cols, frames, weight, affine, blocks):
    lanes = affine.shape[-1]
    gain, bias = (affine[i : i + 1, :].reshape(1, 1, lanes) for i in (0, 1))
    m_one = forward(frames, weight, blocks) * gain + bias
    sig = jax.nn.sigmoid(m_one)
    inside = in_image(rows, cols, lanes, blocks)
    a_one = jnp.where(inside, m_one * sig, 0.0).astype(BF)
    slope_one = jnp.where(inside, sig * (1.0 + m_one * (1.0 - sig)) * gain, 0.0)
    return a_one, slope_one


def second_layer(frames, cot, weight, affine, blocks):
    lanes = affine.shape[-1]
    gain, bias = (affine[i : i + 1, :].reshape(1, 1, lanes) for i in (2, 3))
    m_two = forward(frames, weight, blocks) * gain + bias
    pulled = [cot.get(start, count) for start, count in blocks]
    pulled = jnp.concatenate(pulled, axis=0) if len(pulled) > 1 else pulled[0]
    return pulled.astype(F32) * slope(m_two) * gain


def spread(cols, value):
    own = lax.broadcasted_iota(jnp.int32, (1,) + value.shape[1:], 1) < cols
    kept = jnp.where(own, value, 0.0)
    return jnp.concatenate([turn(kept, -1), kept, turn(kept, 1)], axis=2).astype(BF)


def cut(start, stop, parts):
    step = -(-(stop - start) // parts)
    return [(at, min(step, stop - at)) for at in range(start, stop, step)]


def pack_kernel(
    rows, cols, cache_in_at, frames_in_at, cache_mid_at, cot_at, row_near, row_far, col_near, col_far,
    cache_in, frames_in, cache_mid, cot, sems,
):
    copies = [
        pltpu.make_async_copy(source, target, sems.at[i])
        for i, (source, target) in enumerate(
            (
                (cache_in_at, cache_in),
                (frames_in_at, frames_in),
                (cache_mid_at, cache_mid),
                (cot_at, cot),
            )
        )
    ]
    for copy in copies:
        copy.start()
    for copy in copies:
        copy.wait()
    odd_row, odd_col = is_odd("ha"), is_odd("wa")
    sources = (
        (cache_in, 0), (cache_in, 1), (frames_in, 0), (cache_mid, 0), (cache_mid, 1), (cot, 0)
    )
    last = rows - RIM
    near_at, far_at = jnp.where(odd_row, 0, last), jnp.where(odd_row, last, 0)
    for frame, (ref, i) in enumerate(sources):
        row_near[frame] = ref[i, pl.ds(near_at, RIM)]
        row_far[frame] = ref[i, pl.ds(far_at, RIM)]
    lanes = col_near.shape[-1]
    lower = lax.broadcasted_iota(jnp.int32, (rows, 2 * RIM, lanes), 1) < RIM

    def edges(frame):
        ref, i = sources[frame]
        value = ref[i].astype(F32)
        return value[:, : 2 * RIM], pltpu.roll(value[:, cols - 2 * RIM :], RIM, 1)

    near, far = [], []
    for pair in range(3):
        (head, tail), (head_b, tail_b) = edges(2 * pair), edges(2 * pair + 1)
        heads = jnp.where(lower, head, pltpu.roll(head_b, RIM, 1))
        tails = jnp.where(lower, tail, pltpu.roll(tail_b, RIM, 1))
        near.append(jnp.where(odd_col, heads, tails))
        far.append(jnp.where(odd_col, tails, heads))
    col_near[...] = jnp.stack(near, axis=1).reshape(-1, lanes).astype(BF)
    col_far[...] = jnp.stack(far, axis=1).reshape(-1, lanes).astype(BF)


def ready_kernel(
    w_one, w_two, sc_one, sh_one, sc_two, sh_two, ahead_one, ahead_two, back_one, back_two, affine
):
    lanes = affine.shape[-1]
    for weight, ahead, back in ((w_one, ahead_one, back_one), (w_two, ahead_two, back_two)):
        for a in range(3):
            for b in range(3):
                for c in range(3):
                    at = (a * 3 + b) * lanes
                    ahead[at : at + lanes, c * lanes : (c + 1) * lanes] = weight[a, b, c]
        for b in range(3):
            for c in range(3):
                back[c * lanes : (c + 1) * lanes, b * lanes : (b + 1) * lanes] = weight[2, b, c]
    affine[...] = jnp.concatenate(
        [1.0 + sc_one[...], sh_one[...], 1.0 + sc_two[...], sh_two[...]] * 2, axis=0
    )


def middle_kernel(
    rows, cols, cache_in, frames_in, cache_mid, cot, col_near, col_far, ahead_one, ahead_two, affine,
    field, slope_mid, a_mid, d_mid, moved_mid,
):
    block = [cache_in[0], cache_in[1], frames_in[0], cache_mid[0], cache_mid[1], cot[0]]
    for frame, value in enumerate(join(block, col_near[...], col_far[...])):
        field[frame] = value
    own = [Rows((RIM, Frame(field, i), rows)) for i in range(6)]
    first = RIM + 1
    for start, count in cut(first, RIM + rows - 1, 2):
        a_one, slope_one = first_layer(rows, cols, own[:3], ahead_one, affine, [(start, count)])
        a_mid[start - first : start - first + count] = a_one
        slope_mid[start - first : start - first + count] = slope_one
    frames = own[3:5] + [Rows((first, a_mid, rows - 2))]
    second = RIM + 2
    for start, count in cut(second, RIM + rows - 2, 2):
        value = second_layer(frames, own[5], ahead_two, affine, [(start, count)])
        d_mid[start - second : start - second + count] = value.astype(BF)
        moved_mid[start - second : start - second + count] = spread(cols, value)


def rim_kernel(
    rows, cols, field, slope_mid, a_mid, d_mid, moved_mid, row_near, row_far, corner_near, corner_far,
    ahead_one, ahead_two, back_two, affine, keep, send, d_one,
    top, bottom, slope_rim, a_rim, d_rim, moved_rim, moved_one, grads, sems,
):
    lanes = affine.shape[-1]
    tall = rows + 2 * RIM
    half = corner_near.shape[0] // 2

    def assemble(target, block, corner):
        parts = join([block[i] for i in range(6)], corner[:half], corner[half:])
        for frame, value in enumerate(parts):
            target[frame] = value

    @pl.when(is_odd("ha"))
    def _():
        assemble(top, row_near, corner_near)
        assemble(bottom, row_far, corner_far)

    @pl.when(jnp.logical_not(is_odd("ha")))
    def _():
        assemble(top, row_far, corner_far)
        assemble(bottom, row_near, corner_near)

    whole = [
        Rows(
            (0, Frame(top, i), RIM),
            (RIM, Frame(field, i), rows),
            (RIM + rows, Frame(bottom, i), RIM),
        )
        for i in range(6)
    ]

    def around(rim, mid, first, count):
        size = mid.shape[0]
        return Rows(
            (first, rim, count),
            (first + count, mid, size),
            (first + count + size, Shifted(rim, count), count),
        )

    used = 27 * lanes
    if grads.shape[1] > used:
        grads[:, used:, :] = jnp.zeros((2, grads.shape[1] - used, lanes), BF)
    edge = jnp.zeros((2,) + moved_rim.shape[1:], BF)
    moved_rim[0:2] = edge
    moved_rim[6:8] = edge
    moved_one[0:2] = edge
    moved_one[rows + 2 : rows + 4] = edge

    def gradient(which, frames, moved):
        lhs = jnp.concatenate([flat(frames[a].get(RIM - 1, rows + 2)) for a in range(3)], axis=1)
        for b in range(3):
            rhs = flat(moved.get(RIM - b, rows + 2))
            out = lax.dot_general(lhs, rhs, (((0,), (0,)), ((), ())), preferred_element_type=F32)
            for a in range(3):
                for c in range(3):
                    at = ((a * 3 + b) * 3 + c) * lanes
                    grads[which, at : at + lanes, :] = out[
                        a * lanes : (a + 1) * lanes, c * lanes : (c + 1) * lanes
                    ].astype(BF)

    blocks = [(1, 4), (tall - 5, 4)]
    a_value, slope_value = first_layer(rows, cols, whole[:3], ahead_one, affine, blocks)
    a_rim[...] = a_value
    slope_rim[...] = slope_value
    a_all = around(a_rim, a_mid, 1, 4)
    slope_all = around(slope_rim, slope_mid, 1, 4)

    frames = whole[3:5] + [a_all]
    value = second_layer(frames, whole[5], ahead_two, affine, [(2, 4), (tall - 6, 4)])
    d_rim[...] = value.astype(BF)
    moved_rim[2:6] = spread(cols, value[2:6])
    d_all = around(d_rim, d_mid, 2, 4)
    gradient(1, frames, around(moved_rim, moved_mid, 2, 4))

    for start, count in cut(3, tall - 3, 2):
        value = backward(d_all, back_two, start, count) * slope_all.get(start, count)
        d_one[start - 3 : start - 3 + count] = value.astype(BF)
        low, high = max(start, RIM), min(start + count, RIM + rows)
        moved_one[low - 2 : high - 2] = spread(cols, value[low - start : high - start])
    gradient(0, whole[:3], Rows((2, moved_one, rows + 4)))

    core = lax.axis_index("ha") % 2
    copies = [
        pltpu.make_async_copy(grads.at[core], keep, sems.at[0]),
        pltpu.make_async_copy(grads.at[1 - core], send, sems.at[1]),
    ]
    for copy in copies:
        copy.start()
    for copy in copies:
        copy.wait()


class Shifted:
    def __init__(self, ref, by):
        self.ref, self.by = ref, by

    def __getitem__(self, key):
        return self.ref[key.start + self.by : key.stop + self.by]


def input_kernel(rows, cols, d_one, back_one, gin):
    field = Rows((RIM - 1, d_one, rows + 2))
    for start, count in cut(RIM, RIM + rows, 2):
        value = backward(field, back_one, start, count)
        gin[0, start - RIM : start - RIM + count] = value[:, :cols].astype(BF)


def per_device(
    frames_in, cache_in, cache_mid, w_first, w_second,
    scale_first, shift_first, scale_second, shift_second, cotangent,
):
    _, rows, cols, chans = frames_in.shape
    devices = lax.axis_size("ha") * lax.axis_size("wa")
    factor = 1.0 / (rows * cols * devices) ** 0.5
    full, tall = cols + 2 * RIM, rows + 2 * RIM
    FULL[0] = full
    chips = devices // 2
    total = 27 * chans
    share = -(-total // (8 * chips)) * 8
    inner = pl.BlockSpec(memory_space=pltpu.VMEM)
    anywhere = pl.BlockSpec(memory_space=pl.ANY)

    def shaped(*shape, dtype=BF):
        return jax.ShapeDtypeStruct(shape, dtype)

    def call(kernel, name, out_shape, mebibytes, flops, args, sizes=True, **kwargs):
        def body(*refs):
            kernel(rows, cols, *refs) if sizes else kernel(*refs)

        count = len(out_shape)
        kwargs.setdefault("in_specs", [inner] * len(args))
        kwargs.setdefault("out_specs", (inner,) * count)
        return pl.pallas_call(
            body,
            out_shape=tuple(out_shape),
            cost_estimate=pl.CostEstimate(
                flops=int(flops), bytes_accessed=8 * 10**6, transcendentals=0
            ),
            compiler_params=pltpu.CompilerParams(vmem_limit_bytes=mebibytes * 2**20),
            name=name,
            **kwargs,
        )(*args)

    fields = (cache_in, frames_in, cache_mid, cotangent)
    rim_rows, rim_cols = shaped(6, RIM, cols, chans), shaped(6 * rows * RIM, chans)
    row_near, row_far, col_near, col_far = call(
        pack_kernel, "pack", (rim_rows, rim_rows, rim_cols, rim_cols), 60, 1e9, fields,
        in_specs=[anywhere] * 4,
        scratch_shapes=[pltpu.VMEM(v.shape, BF) for v in fields] + [pltpu.SemaphoreType.DMA((4,))],
    )
    ahead, back = shaped(9 * chans, 3 * chans), shaped(3 * chans, 3 * chans)
    ahead_one, ahead_two, back_one, back_two, affine = call(
        ready_kernel, "ready", (ahead, ahead, back, back, shaped(8, chans, dtype=F32)), 16, 2e9,
        (w_first, w_second, scale_first, shift_first, scale_second, shift_second), sizes=False,
    )
    col_near, col_far = trade("wa", col_near, col_far)
    row_near, row_far = trade("ha", row_near, row_far)
    size = 6 * RIM * RIM
    head = jnp.concatenate([col_near[:size], col_far[:size]], axis=0)
    tail = jnp.concatenate([col_near[-size:], col_far[-size:]], axis=0)
    odd = is_odd("ha")
    corner_near, corner_far = trade("ha", jnp.where(odd, head, tail), jnp.where(odd, tail, head))

    field, slope_mid, a_mid, d_mid, moved_mid = call(
        middle_kernel, "middle",
        (
            shaped(6, rows, full, chans),
            shaped(rows - 2, full, chans, dtype=F32),
            shaped(rows - 2, full, chans),
            shaped(rows - 4, full, chans),
            shaped(rows - 4, full, 3 * chans),
        ),
        28, 5e9, (*fields, col_near, col_far, ahead_one, ahead_two, affine),
    )
    keep, send, d_one = call(
        rim_kernel, "rim",
        (shaped(share * chips, chans), shaped(share * chips, chans), shaped(rows + 2, full, chans)),
        28, 5e9,
        (
            field, slope_mid, a_mid, d_mid, moved_mid, row_near, row_far, corner_near, corner_far,
            ahead_one, ahead_two, back_two, affine,
        ),
        out_specs=(anywhere, anywhere, inner),
        scratch_shapes=[
            pltpu.VMEM((6, RIM, full, chans), BF),
            pltpu.VMEM((6, RIM, full, chans), BF),
            pltpu.VMEM((8, full, chans), F32),
            pltpu.VMEM((8, full, chans), BF),
            pltpu.VMEM((8, full, chans), BF),
            pltpu.VMEM((8, full, 3 * chans), BF),
            pltpu.VMEM((rows + 4, full, 3 * chans), BF),
            pltpu.VMEM((2, share * chips, chans), BF),
            pltpu.SemaphoreType.DMA((2,)),
        ],
    )

    pairs, _ = swaps("ha")
    got = lax.ppermute(send, "ha", pairs)
    (grad_input,) = call(
        input_kernel, "input", (shaped(1, rows, cols, chans),), 28, 1e9, (d_one, back_one)
    )
    chip_sum = (keep.astype(F32) + got.astype(F32)).astype(BF)
    cores = [[c for c in range(devices) if (c // lax.axis_size("wa")) % 2 == k] for k in range(2)]

    def spread_out(value):
        return lax.all_to_all(
            value.reshape(chips, share, chans), BOTH, 0, 0, axis_index_groups=cores, tiled=True
        )

    mine = (jnp.sum(spread_out(chip_sum).astype(F32), axis=0) * factor).astype(BF)
    one = spread_out(jnp.broadcast_to(mine[None], (chips, share, chans))).reshape(-1, chans)
    other = lax.ppermute(one, "ha", pairs)
    even = jnp.logical_not(odd)
    shape = (3, 3, 3, chans, chans)
    one, other = one[:total].astype(F32), other[:total].astype(F32)
    grad_first = jnp.where(even, one, other).reshape(shape)
    grad_second = jnp.where(even, other, one).reshape(shape)
    return (grad_input, grad_first, grad_second)


def solution(mesh):
    tiled = P(None, "ha", "wa", None)
    return jax.shard_map(
        per_device,
        mesh=mesh,
        in_specs=(tiled, tiled, tiled, P(), P(), P(), P(), P(), P(), tiled),
        out_specs=(tiled, P(), P()),
        check_vma=False,
    )
```

```python
import jax
import jax.numpy as jnp
from jax import lax
from jax.experimental import pallas as pl
from jax.experimental.pallas import tpu as pltpu
from jax.sharding import PartitionSpec as P

BF = jnp.bfloat16
F32 = jnp.float32
RIM = 4
BOTH = ("ha", "wa")


def swaps(axis):
    count = lax.axis_size(axis)
    first = [(i, i ^ 1) for i in range(count)]
    second = [(i, i + 1 if i % 2 else i - 1) for i in range(1, count - 1)]
    return first, second


def trade(axis, near, far):
    first, second = swaps(axis)
    return lax.ppermute(near, axis, first), lax.ppermute(far, axis, second)


def is_odd(axis):
    return lax.axis_index(axis) % 2 == 1


def slope(value):
    sig = jax.nn.sigmoid(value)
    return sig * (1.0 + value * (1.0 - sig))


def flat(value):
    return value.reshape(-1, value.shape[-1])


def turn(value, step):
    return pltpu.roll(value, step % value.shape[1], 1)


def join(block, near, far):
    high, _, lanes = block[0].shape
    odd = is_odd("wa")
    near, far = near.astype(F32), far.astype(F32)
    left = jnp.where(odd, near, far).reshape(high, 3, 2 * RIM, lanes)
    right = jnp.where(odd, far, near).reshape(high, 3, 2 * RIM, lanes)
    lower = lax.broadcasted_iota(jnp.int32, (high, 2 * RIM, lanes), 1) < RIM
    frames = []
    for frame in range(6):
        one, other = right[:, frame // 2], left[:, frame // 2]
        if frame % 2 == 0:
            rim = jnp.where(lower, one, pltpu.roll(other, RIM, 1))
        else:
            rim = jnp.where(lower, pltpu.roll(one, RIM, 1), other)
        frames.append(jnp.concatenate([block[frame].astype(F32), rim], axis=1).astype(BF))
    return frames


class Rows:
    def __init__(self, *pieces):
        self.pieces = pieces

    def get(self, start, count):
        out = []
        for first, ref, size in self.pieces:
            low, high = max(start, first), min(start + count, first + size)
            if low < high:
                out.append(ref[low - first : high - first])
        return out[0] if len(out) == 1 else jnp.concatenate(out, axis=0)


class Frame:
    def __init__(self, ref, index):
        self.ref, self.index = ref, index

    def __getitem__(self, key):
        return self.ref[self.index, key]


def forward(frames, weight, blocks):
    lhs = jnp.concatenate(
        [
            jnp.concatenate(
                [flat(frames[a].get(start - 1 + b, count)) for start, count in blocks], axis=0
            )
            for a in range(3)
            for b in range(3)
        ],
        axis=1,
    )
    out = jnp.dot(lhs, weight[...], preferred_element_type=F32)
    return gather_columns(out, 1)


def backward(field, weight, start, count):
    lhs = jnp.concatenate([flat(field.get(start + 1 - b, count)) for b in range(3)], axis=1)
    out = lax.dot_general(lhs, weight[...], (((1,), (1,)), ((), ())), preferred_element_type=F32)
    return gather_columns(out, -1)


def gather_columns(out, step):
    lanes = out.shape[-1] // 3
    out = out.reshape(-1, FULL[0], 3 * lanes)
    return (
        turn(out[..., :lanes], step)
        + out[..., lanes : 2 * lanes]
        + turn(out[..., 2 * lanes :], -step)
    )


FULL = [0]


def in_image(rows, cols, lanes, blocks):
    full = cols + 2 * RIM
    image_rows, image_cols = rows * lax.axis_size("ha"), cols * lax.axis_size("wa")
    col = lax.broadcasted_iota(jnp.int32, (1, full, lanes), 1)
    place = jnp.where(col < cols + RIM, col, col - full) + lax.axis_index("wa") * cols
    col_in = (place >= 0) & (place < image_cols)
    out = []
    for start, count in blocks:
        row = lax.broadcasted_iota(jnp.int32, (count, full, lanes), 0)
        row = row + (start - RIM) + lax.axis_index("ha") * rows
        out.append((row >= 0) & (row < image_rows) & col_in)
    return jnp.concatenate(out, axis=0) if len(out) > 1 else out[0]


def first_layer(rows, cols, frames, weight, affine, blocks):
    lanes = affine.shape[-1]
    gain, bias = (affine[i : i + 1, :].reshape(1, 1, lanes) for i in (0, 1))
    m_one = forward(frames, weight, blocks) * gain + bias
    sig = jax.nn.sigmoid(m_one)
    inside = in_image(rows, cols, lanes, blocks)
    a_one = jnp.where(inside, m_one * sig, 0.0).astype(BF)
    slope_one = jnp.where(inside, sig * (1.0 + m_one * (1.0 - sig)) * gain, 0.0)
    return a_one, slope_one


def second_layer(frames, cot, weight, affine, blocks):
    lanes = affine.shape[-1]
    gain, bias = (affine[i : i + 1, :].reshape(1, 1, lanes) for i in (2, 3))
    m_two = forward(frames, weight, blocks) * gain + bias
    pulled = [cot.get(start, count) for start, count in blocks]
    pulled = jnp.concatenate(pulled, axis=0) if len(pulled) > 1 else pulled[0]
    return pulled.astype(F32) * slope(m_two) * gain


def spread(cols, value):
    own = lax.broadcasted_iota(jnp.int32, (1,) + value.shape[1:], 1) < cols
    kept = jnp.where(own, value, 0.0)
    return jnp.concatenate([turn(kept, -1), kept, turn(kept, 1)], axis=2).astype(BF)


def cut(start, stop, parts):
    step = -(-(stop - start) // parts)
    return [(at, min(step, stop - at)) for at in range(start, stop, step)]


def pack_kernel(
    rows, cols, cache_in_at, frames_in_at, cache_mid_at, cot_at, row_near, row_far, col_near, col_far,
    cache_in, frames_in, cache_mid, cot, sems,
):
    copies = [
        pltpu.make_async_copy(source, target, sems.at[i])
        for i, (source, target) in enumerate(
            (
                (cache_in_at, cache_in),
                (frames_in_at, frames_in),
                (cache_mid_at, cache_mid),
                (cot_at, cot),
            )
        )
    ]
    for copy in copies:
        copy.start()
    for copy in copies:
        copy.wait()
    odd_row, odd_col = is_odd("ha"), is_odd("wa")
    sources = (
        (cache_in, 0), (cache_in, 1), (frames_in, 0), (cache_mid, 0), (cache_mid, 1), (cot, 0)
    )
    last = rows - RIM
    near_at, far_at = jnp.where(odd_row, 0, last), jnp.where(odd_row, last, 0)
    for frame, (ref, i) in enumerate(sources):
        row_near[frame] = ref[i, pl.ds(near_at, RIM)]
        row_far[frame] = ref[i, pl.ds(far_at, RIM)]
    lanes = col_near.shape[-1]
    lower = lax.broadcasted_iota(jnp.int32, (rows, 2 * RIM, lanes), 1) < RIM

    def edges(frame):
        ref, i = sources[frame]
        value = ref[i].astype(F32)
        return value[:, : 2 * RIM], pltpu.roll(value[:, cols - 2 * RIM :], RIM, 1)

    near, far = [], []
    for pair in range(3):
        (head, tail), (head_b, tail_b) = edges(2 * pair), edges(2 * pair + 1)
        heads = jnp.where(lower, head, pltpu.roll(head_b, RIM, 1))
        tails = jnp.where(lower, tail, pltpu.roll(tail_b, RIM, 1))
        near.append(jnp.where(odd_col, heads, tails))
        far.append(jnp.where(odd_col, tails, heads))
    col_near[...] = jnp.stack(near, axis=1).reshape(-1, lanes).astype(BF)
    col_far[...] = jnp.stack(far, axis=1).reshape(-1, lanes).astype(BF)


def ready_kernel(
    w_one, w_two, sc_one, sh_one, sc_two, sh_two, ahead_one, ahead_two, back_one, back_two, affine
):
    lanes = affine.shape[-1]
    for weight, ahead, back in ((w_one, ahead_one, back_one), (w_two, ahead_two, back_two)):
        for a in range(3):
            for b in range(3):
                for c in range(3):
                    at = (a * 3 + b) * lanes
                    ahead[at : at + lanes, c * lanes : (c + 1) * lanes] = weight[a, b, c]
        for b in range(3):
            for c in range(3):
                back[c * lanes : (c + 1) * lanes, b * lanes : (b + 1) * lanes] = weight[2, b, c]
    affine[...] = jnp.concatenate(
        [1.0 + sc_one[...], sh_one[...], 1.0 + sc_two[...], sh_two[...]] * 2, axis=0
    )


def middle_kernel(
    rows, cols, cache_in, frames_in, cache_mid, cot, col_near, col_far, ahead_one, ahead_two, affine,
    field, slope_mid, a_mid, d_mid, moved_mid,
):
    block = [cache_in[0], cache_in[1], frames_in[0], cache_mid[0], cache_mid[1], cot[0]]
    for frame, value in enumerate(join(block, col_near[...], col_far[...])):
        field[frame] = value
    own = [Rows((RIM, Frame(field, i), rows)) for i in range(6)]
    first = RIM + 1
    for start, count in cut(first, RIM + rows - 1, 2):
        a_one, slope_one = first_layer(rows, cols, own[:3], ahead_one, affine, [(start, count)])
        a_mid[start - first : start - first + count] = a_one
        slope_mid[start - first : start - first + count] = slope_one
    frames = own[3:5] + [Rows((first, a_mid, rows - 2))]
    second = RIM + 2
    for start, count in cut(second, RIM + rows - 2, 2):
        value = second_layer(frames, own[5], ahead_two, affine, [(start, count)])
        d_mid[start - second : start - second + count] = value.astype(BF)
        moved_mid[start - second : start - second + count] = spread(cols, value)


def rim_kernel(
    rows, cols, field, slope_mid, a_mid, d_mid, moved_mid, row_near, row_far, corner_near, corner_far,
    ahead_one, ahead_two, back_two, affine, keep, send, d_one,
    top, bottom, slope_rim, a_rim, d_rim, moved_rim, moved_one, grads, sems,
):
    lanes = affine.shape[-1]
    tall = rows + 2 * RIM
    core = lax.axis_index("ha") % 2
    half = corner_near.shape[0] // 2

    def assemble(target, block, corner):
        parts = join([block[i] for i in range(6)], corner[:half], corner[half:])
        for frame, value in enumerate(parts):
            target[frame] = value

    @pl.when(is_odd("ha"))
    def _():
        assemble(top, row_near, corner_near)
        assemble(bottom, row_far, corner_far)

    @pl.when(jnp.logical_not(is_odd("ha")))
    def _():
        assemble(top, row_far, corner_far)
        assemble(bottom, row_near, corner_near)

    whole = [
        Rows(
            (0, Frame(top, i), RIM),
            (RIM, Frame(field, i), rows),
            (RIM + rows, Frame(bottom, i), RIM),
        )
        for i in range(6)
    ]

    def around(rim, mid, first, count):
        size = mid.shape[0]
        return Rows(
            (first, rim, count),
            (first + count, mid, size),
            (first + count + size, Shifted(rim, count), count),
        )

    used = 27 * lanes
    if grads.shape[1] > used:
        grads[:, used:, :] = jnp.zeros((2, grads.shape[1] - used, lanes), BF)
    edge = jnp.zeros((2,) + moved_rim.shape[1:], BF)
    moved_rim[0:2] = edge
    moved_rim[6:8] = edge
    moved_one[0:2] = edge
    moved_one[rows + 2 : rows + 4] = edge

    def gradient(which, frames, moved):
        lhs = jnp.concatenate([flat(frames[a].get(RIM - 1, rows + 2)) for a in range(3)], axis=1)
        for b in range(3):
            rhs = flat(moved.get(RIM - b, rows + 2))
            out = lax.dot_general(lhs, rhs, (((0,), (0,)), ((), ())), preferred_element_type=F32)
            for a in range(3):
                for c in range(3):
                    at = ((a * 3 + b) * 3 + c) * lanes
                    grads[which, at : at + lanes, :] = out[
                        a * lanes : (a + 1) * lanes, c * lanes : (c + 1) * lanes
                    ].astype(BF)

        @pl.when(core == which)
        def _():
            pltpu.make_async_copy(grads.at[which], keep, sems.at[0]).start()

        @pl.when(core != which)
        def _():
            pltpu.make_async_copy(grads.at[which], send, sems.at[1]).start()

    blocks = [(1, 4), (tall - 5, 4)]
    a_value, slope_value = first_layer(rows, cols, whole[:3], ahead_one, affine, blocks)
    a_rim[...] = a_value
    slope_rim[...] = slope_value
    a_all = around(a_rim, a_mid, 1, 4)
    slope_all = around(slope_rim, slope_mid, 1, 4)

    frames = whole[3:5] + [a_all]
    value = second_layer(frames, whole[5], ahead_two, affine, [(2, 4), (tall - 6, 4)])
    d_rim[...] = value.astype(BF)
    moved_rim[2:6] = spread(cols, value[2:6])
    d_all = around(d_rim, d_mid, 2, 4)
    gradient(1, frames, around(moved_rim, moved_mid, 2, 4))

    for start, count in cut(3, tall - 3, 2):
        value = backward(d_all, back_two, start, count) * slope_all.get(start, count)
        d_one[start - 3 : start - 3 + count] = value.astype(BF)
        low, high = max(start, RIM), min(start + count, RIM + rows)
        moved_one[low - 2 : high - 2] = spread(cols, value[low - start : high - start])
    gradient(0, whole[:3], Rows((2, moved_one, rows + 4)))

    pltpu.make_async_copy(grads.at[core], keep, sems.at[0]).wait()
    pltpu.make_async_copy(grads.at[1 - core], send, sems.at[1]).wait()


class Shifted:
    def __init__(self, ref, by):
        self.ref, self.by = ref, by

    def __getitem__(self, key):
        return self.ref[key.start + self.by : key.stop + self.by]


def input_kernel(rows, cols, d_one, back_one, gin):
    field = Rows((RIM - 1, d_one, rows + 2))
    for start, count in cut(RIM, RIM + rows, 2):
        value = backward(field, back_one, start, count)
        gin[0, start - RIM : start - RIM + count] = value[:, :cols].astype(BF)


def place_kernel(parts, first, source, *refs):
    one, other, wide, sems = refs[-4:]
    size = wide.shape[0] // parts
    own_first = jnp.logical_not(is_odd("ha"))
    to_one = own_first if first else jnp.logical_not(own_first)
    for part in range(parts):
        at = pl.ds(part * size, size)
        wide[at, :] = source[at, :].astype(F32)

        @pl.when(to_one)
        def _():
            pltpu.make_async_copy(wide.at[at], one.at[at], sems.at[part]).start()

        @pl.when(jnp.logical_not(to_one))
        def _():
            pltpu.make_async_copy(wide.at[at], other.at[at], sems.at[part]).start()

    for part in range(parts):
        at = pl.ds(part * size, size)
        pltpu.make_async_copy(wide.at[at], one.at[at], sems.at[part]).wait()


def per_device(
    frames_in, cache_in, cache_mid, w_first, w_second,
    scale_first, shift_first, scale_second, shift_second, cotangent,
):
    _, rows, cols, chans = frames_in.shape
    devices = lax.axis_size("ha") * lax.axis_size("wa")
    factor = 1.0 / (rows * cols * devices) ** 0.5
    full, tall = cols + 2 * RIM, rows + 2 * RIM
    FULL[0] = full
    chips = devices // 2
    total = 27 * chans
    share = -(-total // (8 * chips)) * 8
    inner = pl.BlockSpec(memory_space=pltpu.VMEM)
    anywhere = pl.BlockSpec(memory_space=pl.ANY)

    def shaped(*shape, dtype=BF):
        return jax.ShapeDtypeStruct(shape, dtype)

    def call(kernel, name, out_shape, mebibytes, flops, args, sizes=True, **kwargs):
        def body(*refs):
            kernel(rows, cols, *refs) if sizes else kernel(*refs)

        count = len(out_shape)
        kwargs.setdefault("in_specs", [inner] * len(args))
        kwargs.setdefault("out_specs", (inner,) * count)
        return pl.pallas_call(
            body,
            out_shape=tuple(out_shape),
            cost_estimate=pl.CostEstimate(
                flops=int(flops), bytes_accessed=8 * 10**6, transcendentals=0
            ),
            compiler_params=pltpu.CompilerParams(vmem_limit_bytes=mebibytes * 2**20),
            name=name,
            **kwargs,
        )(*args)

    fields = (cache_in, frames_in, cache_mid, cotangent)
    rim_rows, rim_cols = shaped(6, RIM, cols, chans), shaped(6 * rows * RIM, chans)
    row_near, row_far, col_near, col_far = call(
        pack_kernel, "pack", (rim_rows, rim_rows, rim_cols, rim_cols), 60, 1e9, fields,
        in_specs=[anywhere] * 4,
        scratch_shapes=[pltpu.VMEM(v.shape, BF) for v in fields] + [pltpu.SemaphoreType.DMA((4,))],
    )
    ahead, back = shaped(9 * chans, 3 * chans), shaped(3 * chans, 3 * chans)
    ahead_one, ahead_two, back_one, back_two, affine = call(
        ready_kernel, "ready", (ahead, ahead, back, back, shaped(8, chans, dtype=F32)), 16, 2e9,
        (w_first, w_second, scale_first, shift_first, scale_second, shift_second), sizes=False,
    )
    col_near, col_far = trade("wa", col_near, col_far)
    row_near, row_far = trade("ha", row_near, row_far)
    size = 6 * RIM * RIM
    head = jnp.concatenate([col_near[:size], col_far[:size]], axis=0)
    tail = jnp.concatenate([col_near[-size:], col_far[-size:]], axis=0)
    odd = is_odd("ha")
    corner_near, corner_far = trade("ha", jnp.where(odd, head, tail), jnp.where(odd, tail, head))

    field, slope_mid, a_mid, d_mid, moved_mid = call(
        middle_kernel, "middle",
        (
            shaped(6, rows, full, chans),
            shaped(rows - 2, full, chans, dtype=F32),
            shaped(rows - 2, full, chans),
            shaped(rows - 4, full, chans),
            shaped(rows - 4, full, 3 * chans),
        ),
        28, 5e9, (*fields, col_near, col_far, ahead_one, ahead_two, affine),
    )
    keep, send, d_one = call(
        rim_kernel, "rim",
        (shaped(share * chips, chans), shaped(share * chips, chans), shaped(rows + 2, full, chans)),
        28, 5e9,
        (
            field, slope_mid, a_mid, d_mid, moved_mid, row_near, row_far, corner_near, corner_far,
            ahead_one, ahead_two, back_two, affine,
        ),
        out_specs=(anywhere, anywhere, inner),
        scratch_shapes=[
            pltpu.VMEM((6, RIM, full, chans), BF),
            pltpu.VMEM((6, RIM, full, chans), BF),
            pltpu.VMEM((8, full, chans), F32),
            pltpu.VMEM((8, full, chans), BF),
            pltpu.VMEM((8, full, chans), BF),
            pltpu.VMEM((8, full, 3 * chans), BF),
            pltpu.VMEM((rows + 4, full, 3 * chans), BF),
            pltpu.VMEM((2, share * chips, chans), BF),
            pltpu.SemaphoreType.DMA((2,)),
        ],
    )

    pairs, _ = swaps("ha")
    got = lax.ppermute(send, "ha", pairs)
    (grad_input,) = call(
        input_kernel, "input", (shaped(1, rows, cols, chans),), 12, 1e9, (d_one, back_one)
    )
    got, grad_input = lax.optimization_barrier((got, grad_input))
    chip_sum = (keep.astype(F32) + got.astype(F32)).astype(BF)
    cores = [[c for c in range(devices) if (c // lax.axis_size("wa")) % 2 == k] for k in range(2)]

    def spread_out(value):
        return lax.all_to_all(
            value.reshape(chips, share, chans), BOTH, 0, 0, axis_index_groups=cores, tiled=True
        )

    mine = (jnp.sum(spread_out(chip_sum).astype(F32), axis=0) * factor).astype(BF)
    one = spread_out(jnp.broadcast_to(mine[None], (chips, share, chans))).reshape(-1, chans)
    other = lax.ppermute(one, "ha", pairs)
    shape = (3, 3, 3, chans, chans)
    parts = 4

    def place(source, *given):
        return call(
            lambda *refs: place_kernel(parts, not given, *refs), "place",
            [shaped(total, chans, dtype=F32)] * 2, 8, 2e9, (source, *given), sizes=False,
            in_specs=[inner] + [anywhere] * len(given),
            out_specs=(anywhere, anywhere),
            scratch_shapes=[
                pltpu.VMEM((total, chans), F32), pltpu.SemaphoreType.DMA((parts,))
            ],
            input_output_aliases={1: 0, 2: 1} if given else {},
        )

    grad_first, grad_second = place(other, *place(one))
    return (grad_input, grad_first.reshape(shape), grad_second.reshape(shape))


def solution(mesh):
    tiled = P(None, "ha", "wa", None)
    return jax.shard_map(
        per_device,
        mesh=mesh,
        in_specs=(tiled, tiled, tiled, P(), P(), P(), P(), P(), P(), tiled),
        out_specs=(tiled, P(), P()),
        check_vma=False,
    )
```

```python
import jax
import jax.numpy as jnp
from jax import lax
from jax.experimental import pallas as pl
from jax.experimental.pallas import tpu as pltpu
from jax.sharding import PartitionSpec as P

BF = jnp.bfloat16
F32 = jnp.float32
RIM = 4
BOTH = ("ha", "wa")


def swaps(axis):
    count = lax.axis_size(axis)
    first = [(i, i ^ 1) for i in range(count)]
    second = [(i, i + 1 if i % 2 else i - 1) for i in range(1, count - 1)]
    return first, second


def trade(axis, near, far):
    first, second = swaps(axis)
    return lax.ppermute(near, axis, first), lax.ppermute(far, axis, second)


def is_odd(axis):
    return lax.axis_index(axis) % 2 == 1


def slope(value):
    sig = jax.nn.sigmoid(value)
    return sig * (1.0 + value * (1.0 - sig))


def flat(value):
    return value.reshape(-1, value.shape[-1])


def turn(value, step):
    return pltpu.roll(value, step % value.shape[1], 1)


def join(block, near, far):
    high, _, lanes = block[0].shape
    odd = is_odd("wa")
    near, far = near.astype(F32), far.astype(F32)
    left = jnp.where(odd, near, far).reshape(high, 3, 2 * RIM, lanes)
    right = jnp.where(odd, far, near).reshape(high, 3, 2 * RIM, lanes)
    lower = lax.broadcasted_iota(jnp.int32, (high, 2 * RIM, lanes), 1) < RIM
    frames, rims = [], []
    for frame in range(6):
        one, other = right[:, frame // 2], left[:, frame // 2]
        if frame % 2 == 0:
            rim = jnp.where(lower, one, pltpu.roll(other, RIM, 1))
        else:
            rim = jnp.where(lower, pltpu.roll(one, RIM, 1), other)
        frames.append(jnp.concatenate([block[frame].astype(F32), rim], axis=1).astype(BF))
        rims.append(rim)
    return frames, rims


class Rows:
    def __init__(self, *pieces):
        self.pieces = pieces

    def get(self, start, count):
        out = []
        for first, ref, size in self.pieces:
            low, high = max(start, first), min(start + count, first + size)
            if low < high:
                out.append(ref[low - first : high - first])
        return out[0] if len(out) == 1 else jnp.concatenate(out, axis=0)


class Frame:
    def __init__(self, ref, index):
        self.ref, self.index = ref, index

    def __getitem__(self, key):
        return self.ref[self.index, key]


def forward(frames, weight, blocks):
    lhs = jnp.concatenate(
        [
            jnp.concatenate(
                [flat(frames[a].get(start - 1 + b, count)) for start, count in blocks], axis=0
            )
            for a in range(len(frames))
            for b in range(3)
        ],
        axis=1,
    )
    out = jnp.dot(lhs, weight, preferred_element_type=F32)
    return gather_columns(out, 1)


def rim_forward(rims, weight, start, count, cols):
    lhs = jnp.concatenate(
        [
            flat(rim[start - 1 + b - RIM : start - 1 + b - RIM + count])
            for rim in rims
            for b in range(3)
        ],
        axis=1,
    ).astype(BF)
    out = jnp.dot(lhs, weight, preferred_element_type=F32)
    lanes = out.shape[-1] // 3
    out = out.reshape(count, 2 * RIM, 3 * lanes)
    place = lax.broadcasted_iota(jnp.int32, (count, 2 * RIM, lanes), 1)
    last = 2 * RIM - 1
    from_left, from_right = turn(out[..., :lanes], 1), turn(out[..., 2 * lanes :], -1)
    here = (
        out[..., lanes : 2 * lanes]
        + jnp.where(place > 0, from_left, 0.0)
        + jnp.where(place < last, from_right, 0.0)
    )
    return jnp.concatenate(
        [
            jnp.where(place == 0, from_left, 0.0),
            jnp.zeros((count, cols - 4 * RIM, lanes), F32),
            jnp.where(place == last, from_right, 0.0),
            here,
        ],
        axis=1,
    )


def backward(field, weight, start, count):
    lhs = jnp.concatenate([flat(field.get(start + 1 - b, count)) for b in range(3)], axis=1)
    out = lax.dot_general(lhs, weight[...], (((1,), (1,)), ((), ())), preferred_element_type=F32)
    return gather_columns(out, -1)


def gather_columns(out, step):
    lanes = out.shape[-1] // 3
    out = out.reshape(-1, FULL[0], 3 * lanes)
    return (
        turn(out[..., :lanes], step)
        + out[..., lanes : 2 * lanes]
        + turn(out[..., 2 * lanes :], -step)
    )


FULL = [0]


def in_image(rows, cols, lanes, blocks):
    full = cols + 2 * RIM
    image_rows, image_cols = rows * lax.axis_size("ha"), cols * lax.axis_size("wa")
    col = lax.broadcasted_iota(jnp.int32, (1, full, lanes), 1)
    place = jnp.where(col < cols + RIM, col, col - full) + lax.axis_index("wa") * cols
    col_in = (place >= 0) & (place < image_cols)
    out = []
    for start, count in blocks:
        row = lax.broadcasted_iota(jnp.int32, (count, full, lanes), 0)
        row = row + (start - RIM) + lax.axis_index("ha") * rows
        out.append((row >= 0) & (row < image_rows) & col_in)
    return jnp.concatenate(out, axis=0) if len(out) > 1 else out[0]


def first_layer(rows, cols, conv, affine, blocks):
    lanes = affine.shape[-1]
    gain, bias = (affine[i : i + 1, :].reshape(1, 1, lanes) for i in (0, 1))
    m_one = conv * gain + bias
    sig = jax.nn.sigmoid(m_one)
    inside = in_image(rows, cols, lanes, blocks)
    a_one = jnp.where(inside, m_one * sig, 0.0).astype(BF)
    slope_one = jnp.where(inside, sig * (1.0 + m_one * (1.0 - sig)) * gain, 0.0)
    return a_one, slope_one


def second_layer(conv, cot, affine, blocks):
    lanes = affine.shape[-1]
    gain, bias = (affine[i : i + 1, :].reshape(1, 1, lanes) for i in (2, 3))
    m_two = conv * gain + bias
    pulled = [cot.get(start, count) for start, count in blocks]
    pulled = jnp.concatenate(pulled, axis=0) if len(pulled) > 1 else pulled[0]
    return pulled.astype(F32) * slope(m_two) * gain


def spread(cols, value):
    own = lax.broadcasted_iota(jnp.int32, (1,) + value.shape[1:], 1) < cols
    kept = jnp.where(own, value, 0.0)
    return jnp.concatenate([turn(kept, -1), kept, turn(kept, 1)], axis=2).astype(BF)


def cut(start, stop, parts):
    step = -(-(stop - start) // parts)
    return [(at, min(step, stop - at)) for at in range(start, stop, step)]


def pack_kernel(
    rows, cols, cache_in_at, frames_in_at, cache_mid_at, cot_at, row_near, row_far, col_near, col_far,
    cache_in, frames_in, cache_mid, cot, sems,
):
    copies = [
        pltpu.make_async_copy(source, target, sems.at[i])
        for i, (source, target) in enumerate(
            (
                (cache_in_at, cache_in),
                (frames_in_at, frames_in),
                (cache_mid_at, cache_mid),
                (cot_at, cot),
            )
        )
    ]
    odd_row, odd_col = is_odd("ha"), is_odd("wa")
    last = rows - RIM
    near_at, far_at = jnp.where(odd_row, 0, last), jnp.where(odd_row, last, 0)
    for copy in copies:
        copy.start()
    straight, frame = [], 0
    for source in (cache_in_at, frames_in_at, cache_mid_at, cot_at):
        size = source.shape[0]
        for start, target in ((near_at, row_near), (far_at, row_far)):
            straight.append(
                pltpu.make_async_copy(
                    source.at[:, pl.ds(start, RIM)],
                    target.at[frame : frame + size],
                    sems.at[4 + len(straight)],
                )
            )
            straight[-1].start()
        frame += size
    for copy in copies:
        copy.wait()
    sources = (
        (cache_in, 0), (cache_in, 1), (frames_in, 0), (cache_mid, 0), (cache_mid, 1), (cot, 0)
    )
    lanes = col_near.shape[-1]
    lower = lax.broadcasted_iota(jnp.int32, (rows, 2 * RIM, lanes), 1) < RIM

    def edges(frame):
        ref, i = sources[frame]
        value = ref[i].astype(F32)
        return value[:, : 2 * RIM], pltpu.roll(value[:, cols - 2 * RIM :], RIM, 1)

    near, far = [], []
    for pair in range(3):
        (head, tail), (head_b, tail_b) = edges(2 * pair), edges(2 * pair + 1)
        heads = jnp.where(lower, head, pltpu.roll(head_b, RIM, 1))
        tails = jnp.where(lower, tail, pltpu.roll(tail_b, RIM, 1))
        near.append(jnp.where(odd_col, heads, tails))
        far.append(jnp.where(odd_col, tails, heads))
    col_near[...] = jnp.stack(near, axis=1).reshape(-1, lanes).astype(BF)
    col_far[...] = jnp.stack(far, axis=1).reshape(-1, lanes).astype(BF)
    for copy in straight:
        copy.wait()


def ready_kernel(
    w_one, w_two, sc_one, sh_one, sc_two, sh_two, ahead_one, ahead_two, back_one, back_two, affine
):
    lanes = affine.shape[-1]
    for weight, ahead, back in ((w_one, ahead_one, back_one), (w_two, ahead_two, back_two)):
        for a in range(3):
            for b in range(3):
                for c in range(3):
                    at = (a * 3 + b) * lanes
                    ahead[at : at + lanes, c * lanes : (c + 1) * lanes] = weight[a, b, c]
        for b in range(3):
            for c in range(3):
                back[c * lanes : (c + 1) * lanes, b * lanes : (b + 1) * lanes] = weight[2, b, c]
    affine[...] = jnp.concatenate(
        [1.0 + sc_one[...], sh_one[...], 1.0 + sc_two[...], sh_two[...]] * 2, axis=0
    )


def own_kernel(
    rows, cols, cache_in, frames_in, cache_mid, ahead_one, ahead_two, part_one, part_two, field
):
    block = [cache_in[0], cache_in[1], frames_in[0], cache_mid[0], cache_mid[1]]
    none = jnp.zeros((rows, 2 * RIM, block[0].shape[-1]), F32)
    for i, value in enumerate(block):
        field[i] = jnp.concatenate([value.astype(F32), none], axis=1).astype(BF)
    own = [Rows((RIM, Frame(field, i), rows)) for i in range(5)]
    split = 6 * none.shape[-1]
    for frames, weight, part, first in (
        (own[:3], ahead_one[...], part_one, RIM + 1),
        (own[3:], ahead_two[:split], part_two, RIM + 2),
    ):
        for start, count in cut(first, 2 * RIM + rows - first, 2):
            part[start - first : start - first + count] = forward(frames, weight, [(start, count)])


def middle_kernel(
    rows, cols, cache_in, frames_in, cache_mid, cot, col_near, col_far, part_one, part_two,
    ahead_one, ahead_two, affine, field, slope_mid, a_mid, d_mid, moved_mid,
):
    block = [cache_in[0], cache_in[1], frames_in[0], cache_mid[0], cache_mid[1], cot[0]]
    frames, rims = join(block, col_near[...], col_far[...])
    for frame, value in enumerate(frames):
        field[frame] = value
    split = 6 * affine.shape[-1]
    first = RIM + 1
    for start, count in cut(first, RIM + rows - 1, 2):
        at = slice(start - first, start - first + count)
        conv = part_one[at] + rim_forward(rims[:3], ahead_one[...], start, count, cols)
        a_mid[at], slope_mid[at] = first_layer(rows, cols, conv, affine, [(start, count)])
    a_one, cotangent = Rows((first, a_mid, rows - 2)), Rows((RIM, Frame(field, 5), rows))
    second = RIM + 2
    for start, count in cut(second, RIM + rows - 2, 2):
        at = slice(start - second, start - second + count)
        conv = (
            part_two[at]
            + forward([a_one], ahead_two[split:], [(start, count)])
            + rim_forward(rims[3:5], ahead_two[:split], start, count, cols)
        )
        value = second_layer(conv, cotangent, affine, [(start, count)])
        d_mid[at] = value.astype(BF)
        moved_mid[at] = spread(cols, value)


def rim_kernel(
    rows, cols, field, slope_mid, a_mid, d_mid, moved_mid, row_near, row_far, corner_near, corner_far,
    ahead_one, ahead_two, back_two, affine, keep, send, d_one,
    top, bottom, slope_rim, a_rim, d_rim, moved_rim, moved_one, grads, sems,
):
    lanes = affine.shape[-1]
    tall = rows + 2 * RIM
    core = lax.axis_index("ha") % 2
    half = corner_near.shape[0] // 2

    def assemble(target, block, corner):
        parts, _ = join([block[i] for i in range(6)], corner[:half], corner[half:])
        for frame, value in enumerate(parts):
            target[frame] = value

    @pl.when(is_odd("ha"))
    def _():
        assemble(top, row_near, corner_near)
        assemble(bottom, row_far, corner_far)

    @pl.when(jnp.logical_not(is_odd("ha")))
    def _():
        assemble(top, row_far, corner_far)
        assemble(bottom, row_near, corner_near)

    whole = [
        Rows(
            (0, Frame(top, i), RIM),
            (RIM, Frame(field, i), rows),
            (RIM + rows, Frame(bottom, i), RIM),
        )
        for i in range(6)
    ]

    def around(rim, mid, first, count):
        size = mid.shape[0]
        return Rows(
            (first, rim, count),
            (first + count, mid, size),
            (first + count + size, Shifted(rim, count), count),
        )

    used = 27 * lanes
    if grads.shape[1] > used:
        grads[:, used:, :] = jnp.zeros((2, grads.shape[1] - used, lanes), BF)
    edge = jnp.zeros((2,) + moved_rim.shape[1:], BF)
    moved_rim[0:2] = edge
    moved_rim[6:8] = edge
    moved_one[0:2] = edge
    moved_one[rows + 2 : rows + 4] = edge

    def gradient(which, frames, moved):
        lhs = jnp.concatenate([flat(frames[a].get(RIM - 1, rows + 2)) for a in range(3)], axis=1)
        for b in range(3):
            rhs = flat(moved.get(RIM - b, rows + 2))
            out = lax.dot_general(lhs, rhs, (((0,), (0,)), ((), ())), preferred_element_type=F32)
            for a in range(3):
                for c in range(3):
                    at = ((a * 3 + b) * 3 + c) * lanes
                    grads[which, at : at + lanes, :] = out[
                        a * lanes : (a + 1) * lanes, c * lanes : (c + 1) * lanes
                    ].astype(BF)

        @pl.when(core == which)
        def _():
            pltpu.make_async_copy(grads.at[which], keep, sems.at[0]).start()

        @pl.when(core != which)
        def _():
            pltpu.make_async_copy(grads.at[which], send, sems.at[1]).start()

    blocks = [(1, 4), (tall - 5, 4)]
    conv = forward(whole[:3], ahead_one[...], blocks)
    a_value, slope_value = first_layer(rows, cols, conv, affine, blocks)
    a_rim[...] = a_value
    slope_rim[...] = slope_value
    a_all = around(a_rim, a_mid, 1, 4)
    slope_all = around(slope_rim, slope_mid, 1, 4)

    frames = whole[3:5] + [a_all]
    blocks = [(2, 4), (tall - 6, 4)]
    value = second_layer(forward(frames, ahead_two[...], blocks), whole[5], affine, blocks)
    d_rim[...] = value.astype(BF)
    moved_rim[2:6] = spread(cols, value[2:6])
    d_all = around(d_rim, d_mid, 2, 4)
    gradient(1, frames, around(moved_rim, moved_mid, 2, 4))

    for start, count in cut(3, tall - 3, 2):
        value = backward(d_all, back_two, start, count) * slope_all.get(start, count)
        d_one[start - 3 : start - 3 + count] = value.astype(BF)
        low, high = max(start, RIM), min(start + count, RIM + rows)
        moved_one[low - 2 : high - 2] = spread(cols, value[low - start : high - start])
    gradient(0, whole[:3], Rows((2, moved_one, rows + 4)))

    pltpu.make_async_copy(grads.at[core], keep, sems.at[0]).wait()
    pltpu.make_async_copy(grads.at[1 - core], send, sems.at[1]).wait()


class Shifted:
    def __init__(self, ref, by):
        self.ref, self.by = ref, by

    def __getitem__(self, key):
        return self.ref[key.start + self.by : key.stop + self.by]


def input_kernel(rows, cols, d_one, back_one, gin):
    field = Rows((RIM - 1, d_one, rows + 2))
    for start, count in cut(RIM, RIM + rows, 2):
        value = backward(field, back_one, start, count)
        gin[0, start - RIM : start - RIM + count] = value[:, :cols].astype(BF)


def place_kernel(parts, first, source, *refs):
    one, other, wide, sems = refs[-4:]
    size = wide.shape[0] // parts
    own_first = jnp.logical_not(is_odd("ha"))
    to_one = own_first if first else jnp.logical_not(own_first)
    for part in range(parts):
        at = pl.ds(part * size, size)
        wide[at, :] = source[at, :].astype(F32)

        @pl.when(to_one)
        def _():
            pltpu.make_async_copy(wide.at[at], one.at[at], sems.at[part]).start()

        @pl.when(jnp.logical_not(to_one))
        def _():
            pltpu.make_async_copy(wide.at[at], other.at[at], sems.at[part]).start()

    for part in range(parts):
        at = pl.ds(part * size, size)
        pltpu.make_async_copy(wide.at[at], one.at[at], sems.at[part]).wait()


def per_device(
    frames_in, cache_in, cache_mid, w_first, w_second,
    scale_first, shift_first, scale_second, shift_second, cotangent,
):
    _, rows, cols, chans = frames_in.shape
    devices = lax.axis_size("ha") * lax.axis_size("wa")
    factor = 1.0 / (rows * cols * devices) ** 0.5
    full, tall = cols + 2 * RIM, rows + 2 * RIM
    FULL[0] = full
    chips = devices // 2
    total = 27 * chans
    share = -(-total // (8 * chips)) * 8
    inner = pl.BlockSpec(memory_space=pltpu.VMEM)
    anywhere = pl.BlockSpec(memory_space=pl.ANY)

    def shaped(*shape, dtype=BF):
        return jax.ShapeDtypeStruct(shape, dtype)

    def call(kernel, name, out_shape, mebibytes, flops, args, sizes=True, **kwargs):
        def body(*refs):
            kernel(rows, cols, *refs) if sizes else kernel(*refs)

        count = len(out_shape)
        kwargs.setdefault("in_specs", [inner] * len(args))
        kwargs.setdefault("out_specs", (inner,) * count)
        return pl.pallas_call(
            body,
            out_shape=tuple(out_shape),
            cost_estimate=pl.CostEstimate(
                flops=int(flops), bytes_accessed=8 * 10**6, transcendentals=0
            ),
            compiler_params=pltpu.CompilerParams(vmem_limit_bytes=mebibytes * 2**20),
            name=name,
            **kwargs,
        )(*args)

    fields = (cache_in, frames_in, cache_mid, cotangent)
    rim_rows, rim_cols = shaped(6, RIM, cols, chans), shaped(6 * rows * RIM, chans)
    row_near, row_far, col_near, col_far = call(
        pack_kernel, "pack", (rim_rows, rim_rows, rim_cols, rim_cols), 60, 1e9, fields,
        in_specs=[anywhere] * 4,
        out_specs=(anywhere, anywhere, inner, inner),
        scratch_shapes=[pltpu.VMEM(v.shape, BF) for v in fields] + [pltpu.SemaphoreType.DMA((12,))],
    )
    ahead, back = shaped(9 * chans, 3 * chans), shaped(3 * chans, 3 * chans)
    ahead_one, ahead_two, back_one, back_two, affine = call(
        ready_kernel, "ready", (ahead, ahead, back, back, shaped(8, chans, dtype=F32)), 16, 2e9,
        (w_first, w_second, scale_first, shift_first, scale_second, shift_second), sizes=False,
    )
    part_one, part_two = call(
        own_kernel, "own",
        (
            shaped(rows - 2, full, chans, dtype=F32),
            shaped(rows - 4, full, chans, dtype=F32),
        ),
        24, 4e9, (cache_in, frames_in, cache_mid, ahead_one, ahead_two),
        scratch_shapes=[pltpu.VMEM((5, rows, full, chans), BF)],
    )
    col_near, col_far = trade("wa", col_near, col_far)
    row_near, row_far = trade("ha", row_near, row_far)
    size = 6 * RIM * RIM
    head = jnp.concatenate([col_near[:size], col_far[:size]], axis=0)
    tail = jnp.concatenate([col_near[-size:], col_far[-size:]], axis=0)
    odd = is_odd("ha")
    corner_near, corner_far = trade("ha", jnp.where(odd, head, tail), jnp.where(odd, tail, head))

    field, slope_mid, a_mid, d_mid, moved_mid = call(
        middle_kernel, "middle",
        (
            shaped(6, rows, full, chans),
            shaped(rows - 2, full, chans, dtype=F32),
            shaped(rows - 2, full, chans),
            shaped(rows - 4, full, chans),
            shaped(rows - 4, full, 3 * chans),
        ),
        28, 3e9, (*fields, col_near, col_far, part_one, part_two, ahead_one, ahead_two, affine),
    )
    keep, send, d_one = call(
        rim_kernel, "rim",
        (shaped(share * chips, chans), shaped(share * chips, chans), shaped(rows + 2, full, chans)),
        28, 5e9,
        (
            field, slope_mid, a_mid, d_mid, moved_mid, row_near, row_far, corner_near, corner_far,
            ahead_one, ahead_two, back_two, affine,
        ),
        out_specs=(anywhere, anywhere, inner),
        scratch_shapes=[
            pltpu.VMEM((6, RIM, full, chans), BF),
            pltpu.VMEM((6, RIM, full, chans), BF),
            pltpu.VMEM((8, full, chans), F32),
            pltpu.VMEM((8, full, chans), BF),
            pltpu.VMEM((8, full, chans), BF),
            pltpu.VMEM((8, full, 3 * chans), BF),
            pltpu.VMEM((rows + 4, full, 3 * chans), BF),
            pltpu.VMEM((2, share * chips, chans), BF),
            pltpu.SemaphoreType.DMA((2,)),
        ],
    )

    pairs, _ = swaps("ha")
    got = lax.ppermute(send, "ha", pairs)
    (grad_input,) = call(
        input_kernel, "input", (shaped(1, rows, cols, chans),), 12, 1e9, (d_one, back_one)
    )
    got, grad_input = lax.optimization_barrier((got, grad_input))
    chip_sum = (keep.astype(F32) + got.astype(F32)).astype(BF)
    cores = [[c for c in range(devices) if (c // lax.axis_size("wa")) % 2 == k] for k in range(2)]

    def spread_out(value):
        return lax.all_to_all(
            value.reshape(chips, share, chans), BOTH, 0, 0, axis_index_groups=cores, tiled=True
        )

    mine = (jnp.sum(spread_out(chip_sum).astype(F32), axis=0) * factor).astype(BF)
    one = spread_out(jnp.broadcast_to(mine[None], (chips, share, chans))).reshape(-1, chans)
    other = lax.ppermute(one, "ha", pairs)
    shape = (3, 3, 3, chans, chans)
    parts = 4

    def place(source, *given):
        return call(
            lambda *refs: place_kernel(parts, not given, *refs), "place",
            [shaped(total, chans, dtype=F32)] * 2, 8, 2e9, (source, *given), sizes=False,
            in_specs=[inner] + [anywhere] * len(given),
            out_specs=(anywhere, anywhere),
            scratch_shapes=[
                pltpu.VMEM((total, chans), F32), pltpu.SemaphoreType.DMA((parts,))
            ],
            input_output_aliases={1: 0, 2: 1} if given else {},
        )

    grad_first, grad_second = place(other, *place(one))
    return (grad_input, grad_first.reshape(shape), grad_second.reshape(shape))


def solution(mesh):
    tiled = P(None, "ha", "wa", None)
    return jax.shard_map(
        per_device,
        mesh=mesh,
        in_specs=(tiled, tiled, tiled, P(), P(), P(), P(), P(), P(), tiled),
        out_specs=(tiled, P(), P()),
        check_vma=False,
    )
```

```python
import jax
import jax.numpy as jnp
from jax import lax
from jax.experimental import pallas as pl
from jax.experimental.pallas import tpu as pltpu
from jax.sharding import PartitionSpec as P

BF = jnp.bfloat16
F32 = jnp.float32
RIM = 4
BOTH = ("ha", "wa")


def swaps(axis):
    count = lax.axis_size(axis)
    first = [(i, i ^ 1) for i in range(count)]
    second = [(i, i + 1 if i % 2 else i - 1) for i in range(1, count - 1)]
    return first, second


def trade(axis, near, far):
    first, second = swaps(axis)
    return lax.ppermute(near, axis, first), lax.ppermute(far, axis, second)


def is_odd(axis):
    return lax.axis_index(axis) % 2 == 1


def slope(value):
    sig = jax.nn.sigmoid(value)
    return sig * (1.0 + value * (1.0 - sig))


def flat(value):
    return value.reshape(-1, value.shape[-1])


def turn(value, step):
    return pltpu.roll(value, step % value.shape[1], 1)


def join(block, near, far):
    high, _, lanes = block[0].shape
    odd = is_odd("wa")
    near, far = near.astype(F32), far.astype(F32)
    left = jnp.where(odd, near, far).reshape(high, 3, 2 * RIM, lanes)
    right = jnp.where(odd, far, near).reshape(high, 3, 2 * RIM, lanes)
    lower = lax.broadcasted_iota(jnp.int32, (high, 2 * RIM, lanes), 1) < RIM
    frames, rims = [], []
    for frame in range(6):
        one, other = right[:, frame // 2], left[:, frame // 2]
        if frame % 2 == 0:
            rim = jnp.where(lower, one, pltpu.roll(other, RIM, 1))
        else:
            rim = jnp.where(lower, pltpu.roll(one, RIM, 1), other)
        frames.append(jnp.concatenate([block[frame].astype(F32), rim], axis=1).astype(BF))
        rims.append(rim)
    return frames, rims


class Rows:
    def __init__(self, *pieces):
        self.pieces = pieces

    def get(self, start, count):
        out = []
        for first, ref, size in self.pieces:
            low, high = max(start, first), min(start + count, first + size)
            if low < high:
                out.append(ref[low - first : high - first])
        return out[0] if len(out) == 1 else jnp.concatenate(out, axis=0)


class Frame:
    def __init__(self, ref, index):
        self.ref, self.index = ref, index

    def __getitem__(self, key):
        return self.ref[self.index, key]


def forward(frames, weight, blocks):
    lhs = jnp.concatenate(
        [
            jnp.concatenate(
                [flat(frames[a].get(start - 1 + b, count)) for start, count in blocks], axis=0
            )
            for a in range(len(frames))
            for b in range(3)
        ],
        axis=1,
    )
    out = jnp.dot(lhs, weight, preferred_element_type=F32)
    return gather_columns(out, 1)


def rim_forward(rims, weight, start, count, cols):
    lhs = jnp.concatenate(
        [
            flat(rim[start - 1 + b - RIM : start - 1 + b - RIM + count])
            for rim in rims
            for b in range(3)
        ],
        axis=1,
    ).astype(BF)
    out = jnp.dot(lhs, weight, preferred_element_type=F32)
    lanes = out.shape[-1] // 3
    out = out.reshape(count, 2 * RIM, 3 * lanes)
    place = lax.broadcasted_iota(jnp.int32, (count, 2 * RIM, lanes), 1)
    last = 2 * RIM - 1
    from_left, from_right = turn(out[..., :lanes], 1), turn(out[..., 2 * lanes :], -1)
    here = (
        out[..., lanes : 2 * lanes]
        + jnp.where(place > 0, from_left, 0.0)
        + jnp.where(place < last, from_right, 0.0)
    )
    return jnp.concatenate(
        [
            jnp.where(place == 0, from_left, 0.0),
            jnp.zeros((count, cols - 4 * RIM, lanes), F32),
            jnp.where(place == last, from_right, 0.0),
            here,
        ],
        axis=1,
    )


def backward(field, weight, start, count):
    lhs = jnp.concatenate([flat(field.get(start + 1 - b, count)) for b in range(3)], axis=1)
    out = lax.dot_general(lhs, weight[...], (((1,), (1,)), ((), ())), preferred_element_type=F32)
    return gather_columns(out, -1)


def gather_columns(out, step):
    lanes = out.shape[-1] // 3
    out = out.reshape(-1, FULL[0], 3 * lanes)
    return (
        turn(out[..., :lanes], step)
        + out[..., lanes : 2 * lanes]
        + turn(out[..., 2 * lanes :], -step)
    )


FULL = [0]


def in_image(rows, cols, lanes, blocks):
    full = cols + 2 * RIM
    image_rows, image_cols = rows * lax.axis_size("ha"), cols * lax.axis_size("wa")
    col = lax.broadcasted_iota(jnp.int32, (1, full, lanes), 1)
    place = jnp.where(col < cols + RIM, col, col - full) + lax.axis_index("wa") * cols
    col_in = (place >= 0) & (place < image_cols)
    out = []
    for start, count in blocks:
        row = lax.broadcasted_iota(jnp.int32, (count, full, lanes), 0)
        row = row + (start - RIM) + lax.axis_index("ha") * rows
        out.append((row >= 0) & (row < image_rows) & col_in)
    return jnp.concatenate(out, axis=0) if len(out) > 1 else out[0]


def first_layer(rows, cols, conv, affine, blocks):
    lanes = affine.shape[-1]
    gain, bias = (affine[i : i + 1, :].reshape(1, 1, lanes) for i in (0, 1))
    m_one = conv * gain + bias
    sig = jax.nn.sigmoid(m_one)
    inside = in_image(rows, cols, lanes, blocks)
    a_one = jnp.where(inside, m_one * sig, 0.0).astype(BF)
    slope_one = jnp.where(inside, sig * (1.0 + m_one * (1.0 - sig)) * gain, 0.0)
    return a_one, slope_one


def second_layer(conv, cot, affine, blocks):
    lanes = affine.shape[-1]
    gain, bias = (affine[i : i + 1, :].reshape(1, 1, lanes) for i in (2, 3))
    m_two = conv * gain + bias
    pulled = [cot.get(start, count) for start, count in blocks]
    pulled = jnp.concatenate(pulled, axis=0) if len(pulled) > 1 else pulled[0]
    return pulled.astype(F32) * slope(m_two) * gain


def spread(cols, value):
    own = lax.broadcasted_iota(jnp.int32, (1,) + value.shape[1:], 1) < cols
    kept = jnp.where(own, value, 0.0)
    return jnp.concatenate([turn(kept, -1), kept, turn(kept, 1)], axis=2).astype(BF)


def cut(start, stop, parts):
    step = -(-(stop - start) // parts)
    return [(at, min(step, stop - at)) for at in range(start, stop, step)]


def pack_kernel(
    rows, cols, cache_in_at, frames_in_at, cache_mid_at, cot_at, row_near, row_far, col_near, col_far,
    cache_in, frames_in, cache_mid, cot, sems,
):
    copies = [
        pltpu.make_async_copy(source, target, sems.at[i])
        for i, (source, target) in enumerate(
            (
                (cache_in_at, cache_in),
                (frames_in_at, frames_in),
                (cache_mid_at, cache_mid),
                (cot_at, cot),
            )
        )
    ]
    odd_row, odd_col = is_odd("ha"), is_odd("wa")
    for copy in copies:
        copy.start()
    for copy in copies:
        copy.wait()
    sources = (
        (cache_in, 0), (cache_in, 1), (frames_in, 0), (cache_mid, 0), (cache_mid, 1), (cot, 0)
    )
    last = rows - RIM
    near_at, far_at = jnp.where(odd_row, 0, last), jnp.where(odd_row, last, 0)
    for frame, (ref, i) in enumerate(sources):
        row_near[frame] = ref[i, pl.ds(near_at, RIM)]
        row_far[frame] = ref[i, pl.ds(far_at, RIM)]
    lanes = col_near.shape[-1]
    lower = lax.broadcasted_iota(jnp.int32, (rows, 2 * RIM, lanes), 1) < RIM

    def edges(frame):
        ref, i = sources[frame]
        value = ref[i].astype(F32)
        return value[:, : 2 * RIM], pltpu.roll(value[:, cols - 2 * RIM :], RIM, 1)

    near, far = [], []
    for pair in range(3):
        (head, tail), (head_b, tail_b) = edges(2 * pair), edges(2 * pair + 1)
        heads = jnp.where(lower, head, pltpu.roll(head_b, RIM, 1))
        tails = jnp.where(lower, tail, pltpu.roll(tail_b, RIM, 1))
        near.append(jnp.where(odd_col, heads, tails))
        far.append(jnp.where(odd_col, tails, heads))
    col_near[...] = jnp.stack(near, axis=1).reshape(-1, lanes).astype(BF)
    col_far[...] = jnp.stack(far, axis=1).reshape(-1, lanes).astype(BF)


def corner_kernel(col_near, col_far, near, far):
    size = near.shape[0] // 2
    last = col_near.shape[0] - size
    odd = is_odd("ha")
    for target, start in (
        (near, jnp.where(odd, 0, last)),
        (far, jnp.where(odd, last, 0)),
    ):
        at = pl.ds(pl.multiple_of(start, 16), size)
        target[:size] = col_near[at]
        target[size:] = col_far[at]


def ready_kernel(
    w_one, w_two, sc_one, sh_one, sc_two, sh_two, ahead_one, ahead_two, back_one, back_two, affine
):
    lanes = affine.shape[-1]
    for weight, ahead, back in ((w_one, ahead_one, back_one), (w_two, ahead_two, back_two)):
        for a in range(3):
            for b in range(3):
                for c in range(3):
                    at = (a * 3 + b) * lanes
                    ahead[at : at + lanes, c * lanes : (c + 1) * lanes] = weight[a, b, c]
        for b in range(3):
            for c in range(3):
                back[c * lanes : (c + 1) * lanes, b * lanes : (b + 1) * lanes] = weight[2, b, c]
    affine[...] = jnp.concatenate(
        [1.0 + sc_one[...], sh_one[...], 1.0 + sc_two[...], sh_two[...]] * 2, axis=0
    )


def own_kernel(
    rows, cols, cache_in, frames_in, cache_mid, ahead_one, ahead_two, part_one, part_two, field
):
    block = [cache_in[0], cache_in[1], frames_in[0], cache_mid[0], cache_mid[1]]
    none = jnp.zeros((rows, 2 * RIM, block[0].shape[-1]), F32)
    for i, value in enumerate(block):
        field[i] = jnp.concatenate([value.astype(F32), none], axis=1).astype(BF)
    own = [Rows((RIM, Frame(field, i), rows)) for i in range(5)]
    split = 6 * none.shape[-1]
    for frames, weight, part, first in (
        (own[:3], ahead_one[...], part_one, RIM + 1),
        (own[3:], ahead_two[:split], part_two, RIM + 2),
    ):
        for start, count in cut(first, 2 * RIM + rows - first, 2):
            part[start - first : start - first + count] = forward(frames, weight, [(start, count)])


def middle_kernel(
    rows, cols, cache_in, frames_in, cache_mid, cot, col_near, col_far, part_one, part_two,
    ahead_one, ahead_two, affine, field, slope_mid, a_mid, d_mid, moved_mid,
):
    block = [cache_in[0], cache_in[1], frames_in[0], cache_mid[0], cache_mid[1], cot[0]]
    frames, rims = join(block, col_near[...], col_far[...])
    for frame, value in enumerate(frames):
        field[frame] = value
    split = 6 * affine.shape[-1]
    first = RIM + 1
    for start, count in cut(first, RIM + rows - 1, 2):
        at = slice(start - first, start - first + count)
        conv = part_one[at] + rim_forward(rims[:3], ahead_one[...], start, count, cols)
        a_mid[at], slope_mid[at] = first_layer(rows, cols, conv, affine, [(start, count)])
    a_one, cotangent = Rows((first, a_mid, rows - 2)), Rows((RIM, Frame(field, 5), rows))
    second = RIM + 2
    for start, count in cut(second, RIM + rows - 2, 2):
        at = slice(start - second, start - second + count)
        conv = (
            part_two[at]
            + forward([a_one], ahead_two[split:], [(start, count)])
            + rim_forward(rims[3:5], ahead_two[:split], start, count, cols)
        )
        value = second_layer(conv, cotangent, affine, [(start, count)])
        d_mid[at] = value.astype(BF)
        moved_mid[at] = spread(cols, value)


def rim_kernel(
    rows, cols, field, slope_mid, a_mid, d_mid, moved_mid, row_near, row_far, corner_near, corner_far,
    ahead_one, ahead_two, back_two, affine, keep, send, d_one,
    top, bottom, slope_rim, a_rim, d_rim, moved_rim, moved_one, grads, sems,
):
    lanes = affine.shape[-1]
    tall = rows + 2 * RIM
    core = lax.axis_index("ha") % 2
    half = corner_near.shape[0] // 2

    def assemble(target, block, corner):
        parts, _ = join([block[i] for i in range(6)], corner[:half], corner[half:])
        for frame, value in enumerate(parts):
            target[frame] = value

    @pl.when(is_odd("ha"))
    def _():
        assemble(top, row_near, corner_near)
        assemble(bottom, row_far, corner_far)

    @pl.when(jnp.logical_not(is_odd("ha")))
    def _():
        assemble(top, row_far, corner_far)
        assemble(bottom, row_near, corner_near)

    whole = [
        Rows(
            (0, Frame(top, i), RIM),
            (RIM, Frame(field, i), rows),
            (RIM + rows, Frame(bottom, i), RIM),
        )
        for i in range(6)
    ]

    def around(rim, mid, first, count):
        size = mid.shape[0]
        return Rows(
            (first, rim, count),
            (first + count, mid, size),
            (first + count + size, Shifted(rim, count), count),
        )

    used = 27 * lanes
    if grads.shape[1] > used:
        grads[:, used:, :] = jnp.zeros((2, grads.shape[1] - used, lanes), BF)
    edge = jnp.zeros((2,) + moved_rim.shape[1:], BF)
    moved_rim[0:2] = edge
    moved_rim[6:8] = edge
    moved_one[0:2] = edge
    moved_one[rows + 2 : rows + 4] = edge

    def gradient(which, frames, moved):
        lhs = jnp.concatenate([flat(frames[a].get(RIM - 1, rows + 2)) for a in range(3)], axis=1)
        for b in range(3):
            rhs = flat(moved.get(RIM - b, rows + 2))
            out = lax.dot_general(lhs, rhs, (((0,), (0,)), ((), ())), preferred_element_type=F32)
            for a in range(3):
                for c in range(3):
                    at = ((a * 3 + b) * 3 + c) * lanes
                    grads[which, at : at + lanes, :] = out[
                        a * lanes : (a + 1) * lanes, c * lanes : (c + 1) * lanes
                    ].astype(BF)

        @pl.when(core == which)
        def _():
            pltpu.make_async_copy(grads.at[which], keep, sems.at[0]).start()

        @pl.when(core != which)
        def _():
            pltpu.make_async_copy(grads.at[which], send, sems.at[1]).start()

    blocks = [(1, 4), (tall - 5, 4)]
    conv = forward(whole[:3], ahead_one[...], blocks)
    a_value, slope_value = first_layer(rows, cols, conv, affine, blocks)
    a_rim[...] = a_value
    slope_rim[...] = slope_value
    a_all = around(a_rim, a_mid, 1, 4)
    slope_all = around(slope_rim, slope_mid, 1, 4)

    frames = whole[3:5] + [a_all]
    blocks = [(2, 4), (tall - 6, 4)]
    value = second_layer(forward(frames, ahead_two[...], blocks), whole[5], affine, blocks)
    d_rim[...] = value.astype(BF)
    moved_rim[2:6] = spread(cols, value[2:6])
    d_all = around(d_rim, d_mid, 2, 4)
    gradient(1, frames, around(moved_rim, moved_mid, 2, 4))

    for start, count in cut(3, tall - 3, 2):
        value = backward(d_all, back_two, start, count) * slope_all.get(start, count)
        d_one[start - 3 : start - 3 + count] = value.astype(BF)
        low, high = max(start, RIM), min(start + count, RIM + rows)
        moved_one[low - 2 : high - 2] = spread(cols, value[low - start : high - start])
    gradient(0, whole[:3], Rows((2, moved_one, rows + 4)))

    pltpu.make_async_copy(grads.at[core], keep, sems.at[0]).wait()
    pltpu.make_async_copy(grads.at[1 - core], send, sems.at[1]).wait()


class Shifted:
    def __init__(self, ref, by):
        self.ref, self.by = ref, by

    def __getitem__(self, key):
        return self.ref[key.start + self.by : key.stop + self.by]


def input_kernel(rows, cols, d_one, back_one, gin):
    field = Rows((RIM - 1, d_one, rows + 2))
    for start, count in cut(RIM, RIM + rows, 2):
        value = backward(field, back_one, start, count)
        gin[0, start - RIM : start - RIM + count] = value[:, :cols].astype(BF)


def place_kernel(parts, first, source, *refs):
    one, other, wide, sems = refs[-4:]
    size = wide.shape[0] // parts
    own_first = jnp.logical_not(is_odd("ha"))
    to_one = own_first if first else jnp.logical_not(own_first)
    for part in range(parts):
        at = pl.ds(part * size, size)
        wide[at, :] = source[at, :].astype(F32)

        @pl.when(to_one)
        def _():
            pltpu.make_async_copy(wide.at[at], one.at[at], sems.at[part]).start()

        @pl.when(jnp.logical_not(to_one))
        def _():
            pltpu.make_async_copy(wide.at[at], other.at[at], sems.at[part]).start()

    for part in range(parts):
        at = pl.ds(part * size, size)
        pltpu.make_async_copy(wide.at[at], one.at[at], sems.at[part]).wait()


def per_device(
    frames_in, cache_in, cache_mid, w_first, w_second,
    scale_first, shift_first, scale_second, shift_second, cotangent,
):
    _, rows, cols, chans = frames_in.shape
    devices = lax.axis_size("ha") * lax.axis_size("wa")
    factor = 1.0 / (rows * cols * devices) ** 0.5
    full, tall = cols + 2 * RIM, rows + 2 * RIM
    FULL[0] = full
    chips = devices // 2
    total = 27 * chans
    share = -(-total // (8 * chips)) * 8
    inner = pl.BlockSpec(memory_space=pltpu.VMEM)
    anywhere = pl.BlockSpec(memory_space=pl.ANY)

    def shaped(*shape, dtype=BF):
        return jax.ShapeDtypeStruct(shape, dtype)

    def call(kernel, name, out_shape, mebibytes, flops, args, sizes=True, **kwargs):
        def body(*refs):
            kernel(rows, cols, *refs) if sizes else kernel(*refs)

        count = len(out_shape)
        kwargs.setdefault("in_specs", [inner] * len(args))
        kwargs.setdefault("out_specs", (inner,) * count)
        return pl.pallas_call(
            body,
            out_shape=tuple(out_shape),
            cost_estimate=pl.CostEstimate(
                flops=int(flops), bytes_accessed=8 * 10**6, transcendentals=0
            ),
            compiler_params=pltpu.CompilerParams(vmem_limit_bytes=mebibytes * 2**20),
            name=name,
            **kwargs,
        )(*args)

    fields = (cache_in, frames_in, cache_mid, cotangent)
    rim_rows, rim_cols = shaped(6, RIM, cols, chans), shaped(6 * rows * RIM, chans)
    row_near, row_far, col_near, col_far = call(
        pack_kernel, "pack", (rim_rows, rim_rows, rim_cols, rim_cols), 53, 1e9, fields,
        in_specs=[anywhere] * 4,
        scratch_shapes=[pltpu.VMEM(v.shape, BF) for v in fields] + [pltpu.SemaphoreType.DMA((4,))],
    )
    ahead, back = shaped(9 * chans, 3 * chans), shaped(3 * chans, 3 * chans)
    ahead_one, ahead_two, back_one, back_two, affine = call(
        ready_kernel, "ready", (ahead, ahead, back, back, shaped(8, chans, dtype=F32)), 10, 2e9,
        (w_first, w_second, scale_first, shift_first, scale_second, shift_second), sizes=False,
    )
    part_one, part_two = call(
        own_kernel, "own",
        (
            shaped(rows - 2, full, chans, dtype=F32),
            shaped(rows - 4, full, chans, dtype=F32),
        ),
        12, 4e9, (cache_in, frames_in, cache_mid, ahead_one, ahead_two),
        scratch_shapes=[pltpu.VMEM((5, rows, full, chans), BF)],
    )
    col_near, col_far = trade("wa", col_near, col_far)
    row_near, row_far = trade("ha", row_near, row_far)
    size = 6 * RIM * RIM
    corner_near, corner_far = trade(
        "ha",
        *call(
            corner_kernel, "corner", [shaped(2 * size, chans)] * 2, 4, 1e8, (col_near, col_far),
            sizes=False,
        ),
    )

    field, slope_mid, a_mid, d_mid, moved_mid = call(
        middle_kernel, "middle",
        (
            shaped(6, rows, full, chans),
            shaped(rows - 2, full, chans, dtype=F32),
            shaped(rows - 2, full, chans),
            shaped(rows - 4, full, chans),
            shaped(rows - 4, full, 3 * chans),
        ),
        16, 3e9, (*fields, col_near, col_far, part_one, part_two, ahead_one, ahead_two, affine),
    )
    keep, send, d_one = call(
        rim_kernel, "rim",
        (shaped(share * chips, chans), shaped(share * chips, chans), shaped(rows + 2, full, chans)),
        20, 5e9,
        (
            field, slope_mid, a_mid, d_mid, moved_mid, row_near, row_far, corner_near, corner_far,
            ahead_one, ahead_two, back_two, affine,
        ),
        out_specs=(anywhere, anywhere, inner),
        scratch_shapes=[
            pltpu.VMEM((6, RIM, full, chans), BF),
            pltpu.VMEM((6, RIM, full, chans), BF),
            pltpu.VMEM((8, full, chans), F32),
            pltpu.VMEM((8, full, chans), BF),
            pltpu.VMEM((8, full, chans), BF),
            pltpu.VMEM((8, full, 3 * chans), BF),
            pltpu.VMEM((rows + 4, full, 3 * chans), BF),
            pltpu.VMEM((2, share * chips, chans), BF),
            pltpu.SemaphoreType.DMA((2,)),
        ],
    )

    pairs, _ = swaps("ha")
    got = lax.ppermute(send, "ha", pairs)
    (grad_input,) = call(
        input_kernel, "input", (shaped(1, rows, cols, chans),), 8, 1e9, (d_one, back_one)
    )
    got, grad_input = lax.optimization_barrier((got, grad_input))
    chip_sum = (keep.astype(F32) + got.astype(F32)).astype(BF)
    cores = [[c for c in range(devices) if (c // lax.axis_size("wa")) % 2 == k] for k in range(2)]

    def spread_out(value):
        return lax.all_to_all(
            value.reshape(chips, share, chans), BOTH, 0, 0, axis_index_groups=cores, tiled=True
        )

    mine = (jnp.sum(spread_out(chip_sum).astype(F32), axis=0) * factor).astype(BF)
    one = spread_out(jnp.broadcast_to(mine[None], (chips, share, chans))).reshape(-1, chans)
    other = lax.ppermute(one, "ha", pairs)
    shape = (3, 3, 3, chans, chans)
    parts = 4

    def place(source, *given):
        return call(
            lambda *refs: place_kernel(parts, not given, *refs), "place",
            [shaped(total, chans, dtype=F32)] * 2, 6, 2e9, (source, *given), sizes=False,
            in_specs=[inner] + [anywhere] * len(given),
            out_specs=(anywhere, anywhere),
            scratch_shapes=[
                pltpu.VMEM((total, chans), F32), pltpu.SemaphoreType.DMA((parts,))
            ],
            input_output_aliases={1: 0, 2: 1} if given else {},
        )

    grad_first, grad_second = place(other, *place(one))
    return (grad_input, grad_first.reshape(shape), grad_second.reshape(shape))


def solution(mesh):
    tiled = P(None, "ha", "wa", None)
    return jax.shard_map(
        per_device,
        mesh=mesh,
        in_specs=(tiled, tiled, tiled, P(), P(), P(), P(), P(), P(), tiled),
        out_specs=(tiled, P(), P()),
        check_vma=False,
    )
```

```python
import jax
import jax.numpy as jnp
from jax import lax
from jax.experimental import pallas as pl
from jax.experimental.pallas import tpu as pltpu
from jax.sharding import PartitionSpec as P

BF = jnp.bfloat16
F32 = jnp.float32
RIM = 4
BOTH = ("ha", "wa")


def swaps(axis):
    count = lax.axis_size(axis)
    first = [(i, i ^ 1) for i in range(count)]
    second = [(i, i + 1 if i % 2 else i - 1) for i in range(1, count - 1)]
    return first, second


def trade(axis, near, far):
    first, second = swaps(axis)
    far = lax.ppermute(far, axis, second)
    return lax.ppermute(near, axis, first), far


def is_odd(axis):
    return lax.axis_index(axis) % 2 == 1


def slope(value):
    sig = jax.nn.sigmoid(value)
    return sig * (1.0 + value * (1.0 - sig))


def flat(value):
    return value.reshape(-1, value.shape[-1])


def turn(value, step):
    return pltpu.roll(value, step % value.shape[1], 1)


def join(block, near, far):
    high, _, lanes = block[0].shape
    odd = is_odd("wa")
    near, far = near.astype(F32), far.astype(F32)
    left = jnp.where(odd, near, far).reshape(high, 3, 2 * RIM, lanes)
    right = jnp.where(odd, far, near).reshape(high, 3, 2 * RIM, lanes)
    lower = lax.broadcasted_iota(jnp.int32, (high, 2 * RIM, lanes), 1) < RIM
    frames, rims = [], []
    for frame in range(6):
        one, other = right[:, frame // 2], left[:, frame // 2]
        if frame % 2 == 0:
            rim = jnp.where(lower, one, pltpu.roll(other, RIM, 1))
        else:
            rim = jnp.where(lower, pltpu.roll(one, RIM, 1), other)
        frames.append(jnp.concatenate([block[frame].astype(F32), rim], axis=1).astype(BF))
        rims.append(rim)
    return frames, rims


class Rows:
    def __init__(self, *pieces):
        self.pieces = pieces

    def get(self, start, count):
        out = []
        for first, ref, size in self.pieces:
            low, high = max(start, first), min(start + count, first + size)
            if low < high:
                out.append(ref[low - first : high - first])
        return out[0] if len(out) == 1 else jnp.concatenate(out, axis=0)


class Frame:
    def __init__(self, ref, index):
        self.ref, self.index = ref, index

    def __getitem__(self, key):
        return self.ref[self.index, key]


def forward(frames, weight, blocks):
    lhs = jnp.concatenate(
        [
            jnp.concatenate(
                [flat(frames[a].get(start - 1 + b, count)) for start, count in blocks], axis=0
            )
            for a in range(len(frames))
            for b in range(3)
        ],
        axis=1,
    )
    out = jnp.dot(lhs, weight, preferred_element_type=F32)
    return gather_columns(out, 1)


def rim_forward(rims, weight, start, count, cols):
    lhs = jnp.concatenate(
        [
            flat(rim[start - 1 + b - RIM : start - 1 + b - RIM + count])
            for rim in rims
            for b in range(3)
        ],
        axis=1,
    ).astype(BF)
    out = jnp.dot(lhs, weight, preferred_element_type=F32)
    lanes = out.shape[-1] // 3
    out = out.reshape(count, 2 * RIM, 3 * lanes)
    place = lax.broadcasted_iota(jnp.int32, (count, 2 * RIM, lanes), 1)
    last = 2 * RIM - 1
    from_left, from_right = turn(out[..., :lanes], 1), turn(out[..., 2 * lanes :], -1)
    here = (
        out[..., lanes : 2 * lanes]
        + jnp.where(place > 0, from_left, 0.0)
        + jnp.where(place < last, from_right, 0.0)
    )
    return jnp.concatenate(
        [
            jnp.where(place == 0, from_left, 0.0),
            jnp.zeros((count, cols - 4 * RIM, lanes), F32),
            jnp.where(place == last, from_right, 0.0),
            here,
        ],
        axis=1,
    )


def backward(field, weight, start, count):
    lhs = jnp.concatenate([flat(field.get(start + 1 - b, count)) for b in range(3)], axis=1)
    out = lax.dot_general(lhs, weight[...], (((1,), (1,)), ((), ())), preferred_element_type=F32)
    return gather_columns(out, -1)


def gather_columns(out, step):
    lanes = out.shape[-1] // 3
    out = out.reshape(-1, FULL[0], 3 * lanes)
    return (
        turn(out[..., :lanes], step)
        + out[..., lanes : 2 * lanes]
        + turn(out[..., 2 * lanes :], -step)
    )


FULL = [0]


def in_image(rows, cols, lanes, blocks):
    full = cols + 2 * RIM
    image_rows, image_cols = rows * lax.axis_size("ha"), cols * lax.axis_size("wa")
    col = lax.broadcasted_iota(jnp.int32, (1, full, lanes), 1)
    place = jnp.where(col < cols + RIM, col, col - full) + lax.axis_index("wa") * cols
    col_in = (place >= 0) & (place < image_cols)
    out = []
    for start, count in blocks:
        row = lax.broadcasted_iota(jnp.int32, (count, full, lanes), 0)
        row = row + (start - RIM) + lax.axis_index("ha") * rows
        out.append((row >= 0) & (row < image_rows) & col_in)
    return jnp.concatenate(out, axis=0) if len(out) > 1 else out[0]


def first_layer(rows, cols, conv, affine, blocks):
    lanes = affine.shape[-1]
    gain, bias = (affine[i : i + 1, :].reshape(1, 1, lanes) for i in (0, 1))
    m_one = conv * gain + bias
    sig = jax.nn.sigmoid(m_one)
    inside = in_image(rows, cols, lanes, blocks)
    a_one = jnp.where(inside, m_one * sig, 0.0).astype(BF)
    slope_one = jnp.where(inside, sig * (1.0 + m_one * (1.0 - sig)) * gain, 0.0)
    return a_one, slope_one


def second_layer(conv, cot, affine, blocks):
    lanes = affine.shape[-1]
    gain, bias = (affine[i : i + 1, :].reshape(1, 1, lanes) for i in (2, 3))
    m_two = conv * gain + bias
    pulled = [cot.get(start, count) for start, count in blocks]
    pulled = jnp.concatenate(pulled, axis=0) if len(pulled) > 1 else pulled[0]
    return pulled.astype(F32) * slope(m_two) * gain


def spread(cols, value):
    own = lax.broadcasted_iota(jnp.int32, (1,) + value.shape[1:], 1) < cols
    kept = jnp.where(own, value, 0.0)
    return jnp.concatenate([turn(kept, -1), kept, turn(kept, 1)], axis=2).astype(BF)


def cut(start, stop, parts):
    step = -(-(stop - start) // parts)
    return [(at, min(step, stop - at)) for at in range(start, stop, step)]


def pack_kernel(
    rows, cols, cache_in_at, frames_in_at, cache_mid_at, cot_at, row_near, row_far, col_near, col_far,
    cache_in, frames_in, cache_mid, cot, sems,
):
    copies = [
        pltpu.make_async_copy(source, target, sems.at[i])
        for i, (source, target) in enumerate(
            (
                (cache_in_at, cache_in),
                (frames_in_at, frames_in),
                (cache_mid_at, cache_mid),
                (cot_at, cot),
            )
        )
    ]
    odd_row, odd_col = is_odd("ha"), is_odd("wa")
    for copy in copies:
        copy.start()
    for copy in copies:
        copy.wait()
    sources = (
        (cache_in, 0), (cache_in, 1), (frames_in, 0), (cache_mid, 0), (cache_mid, 1), (cot, 0)
    )
    last = rows - RIM
    near_at, far_at = jnp.where(odd_row, 0, last), jnp.where(odd_row, last, 0)
    for frame, (ref, i) in enumerate(sources):
        row_near[frame] = ref[i, pl.ds(near_at, RIM)]
        row_far[frame] = ref[i, pl.ds(far_at, RIM)]
    lanes = col_near.shape[-1]
    lower = lax.broadcasted_iota(jnp.int32, (rows, 2 * RIM, lanes), 1) < RIM

    def edges(frame):
        ref, i = sources[frame]
        value = ref[i].astype(F32)
        return value[:, : 2 * RIM], pltpu.roll(value[:, cols - 2 * RIM :], RIM, 1)

    near, far = [], []
    for pair in range(3):
        (head, tail), (head_b, tail_b) = edges(2 * pair), edges(2 * pair + 1)
        heads = jnp.where(lower, head, pltpu.roll(head_b, RIM, 1))
        tails = jnp.where(lower, tail, pltpu.roll(tail_b, RIM, 1))
        near.append(jnp.where(odd_col, heads, tails))
        far.append(jnp.where(odd_col, tails, heads))
    col_near[...] = jnp.stack(near, axis=1).reshape(-1, lanes).astype(BF)
    col_far[...] = jnp.stack(far, axis=1).reshape(-1, lanes).astype(BF)


def corner_kernel(col_near, col_far, near, far):
    size = near.shape[0] // 2
    last = col_near.shape[0] - size
    odd = is_odd("ha")
    for target, start in (
        (near, jnp.where(odd, 0, last)),
        (far, jnp.where(odd, last, 0)),
    ):
        at = pl.ds(pl.multiple_of(start, 16), size)
        target[:size] = col_near[at]
        target[size:] = col_far[at]


def ready_kernel(
    w_one, w_two, sc_one, sh_one, sc_two, sh_two, ahead_one, ahead_two, back_one, back_two, affine
):
    lanes = affine.shape[-1]
    for weight, ahead, back in ((w_one, ahead_one, back_one), (w_two, ahead_two, back_two)):
        for a in range(3):
            for b in range(3):
                for c in range(3):
                    at = (a * 3 + b) * lanes
                    ahead[at : at + lanes, c * lanes : (c + 1) * lanes] = weight[a, b, c]
        for b in range(3):
            for c in range(3):
                back[c * lanes : (c + 1) * lanes, b * lanes : (b + 1) * lanes] = weight[2, b, c]
    affine[...] = jnp.concatenate(
        [1.0 + sc_one[...], sh_one[...], 1.0 + sc_two[...], sh_two[...]] * 2, axis=0
    )


def own_kernel(
    rows, cols, cache_in, frames_in, cache_mid, ahead_one, ahead_two, part_one, part_two, field
):
    block = [cache_in[0], cache_in[1], frames_in[0], cache_mid[0], cache_mid[1]]
    none = jnp.zeros((rows, 2 * RIM, block[0].shape[-1]), F32)
    for i, value in enumerate(block):
        field[i] = jnp.concatenate([value.astype(F32), none], axis=1).astype(BF)
    own = [Rows((RIM, Frame(field, i), rows)) for i in range(5)]
    split = 6 * none.shape[-1]
    for frames, weight, part, first in (
        (own[:3], ahead_one[...], part_one, RIM + 1),
        (own[3:], ahead_two[:split], part_two, RIM + 2),
    ):
        for start, count in cut(first, 2 * RIM + rows - first, 2):
            part[start - first : start - first + count] = forward(frames, weight, [(start, count)])


def middle_kernel(
    rows, cols, cache_in, frames_in, cache_mid, cot, col_near, col_far, part_one, part_two,
    ahead_one, ahead_two, affine, field, slope_mid, a_mid, d_mid, moved_mid,
):
    block = [cache_in[0], cache_in[1], frames_in[0], cache_mid[0], cache_mid[1], cot[0]]
    frames, rims = join(block, col_near[...], col_far[...])
    for frame, value in enumerate(frames):
        field[frame] = value
    split = 6 * affine.shape[-1]
    first = RIM + 1
    for start, count in cut(first, RIM + rows - 1, 2):
        at = slice(start - first, start - first + count)
        conv = part_one[at] + rim_forward(rims[:3], ahead_one[...], start, count, cols)
        a_mid[at], slope_mid[at] = first_layer(rows, cols, conv, affine, [(start, count)])
    a_one, cotangent = Rows((first, a_mid, rows - 2)), Rows((RIM, Frame(field, 5), rows))
    second = RIM + 2
    for start, count in cut(second, RIM + rows - 2, 2):
        at = slice(start - second, start - second + count)
        conv = (
            part_two[at]
            + forward([a_one], ahead_two[split:], [(start, count)])
            + rim_forward(rims[3:5], ahead_two[:split], start, count, cols)
        )
        value = second_layer(conv, cotangent, affine, [(start, count)])
        d_mid[at] = value.astype(BF)
        moved_mid[at] = spread(cols, value)


def rim_kernel(
    rows, cols, field, slope_mid, a_mid, d_mid, moved_mid, row_near, row_far, corner_near, corner_far,
    ahead_one, ahead_two, back_two, affine, keep, send, d_one,
    top, bottom, slope_rim, a_rim, d_rim, moved_rim, moved_one, grads, sems,
):
    lanes = affine.shape[-1]
    tall = rows + 2 * RIM
    core = lax.axis_index("ha") % 2
    half = corner_near.shape[0] // 2

    def assemble(target, block, corner):
        parts, _ = join([block[i] for i in range(6)], corner[:half], corner[half:])
        for frame, value in enumerate(parts):
            target[frame] = value

    @pl.when(is_odd("ha"))
    def _():
        assemble(top, row_near, corner_near)
        assemble(bottom, row_far, corner_far)

    @pl.when(jnp.logical_not(is_odd("ha")))
    def _():
        assemble(top, row_far, corner_far)
        assemble(bottom, row_near, corner_near)

    whole = [
        Rows(
            (0, Frame(top, i), RIM),
            (RIM, Frame(field, i), rows),
            (RIM + rows, Frame(bottom, i), RIM),
        )
        for i in range(6)
    ]

    def around(rim, mid, first, count):
        size = mid.shape[0]
        return Rows(
            (first, rim, count),
            (first + count, mid, size),
            (first + count + size, Shifted(rim, count), count),
        )

    used = 27 * lanes
    if grads.shape[1] > used:
        grads[:, used:, :] = jnp.zeros((2, grads.shape[1] - used, lanes), BF)
    edge = jnp.zeros((2,) + moved_rim.shape[1:], BF)
    moved_rim[0:2] = edge
    moved_rim[6:8] = edge
    moved_one[0:2] = edge
    moved_one[rows + 2 : rows + 4] = edge

    def gradient(which, frames, moved):
        lhs = jnp.concatenate([flat(frames[a].get(RIM - 1, rows + 2)) for a in range(3)], axis=1)
        for b in range(3):
            rhs = flat(moved.get(RIM - b, rows + 2))
            out = lax.dot_general(lhs, rhs, (((0,), (0,)), ((), ())), preferred_element_type=F32)
            for a in range(3):
                for c in range(3):
                    at = ((a * 3 + b) * 3 + c) * lanes
                    grads[which, at : at + lanes, :] = out[
                        a * lanes : (a + 1) * lanes, c * lanes : (c + 1) * lanes
                    ].astype(BF)

        @pl.when(core == which)
        def _():
            pltpu.make_async_copy(grads.at[which], keep, sems.at[0]).start()

        @pl.when(core != which)
        def _():
            pltpu.make_async_copy(grads.at[which], send, sems.at[1]).start()

    blocks = [(1, 4), (tall - 5, 4)]
    conv = forward(whole[:3], ahead_one[...], blocks)
    a_value, slope_value = first_layer(rows, cols, conv, affine, blocks)
    a_rim[...] = a_value
    slope_rim[...] = slope_value
    a_all = around(a_rim, a_mid, 1, 4)
    slope_all = around(slope_rim, slope_mid, 1, 4)

    frames = whole[3:5] + [a_all]
    blocks = [(2, 4), (tall - 6, 4)]
    value = second_layer(forward(frames, ahead_two[...], blocks), whole[5], affine, blocks)
    d_rim[...] = value.astype(BF)
    moved_rim[2:6] = spread(cols, value[2:6])
    d_all = around(d_rim, d_mid, 2, 4)
    gradient(1, frames, around(moved_rim, moved_mid, 2, 4))

    for start, count in cut(3, tall - 3, 2):
        value = backward(d_all, back_two, start, count) * slope_all.get(start, count)
        d_one[start - 3 : start - 3 + count] = value.astype(BF)
        low, high = max(start, RIM), min(start + count, RIM + rows)
        moved_one[low - 2 : high - 2] = spread(cols, value[low - start : high - start])
    gradient(0, whole[:3], Rows((2, moved_one, rows + 4)))

    pltpu.make_async_copy(grads.at[core], keep, sems.at[0]).wait()
    pltpu.make_async_copy(grads.at[1 - core], send, sems.at[1]).wait()


class Shifted:
    def __init__(self, ref, by):
        self.ref, self.by = ref, by

    def __getitem__(self, key):
        return self.ref[key.start + self.by : key.stop + self.by]


def input_kernel(rows, cols, d_one, back_one, gin):
    field = Rows((RIM - 1, d_one, rows + 2))
    for start, count in cut(RIM, RIM + rows, 2):
        value = backward(field, back_one, start, count)
        gin[0, start - RIM : start - RIM + count] = value[:, :cols].astype(BF)


def place_kernel(parts, first, source, *refs):
    one, other, wide, sems = refs[-4:]
    size = wide.shape[0] // parts
    own_first = jnp.logical_not(is_odd("ha"))
    to_one = own_first if first else jnp.logical_not(own_first)
    for part in range(parts):
        at = pl.ds(part * size, size)
        wide[at, :] = source[at, :].astype(F32)

        @pl.when(to_one)
        def _():
            pltpu.make_async_copy(wide.at[at], one.at[at], sems.at[part]).start()

        @pl.when(jnp.logical_not(to_one))
        def _():
            pltpu.make_async_copy(wide.at[at], other.at[at], sems.at[part]).start()

    for part in range(parts):
        at = pl.ds(part * size, size)
        pltpu.make_async_copy(wide.at[at], one.at[at], sems.at[part]).wait()


def per_device(
    frames_in, cache_in, cache_mid, w_first, w_second,
    scale_first, shift_first, scale_second, shift_second, cotangent,
):
    _, rows, cols, chans = frames_in.shape
    devices = lax.axis_size("ha") * lax.axis_size("wa")
    factor = 1.0 / (rows * cols * devices) ** 0.5
    full, tall = cols + 2 * RIM, rows + 2 * RIM
    FULL[0] = full
    chips = devices // 2
    total = 27 * chans
    share = -(-total // (8 * chips)) * 8
    inner = pl.BlockSpec(memory_space=pltpu.VMEM)
    anywhere = pl.BlockSpec(memory_space=pl.ANY)

    def shaped(*shape, dtype=BF):
        return jax.ShapeDtypeStruct(shape, dtype)

    def call(kernel, name, out_shape, mebibytes, flops, args, sizes=True, **kwargs):
        def body(*refs):
            kernel(rows, cols, *refs) if sizes else kernel(*refs)

        count = len(out_shape)
        kwargs.setdefault("in_specs", [inner] * len(args))
        kwargs.setdefault("out_specs", (inner,) * count)
        return pl.pallas_call(
            body,
            out_shape=tuple(out_shape),
            cost_estimate=pl.CostEstimate(
                flops=int(flops), bytes_accessed=8 * 10**6, transcendentals=0
            ),
            compiler_params=pltpu.CompilerParams(vmem_limit_bytes=mebibytes * 2**20),
            name=name,
            **kwargs,
        )(*args)

    fields = (cache_in, frames_in, cache_mid, cotangent)
    rim_rows, rim_cols = shaped(6, RIM, cols, chans), shaped(6 * rows * RIM, chans)
    row_near, row_far, col_near, col_far = call(
        pack_kernel, "pack", (rim_rows, rim_rows, rim_cols, rim_cols), 53, 1e9, fields,
        in_specs=[anywhere] * 4,
        scratch_shapes=[pltpu.VMEM(v.shape, BF) for v in fields] + [pltpu.SemaphoreType.DMA((4,))],
    )
    ahead, back = shaped(9 * chans, 3 * chans), shaped(3 * chans, 3 * chans)
    ahead_one, ahead_two, back_one, back_two, affine = call(
        ready_kernel, "ready", (ahead, ahead, back, back, shaped(8, chans, dtype=F32)), 10, 2e9,
        (w_first, w_second, scale_first, shift_first, scale_second, shift_second), sizes=False,
    )
    part_one, part_two = call(
        own_kernel, "own",
        (
            shaped(rows - 2, full, chans, dtype=F32),
            shaped(rows - 4, full, chans, dtype=F32),
        ),
        12, 4e9, (cache_in, frames_in, cache_mid, ahead_one, ahead_two),
        scratch_shapes=[pltpu.VMEM((5, rows, full, chans), BF)],
    )
    col_near, col_far = trade("wa", col_near, col_far)
    row_near, row_far = trade("ha", row_near, row_far)
    size = 6 * RIM * RIM
    corner_near, corner_far = trade(
        "ha",
        *call(
            corner_kernel, "corner", [shaped(2 * size, chans)] * 2, 4, 1e8, (col_near, col_far),
            sizes=False,
        ),
    )

    field, slope_mid, a_mid, d_mid, moved_mid = call(
        middle_kernel, "middle",
        (
            shaped(6, rows, full, chans),
            shaped(rows - 2, full, chans, dtype=F32),
            shaped(rows - 2, full, chans),
            shaped(rows - 4, full, chans),
            shaped(rows - 4, full, 3 * chans),
        ),
        16, 3e9, (*fields, col_near, col_far, part_one, part_two, ahead_one, ahead_two, affine),
    )
    keep, send, d_one = call(
        rim_kernel, "rim",
        (shaped(share * chips, chans), shaped(share * chips, chans), shaped(rows + 2, full, chans)),
        20, 5e9,
        (
            field, slope_mid, a_mid, d_mid, moved_mid, row_near, row_far, corner_near, corner_far,
            ahead_one, ahead_two, back_two, affine,
        ),
        out_specs=(anywhere, anywhere, inner),
        scratch_shapes=[
            pltpu.VMEM((6, RIM, full, chans), BF),
            pltpu.VMEM((6, RIM, full, chans), BF),
            pltpu.VMEM((8, full, chans), F32),
            pltpu.VMEM((8, full, chans), BF),
            pltpu.VMEM((8, full, chans), BF),
            pltpu.VMEM((8, full, 3 * chans), BF),
            pltpu.VMEM((rows + 4, full, 3 * chans), BF),
            pltpu.VMEM((2, share * chips, chans), BF),
            pltpu.SemaphoreType.DMA((2,)),
        ],
    )

    pairs, _ = swaps("ha")
    got = lax.ppermute(send, "ha", pairs)
    (grad_input,) = call(
        input_kernel, "input", (shaped(1, rows, cols, chans),), 8, 1e9, (d_one, back_one)
    )
    got, grad_input = lax.optimization_barrier((got, grad_input))
    chip_sum = (keep.astype(F32) + got.astype(F32)).astype(BF)
    cores = [[c for c in range(devices) if (c // lax.axis_size("wa")) % 2 == k] for k in range(2)]
    cores = [group[::-1] for group in cores]

    def spread_out(value):
        return lax.all_to_all(
            value.reshape(chips, share, chans), BOTH, 0, 0, axis_index_groups=cores, tiled=True
        )

    mine = (jnp.sum(spread_out(chip_sum).astype(F32), axis=0) * factor).astype(BF)
    one = spread_out(jnp.broadcast_to(mine[None], (chips, share, chans))).reshape(-1, chans)
    other = lax.ppermute(one, "ha", pairs)
    shape = (3, 3, 3, chans, chans)
    parts = 4

    def place(source, *given):
        return call(
            lambda *refs: place_kernel(parts, not given, *refs), "place",
            [shaped(total, chans, dtype=F32)] * 2, 6, 2e9, (source, *given), sizes=False,
            in_specs=[inner] + [anywhere] * len(given),
            out_specs=(anywhere, anywhere),
            scratch_shapes=[
                pltpu.VMEM((total, chans), F32), pltpu.SemaphoreType.DMA((parts,))
            ],
            input_output_aliases={1: 0, 2: 1} if given else {},
        )

    grad_first, grad_second = place(other, *place(one))
    return (grad_input, grad_first.reshape(shape), grad_second.reshape(shape))


def solution(mesh):
    tiled = P(None, "ha", "wa", None)
    return jax.shard_map(
        per_device,
        mesh=mesh,
        in_specs=(tiled, tiled, tiled, P(), P(), P(), P(), P(), P(), tiled),
        out_specs=(tiled, P(), P()),
        check_vma=False,
    )
```

```python
import jax
import jax.numpy as jnp
from jax import lax
from jax.experimental import pallas as pl
from jax.experimental.pallas import tpu as pltpu
from jax.sharding import PartitionSpec as P

BF = jnp.bfloat16
F32 = jnp.float32
RIM = 4
BOTH = ("ha", "wa")


def swaps(axis):
    count = lax.axis_size(axis)
    first = [(i, i ^ 1) for i in range(count)]
    second = [(i, i + 1 if i % 2 else i - 1) for i in range(1, count - 1)]
    return first, second


def trade(axis, near, far):
    first, second = swaps(axis)
    far = lax.ppermute(far, axis, second)
    return lax.ppermute(near, axis, first), far


def is_odd(axis):
    return lax.axis_index(axis) % 2 == 1


def slope(value):
    sig = jax.nn.sigmoid(value)
    return sig * (1.0 + value * (1.0 - sig))


def flat(value):
    return value.reshape(-1, value.shape[-1])


def turn(value, step):
    return pltpu.roll(value, step % value.shape[1], 1)


def join(block, near, far):
    high, _, lanes = block[0].shape
    odd = is_odd("wa")
    near, far = near.astype(F32), far.astype(F32)
    left = jnp.where(odd, near, far).reshape(high, 3, 2 * RIM, lanes)
    right = jnp.where(odd, far, near).reshape(high, 3, 2 * RIM, lanes)
    lower = lax.broadcasted_iota(jnp.int32, (high, 2 * RIM, lanes), 1) < RIM
    frames, rims = [], []
    for frame in range(6):
        one, other = right[:, frame // 2], left[:, frame // 2]
        if frame % 2 == 0:
            rim = jnp.where(lower, one, pltpu.roll(other, RIM, 1))
        else:
            rim = jnp.where(lower, pltpu.roll(one, RIM, 1), other)
        frames.append(jnp.concatenate([block[frame].astype(F32), rim], axis=1).astype(BF))
        rims.append(rim)
    return frames, rims


class Rows:
    def __init__(self, *pieces):
        self.pieces = pieces

    def get(self, start, count):
        out = []
        for first, ref, size in self.pieces:
            low, high = max(start, first), min(start + count, first + size)
            if low < high:
                out.append(ref[low - first : high - first])
        return out[0] if len(out) == 1 else jnp.concatenate(out, axis=0)


class Frame:
    def __init__(self, ref, index):
        self.ref, self.index = ref, index

    def __getitem__(self, key):
        return self.ref[self.index, key]


def forward(frames, weight, blocks):
    lhs = jnp.concatenate(
        [
            jnp.concatenate(
                [flat(frames[a].get(start - 1 + b, count)) for start, count in blocks], axis=0
            )
            for a in range(len(frames))
            for b in range(3)
        ],
        axis=1,
    )
    out = jnp.dot(lhs, weight, preferred_element_type=F32)
    return gather_columns(out, 1)


def rim_forward(rims, weight, start, count, cols):
    lhs = jnp.concatenate(
        [
            flat(rim[start - 1 + b - RIM : start - 1 + b - RIM + count])
            for rim in rims
            for b in range(3)
        ],
        axis=1,
    ).astype(BF)
    out = jnp.dot(lhs, weight, preferred_element_type=F32)
    lanes = out.shape[-1] // 3
    out = out.reshape(count, 2 * RIM, 3 * lanes)
    place = lax.broadcasted_iota(jnp.int32, (count, 2 * RIM, lanes), 1)
    last = 2 * RIM - 1
    from_left, from_right = turn(out[..., :lanes], 1), turn(out[..., 2 * lanes :], -1)
    here = (
        out[..., lanes : 2 * lanes]
        + jnp.where(place > 0, from_left, 0.0)
        + jnp.where(place < last, from_right, 0.0)
    )
    return jnp.concatenate(
        [
            jnp.where(place == 0, from_left, 0.0),
            jnp.zeros((count, cols - 4 * RIM, lanes), F32),
            jnp.where(place == last, from_right, 0.0),
            here,
        ],
        axis=1,
    )


def backward(field, weight, start, count):
    lhs = jnp.concatenate([flat(field.get(start + 1 - b, count)) for b in range(3)], axis=1)
    out = lax.dot_general(lhs, weight[...], (((1,), (1,)), ((), ())), preferred_element_type=F32)
    return gather_columns(out, -1)


def gather_columns(out, step):
    lanes = out.shape[-1] // 3
    out = out.reshape(-1, FULL[0], 3 * lanes)
    return (
        turn(out[..., :lanes], step)
        + out[..., lanes : 2 * lanes]
        + turn(out[..., 2 * lanes :], -step)
    )


FULL = [0]


def in_image(rows, cols, lanes, blocks):
    full = cols + 2 * RIM
    image_rows, image_cols = rows * lax.axis_size("ha"), cols * lax.axis_size("wa")
    col = lax.broadcasted_iota(jnp.int32, (1, full, lanes), 1)
    place = jnp.where(col < cols + RIM, col, col - full) + lax.axis_index("wa") * cols
    col_in = (place >= 0) & (place < image_cols)
    out = []
    for start, count in blocks:
        row = lax.broadcasted_iota(jnp.int32, (count, full, lanes), 0)
        row = row + (start - RIM) + lax.axis_index("ha") * rows
        out.append((row >= 0) & (row < image_rows) & col_in)
    return jnp.concatenate(out, axis=0) if len(out) > 1 else out[0]


def first_layer(rows, cols, conv, affine, blocks):
    lanes = affine.shape[-1]
    gain, bias = (affine[i : i + 1, :].reshape(1, 1, lanes) for i in (0, 1))
    m_one = conv * gain + bias
    sig = jax.nn.sigmoid(m_one)
    inside = in_image(rows, cols, lanes, blocks)
    a_one = jnp.where(inside, m_one * sig, 0.0).astype(BF)
    slope_one = jnp.where(inside, sig * (1.0 + m_one * (1.0 - sig)) * gain, 0.0)
    return a_one, slope_one


def second_layer(conv, cot, affine, blocks):
    lanes = affine.shape[-1]
    gain, bias = (affine[i : i + 1, :].reshape(1, 1, lanes) for i in (2, 3))
    m_two = conv * gain + bias
    pulled = [cot.get(start, count) for start, count in blocks]
    pulled = jnp.concatenate(pulled, axis=0) if len(pulled) > 1 else pulled[0]
    return pulled.astype(F32) * slope(m_two) * gain


def spread(cols, value):
    own = lax.broadcasted_iota(jnp.int32, (1,) + value.shape[1:], 1) < cols
    kept = jnp.where(own, value, 0.0)
    return jnp.concatenate([turn(kept, -1), kept, turn(kept, 1)], axis=2).astype(BF)


def cut(start, stop, parts):
    step = -(-(stop - start) // parts)
    return [(at, min(step, stop - at)) for at in range(start, stop, step)]


def pack_kernel(
    rows, cols, cache_in_at, frames_in_at, cache_mid_at, cot_at, row_near, row_far, col_near, col_far,
    cache_in, frames_in, cache_mid, cot, sems,
):
    copies = [
        pltpu.make_async_copy(source, target, sems.at[i])
        for i, (source, target) in enumerate(
            (
                (cache_in_at, cache_in),
                (frames_in_at, frames_in),
                (cache_mid_at, cache_mid),
                (cot_at, cot),
            )
        )
    ]
    odd_row, odd_col = is_odd("ha"), is_odd("wa")
    for copy in copies:
        copy.start()
    for copy in copies:
        copy.wait()
    sources = (
        (cache_in, 0), (cache_in, 1), (frames_in, 0), (cache_mid, 0), (cache_mid, 1), (cot, 0)
    )
    last = rows - RIM
    near_at, far_at = jnp.where(odd_row, 0, last), jnp.where(odd_row, last, 0)
    for frame, (ref, i) in enumerate(sources):
        row_near[frame] = ref[i, pl.ds(near_at, RIM)]
        row_far[frame] = ref[i, pl.ds(far_at, RIM)]
    lanes = col_near.shape[-1]
    lower = lax.broadcasted_iota(jnp.int32, (rows, 2 * RIM, lanes), 1) < RIM

    def edges(frame):
        ref, i = sources[frame]
        value = ref[i].astype(F32)
        return value[:, : 2 * RIM], pltpu.roll(value[:, cols - 2 * RIM :], RIM, 1)

    near, far = [], []
    for pair in range(3):
        (head, tail), (head_b, tail_b) = edges(2 * pair), edges(2 * pair + 1)
        heads = jnp.where(lower, head, pltpu.roll(head_b, RIM, 1))
        tails = jnp.where(lower, tail, pltpu.roll(tail_b, RIM, 1))
        near.append(jnp.where(odd_col, heads, tails))
        far.append(jnp.where(odd_col, tails, heads))
    col_near[...] = jnp.stack(near, axis=1).reshape(-1, lanes).astype(BF)
    col_far[...] = jnp.stack(far, axis=1).reshape(-1, lanes).astype(BF)


def corner_kernel(col_near, col_far, near, far):
    size = near.shape[0] // 2
    last = col_near.shape[0] - size
    odd = is_odd("ha")
    for target, start in (
        (near, jnp.where(odd, 0, last)),
        (far, jnp.where(odd, last, 0)),
    ):
        at = pl.ds(pl.multiple_of(start, 16), size)
        target[:size] = col_near[at]
        target[size:] = col_far[at]


def ready_kernel(
    w_one, w_two, sc_one, sh_one, sc_two, sh_two, ahead_one, ahead_two, back_one, back_two, affine
):
    lanes = affine.shape[-1]
    for weight, ahead, back in ((w_one, ahead_one, back_one), (w_two, ahead_two, back_two)):
        for a in range(3):
            for b in range(3):
                for c in range(3):
                    at = (a * 3 + b) * lanes
                    ahead[at : at + lanes, c * lanes : (c + 1) * lanes] = weight[a, b, c]
        for b in range(3):
            for c in range(3):
                back[c * lanes : (c + 1) * lanes, b * lanes : (b + 1) * lanes] = weight[2, b, c]
    affine[...] = jnp.concatenate(
        [1.0 + sc_one[...], sh_one[...], 1.0 + sc_two[...], sh_two[...]] * 2, axis=0
    )


def own_kernel(rows, cols, cache_in, frames_in, ahead_one, part_one, field):
    block = [cache_in[0], cache_in[1], frames_in[0]]
    none = jnp.zeros((rows, 2 * RIM, block[0].shape[-1]), F32)
    for i, value in enumerate(block):
        field[i] = jnp.concatenate([value.astype(F32), none], axis=1).astype(BF)
    own = [Rows((RIM, Frame(field, i), rows)) for i in range(3)]
    first = RIM + 1
    for start, count in cut(first, RIM + rows - 1, 2):
        part_one[start - first : start - first + count] = forward(
            own, ahead_one[...], [(start, count)]
        )


def middle_kernel(
    rows, cols, cache_in, frames_in, cache_mid, cot, col_near, col_far, part_one,
    ahead_one, ahead_two, affine, field, slope_mid, a_mid, d_mid, moved_mid,
):
    block = [cache_in[0], cache_in[1], frames_in[0], cache_mid[0], cache_mid[1], cot[0]]
    frames, rims = join(block, col_near[...], col_far[...])
    for frame, value in enumerate(frames):
        field[frame] = value
    first = RIM + 1
    for start, count in cut(first, RIM + rows - 1, 2):
        at = slice(start - first, start - first + count)
        conv = part_one[at] + rim_forward(rims[:3], ahead_one[...], start, count, cols)
        a_mid[at], slope_mid[at] = first_layer(rows, cols, conv, affine, [(start, count)])
    frames = [Rows((RIM, Frame(field, i), rows)) for i in (3, 4)] + [Rows((first, a_mid, rows - 2))]
    cotangent = Rows((RIM, Frame(field, 5), rows))
    second = RIM + 2
    for start, count in cut(second, RIM + rows - 2, 2):
        at = slice(start - second, start - second + count)
        conv = forward(frames, ahead_two[...], [(start, count)])
        value = second_layer(conv, cotangent, affine, [(start, count)])
        d_mid[at] = value.astype(BF)
        moved_mid[at] = spread(cols, value)


def rim_kernel(
    rows, cols, field, slope_mid, a_mid, d_mid, moved_mid, row_near, row_far, corner_near, corner_far,
    ahead_one, ahead_two, back_two, affine, keep, send, d_one,
    top, bottom, slope_rim, a_rim, d_rim, moved_rim, moved_one, grads, sems,
):
    lanes = affine.shape[-1]
    tall = rows + 2 * RIM
    core = lax.axis_index("ha") % 2
    half = corner_near.shape[0] // 2

    def assemble(target, block, corner):
        parts, _ = join([block[i] for i in range(6)], corner[:half], corner[half:])
        for frame, value in enumerate(parts):
            target[frame] = value

    @pl.when(is_odd("ha"))
    def _():
        assemble(top, row_near, corner_near)
        assemble(bottom, row_far, corner_far)

    @pl.when(jnp.logical_not(is_odd("ha")))
    def _():
        assemble(top, row_far, corner_far)
        assemble(bottom, row_near, corner_near)

    whole = [
        Rows(
            (0, Frame(top, i), RIM),
            (RIM, Frame(field, i), rows),
            (RIM + rows, Frame(bottom, i), RIM),
        )
        for i in range(6)
    ]

    def around(rim, mid, first, count):
        size = mid.shape[0]
        return Rows(
            (first, rim, count),
            (first + count, mid, size),
            (first + count + size, Shifted(rim, count), count),
        )

    used = 27 * lanes
    if grads.shape[1] > used:
        grads[:, used:, :] = jnp.zeros((2, grads.shape[1] - used, lanes), BF)
    edge = jnp.zeros((2,) + moved_rim.shape[1:], BF)
    moved_rim[0:2] = edge
    moved_rim[6:8] = edge
    moved_one[0:2] = edge
    moved_one[rows + 2 : rows + 4] = edge

    def gradient(which, frames, moved):
        lhs = jnp.concatenate([flat(frames[a].get(RIM - 1, rows + 2)) for a in range(3)], axis=1)
        for b in range(3):
            rhs = flat(moved.get(RIM - b, rows + 2))
            out = lax.dot_general(lhs, rhs, (((0,), (0,)), ((), ())), preferred_element_type=F32)
            for a in range(3):
                for c in range(3):
                    at = ((a * 3 + b) * 3 + c) * lanes
                    grads[which, at : at + lanes, :] = out[
                        a * lanes : (a + 1) * lanes, c * lanes : (c + 1) * lanes
                    ].astype(BF)

        @pl.when(core == which)
        def _():
            pltpu.make_async_copy(grads.at[which], keep, sems.at[0]).start()

        @pl.when(core != which)
        def _():
            pltpu.make_async_copy(grads.at[which], send, sems.at[1]).start()

    blocks = [(1, 4), (tall - 5, 4)]
    conv = forward(whole[:3], ahead_one[...], blocks)
    a_value, slope_value = first_layer(rows, cols, conv, affine, blocks)
    a_rim[...] = a_value
    slope_rim[...] = slope_value
    a_all = around(a_rim, a_mid, 1, 4)
    slope_all = around(slope_rim, slope_mid, 1, 4)

    frames = whole[3:5] + [a_all]
    blocks = [(2, 4), (tall - 6, 4)]
    value = second_layer(forward(frames, ahead_two[...], blocks), whole[5], affine, blocks)
    d_rim[...] = value.astype(BF)
    moved_rim[2:6] = spread(cols, value[2:6])
    d_all = around(d_rim, d_mid, 2, 4)
    gradient(1, frames, around(moved_rim, moved_mid, 2, 4))

    for start, count in cut(3, tall - 3, 2):
        value = backward(d_all, back_two, start, count) * slope_all.get(start, count)
        d_one[start - 3 : start - 3 + count] = value.astype(BF)
        low, high = max(start, RIM), min(start + count, RIM + rows)
        moved_one[low - 2 : high - 2] = spread(cols, value[low - start : high - start])
    gradient(0, whole[:3], Rows((2, moved_one, rows + 4)))

    pltpu.make_async_copy(grads.at[core], keep, sems.at[0]).wait()
    pltpu.make_async_copy(grads.at[1 - core], send, sems.at[1]).wait()


class Shifted:
    def __init__(self, ref, by):
        self.ref, self.by = ref, by

    def __getitem__(self, key):
        return self.ref[key.start + self.by : key.stop + self.by]


def input_kernel(rows, cols, d_one, back_one, gin):
    field = Rows((RIM - 1, d_one, rows + 2))
    for start, count in cut(RIM, RIM + rows, 2):
        value = backward(field, back_one, start, count)
        gin[0, start - RIM : start - RIM + count] = value[:, :cols].astype(BF)


def place_kernel(parts, first, source, *refs):
    one, other, wide, sems = refs[-4:]
    size = wide.shape[0] // parts
    own_first = jnp.logical_not(is_odd("ha"))
    to_one = own_first if first else jnp.logical_not(own_first)
    for part in range(parts):
        at = pl.ds(part * size, size)
        wide[at, :] = source[at, :].astype(F32)

        @pl.when(to_one)
        def _():
            pltpu.make_async_copy(wide.at[at], one.at[at], sems.at[part]).start()

        @pl.when(jnp.logical_not(to_one))
        def _():
            pltpu.make_async_copy(wide.at[at], other.at[at], sems.at[part]).start()

    for part in range(parts):
        at = pl.ds(part * size, size)
        pltpu.make_async_copy(wide.at[at], one.at[at], sems.at[part]).wait()


def per_device(
    frames_in, cache_in, cache_mid, w_first, w_second,
    scale_first, shift_first, scale_second, shift_second, cotangent,
):
    _, rows, cols, chans = frames_in.shape
    devices = lax.axis_size("ha") * lax.axis_size("wa")
    factor = 1.0 / (rows * cols * devices) ** 0.5
    full, tall = cols + 2 * RIM, rows + 2 * RIM
    FULL[0] = full
    chips = devices // 2
    total = 27 * chans
    share = -(-total // (8 * chips)) * 8
    inner = pl.BlockSpec(memory_space=pltpu.VMEM)
    anywhere = pl.BlockSpec(memory_space=pl.ANY)

    def shaped(*shape, dtype=BF):
        return jax.ShapeDtypeStruct(shape, dtype)

    def call(kernel, name, out_shape, mebibytes, flops, args, sizes=True, **kwargs):
        def body(*refs):
            kernel(rows, cols, *refs) if sizes else kernel(*refs)

        count = len(out_shape)
        kwargs.setdefault("in_specs", [inner] * len(args))
        kwargs.setdefault("out_specs", (inner,) * count)
        return pl.pallas_call(
            body,
            out_shape=tuple(out_shape),
            cost_estimate=pl.CostEstimate(
                flops=int(flops), bytes_accessed=8 * 10**6, transcendentals=0
            ),
            compiler_params=pltpu.CompilerParams(vmem_limit_bytes=mebibytes * 2**20),
            name=name,
            **kwargs,
        )(*args)

    fields = (cache_in, frames_in, cache_mid, cotangent)
    rim_rows, rim_cols = shaped(6, RIM, cols, chans), shaped(6 * rows * RIM, chans)
    row_near, row_far, col_near, col_far = call(
        pack_kernel, "pack", (rim_rows, rim_rows, rim_cols, rim_cols), 53, 1e9, fields,
        in_specs=[anywhere] * 4,
        scratch_shapes=[pltpu.VMEM(v.shape, BF) for v in fields] + [pltpu.SemaphoreType.DMA((4,))],
    )
    ahead, back = shaped(9 * chans, 3 * chans), shaped(3 * chans, 3 * chans)
    ahead_one, ahead_two, back_one, back_two, affine = call(
        ready_kernel, "ready", (ahead, ahead, back, back, shaped(8, chans, dtype=F32)), 10, 2e9,
        (w_first, w_second, scale_first, shift_first, scale_second, shift_second), sizes=False,
    )
    (part_one,) = call(
        own_kernel, "own", (shaped(rows - 2, full, chans, dtype=F32),),
        12, 3e9, (cache_in, frames_in, ahead_one),
        scratch_shapes=[pltpu.VMEM((3, rows, full, chans), BF)],
    )
    col_near, col_far = trade("wa", col_near, col_far)
    row_near, row_far = trade("ha", row_near, row_far)
    size = 6 * RIM * RIM
    corner_near, corner_far = trade(
        "ha",
        *call(
            corner_kernel, "corner", [shaped(2 * size, chans)] * 2, 4, 1e8, (col_near, col_far),
            sizes=False,
        ),
    )

    field, slope_mid, a_mid, d_mid, moved_mid = call(
        middle_kernel, "middle",
        (
            shaped(6, rows, full, chans),
            shaped(rows - 2, full, chans, dtype=F32),
            shaped(rows - 2, full, chans),
            shaped(rows - 4, full, chans),
            shaped(rows - 4, full, 3 * chans),
        ),
        16, 3e9, (*fields, col_near, col_far, part_one, ahead_one, ahead_two, affine),
    )
    keep, send, d_one = call(
        rim_kernel, "rim",
        (shaped(share * chips, chans), shaped(share * chips, chans), shaped(rows + 2, full, chans)),
        20, 5e9,
        (
            field, slope_mid, a_mid, d_mid, moved_mid, row_near, row_far, corner_near, corner_far,
            ahead_one, ahead_two, back_two, affine,
        ),
        out_specs=(anywhere, anywhere, inner),
        scratch_shapes=[
            pltpu.VMEM((6, RIM, full, chans), BF),
            pltpu.VMEM((6, RIM, full, chans), BF),
            pltpu.VMEM((8, full, chans), F32),
            pltpu.VMEM((8, full, chans), BF),
            pltpu.VMEM((8, full, chans), BF),
            pltpu.VMEM((8, full, 3 * chans), BF),
            pltpu.VMEM((rows + 4, full, 3 * chans), BF),
            pltpu.VMEM((2, share * chips, chans), BF),
            pltpu.SemaphoreType.DMA((2,)),
        ],
    )

    pairs, _ = swaps("ha")
    got = lax.ppermute(send, "ha", pairs)
    (grad_input,) = call(
        input_kernel, "input", (shaped(1, rows, cols, chans),), 8, 1e9, (d_one, back_one)
    )
    got, grad_input = lax.optimization_barrier((got, grad_input))
    chip_sum = (keep.astype(F32) + got.astype(F32)).astype(BF)
    cores = [[c for c in range(devices) if (c // lax.axis_size("wa")) % 2 == k] for k in range(2)]
    cores = [group[::-1] for group in cores]

    def spread_out(value):
        return lax.all_to_all(
            value.reshape(chips, share, chans), BOTH, 0, 0, axis_index_groups=cores, tiled=True
        )

    mine = (jnp.sum(spread_out(chip_sum).astype(F32), axis=0) * factor).astype(BF)
    one = spread_out(jnp.broadcast_to(mine[None], (chips, share, chans))).reshape(-1, chans)
    other = lax.ppermute(one, "ha", pairs)
    shape = (3, 3, 3, chans, chans)
    parts = 4

    def place(source, *given):
        return call(
            lambda *refs: place_kernel(parts, not given, *refs), "place",
            [shaped(total, chans, dtype=F32)] * 2, 6, 2e9, (source, *given), sizes=False,
            in_specs=[inner] + [anywhere] * len(given),
            out_specs=(anywhere, anywhere),
            scratch_shapes=[
                pltpu.VMEM((total, chans), F32), pltpu.SemaphoreType.DMA((parts,))
            ],
            input_output_aliases={1: 0, 2: 1} if given else {},
        )

    grad_first, grad_second = place(other, *place(one))
    return (grad_input, grad_first.reshape(shape), grad_second.reshape(shape))


def solution(mesh):
    tiled = P(None, "ha", "wa", None)
    return jax.shard_map(
        per_device,
        mesh=mesh,
        in_specs=(tiled, tiled, tiled, P(), P(), P(), P(), P(), P(), tiled),
        out_specs=(tiled, P(), P()),
        check_vma=False,
    )
```

```python
import jax
import jax.numpy as jnp
from jax import lax
from jax.experimental import pallas as pl
from jax.experimental.pallas import tpu as pltpu
from jax.sharding import PartitionSpec as P

BF = jnp.bfloat16
F32 = jnp.float32
RIM = 4
BOTH = ("ha", "wa")


def swaps(axis):
    count = lax.axis_size(axis)
    first = [(i, i ^ 1) for i in range(count)]
    second = [(i, i + 1 if i % 2 else i - 1) for i in range(1, count - 1)]
    return first, second


def trade(axis, near, far):
    first, second = swaps(axis)
    far = lax.ppermute(far, axis, second)
    return lax.ppermute(near, axis, first), far


def is_odd(axis):
    return lax.axis_index(axis) % 2 == 1


def slope(value):
    sig = jax.nn.sigmoid(value)
    return sig * (1.0 + value * (1.0 - sig))


def flat(value):
    return value.reshape(-1, value.shape[-1])


def turn(value, step):
    return pltpu.roll(value, step % value.shape[1], 1)


def join(block, near, far):
    high, _, lanes = block[0].shape
    odd = is_odd("wa")
    near, far = near.astype(F32), far.astype(F32)
    left = jnp.where(odd, near, far).reshape(high, 3, 2 * RIM, lanes)
    right = jnp.where(odd, far, near).reshape(high, 3, 2 * RIM, lanes)
    lower = lax.broadcasted_iota(jnp.int32, (high, 2 * RIM, lanes), 1) < RIM
    frames, rims = [], []
    for frame in range(6):
        one, other = right[:, frame // 2], left[:, frame // 2]
        if frame % 2 == 0:
            rim = jnp.where(lower, one, pltpu.roll(other, RIM, 1))
        else:
            rim = jnp.where(lower, pltpu.roll(one, RIM, 1), other)
        frames.append(jnp.concatenate([block[frame].astype(F32), rim], axis=1).astype(BF))
        rims.append(rim)
    return frames, rims


class Rows:
    def __init__(self, *pieces):
        self.pieces = pieces

    def get(self, start, count):
        out = []
        for first, ref, size in self.pieces:
            low, high = max(start, first), min(start + count, first + size)
            if low < high:
                out.append(ref[low - first : high - first])
        return out[0] if len(out) == 1 else jnp.concatenate(out, axis=0)


class Frame:
    def __init__(self, ref, index):
        self.ref, self.index = ref, index

    def __getitem__(self, key):
        return self.ref[self.index, key]


def forward(frames, weight, blocks):
    lhs = jnp.concatenate(
        [
            jnp.concatenate(
                [flat(frames[a].get(start - 1 + b, count)) for start, count in blocks], axis=0
            )
            for a in range(len(frames))
            for b in range(3)
        ],
        axis=1,
    )
    out = jnp.dot(lhs, weight, preferred_element_type=F32)
    return gather_columns(out, 1)


def rim_forward(rims, weight, start, count, cols):
    lhs = jnp.concatenate(
        [
            flat(rim[start - 1 + b - RIM : start - 1 + b - RIM + count])
            for rim in rims
            for b in range(3)
        ],
        axis=1,
    ).astype(BF)
    out = jnp.dot(lhs, weight, preferred_element_type=F32)
    lanes = out.shape[-1] // 3
    out = out.reshape(count, 2 * RIM, 3 * lanes)
    place = lax.broadcasted_iota(jnp.int32, (count, 2 * RIM, lanes), 1)
    last = 2 * RIM - 1
    from_left, from_right = turn(out[..., :lanes], 1), turn(out[..., 2 * lanes :], -1)
    here = (
        out[..., lanes : 2 * lanes]
        + jnp.where(place > 0, from_left, 0.0)
        + jnp.where(place < last, from_right, 0.0)
    )
    return jnp.concatenate(
        [
            jnp.where(place == 0, from_left, 0.0),
            jnp.zeros((count, cols - 4 * RIM, lanes), F32),
            jnp.where(place == last, from_right, 0.0),
            here,
        ],
        axis=1,
    )


def backward(field, weight, start, count):
    lhs = jnp.concatenate([flat(field.get(start + 1 - b, count)) for b in range(3)], axis=1)
    out = lax.dot_general(lhs, weight[...], (((1,), (1,)), ((), ())), preferred_element_type=F32)
    return gather_columns(out, -1)


def gather_columns(out, step):
    lanes = out.shape[-1] // 3
    out = out.reshape(-1, FULL[0], 3 * lanes)
    return (
        turn(out[..., :lanes], step)
        + out[..., lanes : 2 * lanes]
        + turn(out[..., 2 * lanes :], -step)
    )


FULL = [0]


def in_image(rows, cols, lanes, blocks):
    full = cols + 2 * RIM
    image_rows, image_cols = rows * lax.axis_size("ha"), cols * lax.axis_size("wa")
    col = lax.broadcasted_iota(jnp.int32, (1, full, lanes), 1)
    place = jnp.where(col < cols + RIM, col, col - full) + lax.axis_index("wa") * cols
    col_in = (place >= 0) & (place < image_cols)
    out = []
    for start, count in blocks:
        row = lax.broadcasted_iota(jnp.int32, (count, full, lanes), 0)
        row = row + (start - RIM) + lax.axis_index("ha") * rows
        out.append((row >= 0) & (row < image_rows) & col_in)
    return jnp.concatenate(out, axis=0) if len(out) > 1 else out[0]


def first_layer(rows, cols, conv, affine, blocks):
    lanes = affine.shape[-1]
    gain, bias = (affine[i : i + 1, :].reshape(1, 1, lanes) for i in (0, 1))
    m_one = conv * gain + bias
    sig = jax.nn.sigmoid(m_one)
    inside = in_image(rows, cols, lanes, blocks)
    a_one = jnp.where(inside, m_one * sig, 0.0).astype(BF)
    slope_one = jnp.where(inside, sig * (1.0 + m_one * (1.0 - sig)) * gain, 0.0)
    return a_one, slope_one


def second_layer(conv, cot, affine, blocks):
    lanes = affine.shape[-1]
    gain, bias = (affine[i : i + 1, :].reshape(1, 1, lanes) for i in (2, 3))
    m_two = conv * gain + bias
    pulled = [cot.get(start, count) for start, count in blocks]
    pulled = jnp.concatenate(pulled, axis=0) if len(pulled) > 1 else pulled[0]
    return pulled.astype(F32) * slope(m_two) * gain


def spread(cols, value):
    own = lax.broadcasted_iota(jnp.int32, (1,) + value.shape[1:], 1) < cols
    kept = jnp.where(own, value, 0.0)
    return jnp.concatenate([turn(kept, -1), kept, turn(kept, 1)], axis=2).astype(BF)


def cut(start, stop, parts):
    step = -(-(stop - start) // parts)
    return [(at, min(step, stop - at)) for at in range(start, stop, step)]


def pack_kernel(
    rows, cols, cache_in_at, frames_in_at, cache_mid_at, cot_at, row_near, row_far, col_near, col_far,
    cache_in, frames_in, cache_mid, cot, sems,
):
    copies = [
        pltpu.make_async_copy(source, target, sems.at[i])
        for i, (source, target) in enumerate(
            (
                (cache_in_at, cache_in),
                (frames_in_at, frames_in),
                (cache_mid_at, cache_mid),
                (cot_at, cot),
            )
        )
    ]
    odd_row, odd_col = is_odd("ha"), is_odd("wa")
    for copy in copies:
        copy.start()
    for copy in copies:
        copy.wait()
    sources = (
        (cache_in, 0), (cache_in, 1), (frames_in, 0), (cache_mid, 0), (cache_mid, 1), (cot, 0)
    )
    last = rows - RIM
    near_at, far_at = jnp.where(odd_row, 0, last), jnp.where(odd_row, last, 0)
    for frame, (ref, i) in enumerate(sources):
        row_near[frame] = ref[i, pl.ds(near_at, RIM)]
        row_far[frame] = ref[i, pl.ds(far_at, RIM)]
    lanes = col_near.shape[-1]
    lower = lax.broadcasted_iota(jnp.int32, (rows, 2 * RIM, lanes), 1) < RIM

    def edges(frame):
        ref, i = sources[frame]
        value = ref[i].astype(F32)
        return value[:, : 2 * RIM], pltpu.roll(value[:, cols - 2 * RIM :], RIM, 1)

    near, far = [], []
    for pair in range(3):
        (head, tail), (head_b, tail_b) = edges(2 * pair), edges(2 * pair + 1)
        heads = jnp.where(lower, head, pltpu.roll(head_b, RIM, 1))
        tails = jnp.where(lower, tail, pltpu.roll(tail_b, RIM, 1))
        near.append(jnp.where(odd_col, heads, tails))
        far.append(jnp.where(odd_col, tails, heads))
    col_near[...] = jnp.stack(near, axis=1).reshape(-1, lanes).astype(BF)
    col_far[...] = jnp.stack(far, axis=1).reshape(-1, lanes).astype(BF)


def corner_kernel(col_near, col_far, near, far):
    size = near.shape[0] // 2
    last = col_near.shape[0] - size
    odd = is_odd("ha")
    for target, start in (
        (near, jnp.where(odd, 0, last)),
        (far, jnp.where(odd, last, 0)),
    ):
        at = pl.ds(pl.multiple_of(start, 16), size)
        target[:size] = col_near[at]
        target[size:] = col_far[at]


def ready_kernel(
    w_one, w_two, sc_one, sh_one, sc_two, sh_two, ahead_one, ahead_two, back_one, back_two, affine
):
    lanes = affine.shape[-1]
    for weight, ahead, back in ((w_one, ahead_one, back_one), (w_two, ahead_two, back_two)):
        for a in range(3):
            for b in range(3):
                for c in range(3):
                    at = (a * 3 + b) * lanes
                    ahead[at : at + lanes, c * lanes : (c + 1) * lanes] = weight[a, b, c]
        for b in range(3):
            for c in range(3):
                back[c * lanes : (c + 1) * lanes, b * lanes : (b + 1) * lanes] = weight[2, b, c]
    affine[...] = jnp.concatenate(
        [1.0 + sc_one[...], sh_one[...], 1.0 + sc_two[...], sh_two[...]] * 2, axis=0
    )


def own_kernel(rows, cols, cache_in, frames_in, ahead_one, part_one, field):
    block = [cache_in[0], cache_in[1], frames_in[0]]
    none = jnp.zeros((rows, 2 * RIM, block[0].shape[-1]), F32)
    for i, value in enumerate(block):
        field[i] = jnp.concatenate([value.astype(F32), none], axis=1).astype(BF)
    own = [Rows((RIM, Frame(field, i), rows)) for i in range(3)]
    first = RIM + 1
    for start, count in cut(first, RIM + rows - 1, 2):
        part_one[start - first : start - first + count] = forward(
            own, ahead_one[...], [(start, count)]
        )


def middle_kernel(
    rows, cols, cache_in, frames_in, cache_mid, cot, col_near, col_far, part_one,
    ahead_one, ahead_two, affine, field, slope_mid, a_mid, d_mid, moved_mid,
):
    block = [cache_in[0], cache_in[1], frames_in[0], cache_mid[0], cache_mid[1], cot[0]]
    frames, rims = join(block, col_near[...], col_far[...])
    for frame, value in enumerate(frames):
        field[frame] = value
    first = RIM + 1
    for start, count in cut(first, RIM + rows - 1, 2):
        at = slice(start - first, start - first + count)
        conv = part_one[at] + rim_forward(rims[:3], ahead_one[...], start, count, cols)
        a_mid[at], slope_mid[at] = first_layer(rows, cols, conv, affine, [(start, count)])
    frames = [Rows((RIM, Frame(field, i), rows)) for i in (3, 4)] + [Rows((first, a_mid, rows - 2))]
    cotangent = Rows((RIM, Frame(field, 5), rows))
    second = RIM + 2
    for start, count in cut(second, RIM + rows - 2, 2):
        at = slice(start - second, start - second + count)
        conv = forward(frames, ahead_two[...], [(start, count)])
        value = second_layer(conv, cotangent, affine, [(start, count)])
        d_mid[at] = value.astype(BF)
        moved_mid[at] = spread(cols, value)


def rim_kernel(
    rows, cols, field, slope_mid, a_mid, d_mid, moved_mid, row_near, row_far, corner_near, corner_far,
    ahead_one, ahead_two, back_two, affine, keep, send, d_one,
    top, bottom, slope_rim, a_rim, d_rim, moved_rim, moved_one, grads, sems,
):
    lanes = affine.shape[-1]
    tall = rows + 2 * RIM
    core = lax.axis_index("ha") % 2
    half = corner_near.shape[0] // 2

    def assemble(target, block, corner):
        parts, _ = join([block[i] for i in range(6)], corner[:half], corner[half:])
        for frame, value in enumerate(parts):
            target[frame] = value

    @pl.when(is_odd("ha"))
    def _():
        assemble(top, row_near, corner_near)
        assemble(bottom, row_far, corner_far)

    @pl.when(jnp.logical_not(is_odd("ha")))
    def _():
        assemble(top, row_far, corner_far)
        assemble(bottom, row_near, corner_near)

    whole = [
        Rows(
            (0, Frame(top, i), RIM),
            (RIM, Frame(field, i), rows),
            (RIM + rows, Frame(bottom, i), RIM),
        )
        for i in range(6)
    ]

    def around(rim, mid, first, count):
        size = mid.shape[0]
        return Rows(
            (first, rim, count),
            (first + count, mid, size),
            (first + count + size, Shifted(rim, count), count),
        )

    used = 27 * lanes
    if grads.shape[1] > used:
        grads[:, used:, :] = jnp.zeros((2, grads.shape[1] - used, lanes), BF)
    edge = jnp.zeros((2,) + moved_rim.shape[1:], BF)
    moved_rim[0:2] = edge
    moved_rim[6:8] = edge
    moved_one[0:2] = edge
    moved_one[rows + 2 : rows + 4] = edge

    def gradient(which, frames, moved):
        rhs = jnp.concatenate([flat(moved.get(RIM - b, rows + 2)) for b in range(3)], axis=1)
        for a in range(3):
            lhs = flat(frames[a].get(RIM - 1, rows + 2))
            out = lax.dot_general(lhs, rhs, (((0,), (0,)), ((), ())), preferred_element_type=F32)
            for b in range(3):
                for c in range(3):
                    at = ((a * 3 + b) * 3 + c) * lanes
                    grads[which, at : at + lanes, :] = out[
                        :, (b * 3 + c) * lanes : (b * 3 + c + 1) * lanes
                    ].astype(BF)

        @pl.when(core == which)
        def _():
            pltpu.make_async_copy(grads.at[which], keep, sems.at[0]).start()

        @pl.when(core != which)
        def _():
            pltpu.make_async_copy(grads.at[which], send, sems.at[1]).start()

    blocks = [(1, 4), (tall - 5, 4)]
    conv = forward(whole[:3], ahead_one[...], blocks)
    a_value, slope_value = first_layer(rows, cols, conv, affine, blocks)
    a_rim[...] = a_value
    slope_rim[...] = slope_value
    a_all = around(a_rim, a_mid, 1, 4)
    slope_all = around(slope_rim, slope_mid, 1, 4)

    frames = whole[3:5] + [a_all]
    blocks = [(2, 4), (tall - 6, 4)]
    value = second_layer(forward(frames, ahead_two[...], blocks), whole[5], affine, blocks)
    d_rim[...] = value.astype(BF)
    moved_rim[2:6] = spread(cols, value[2:6])
    d_all = around(d_rim, d_mid, 2, 4)
    gradient(1, frames, around(moved_rim, moved_mid, 2, 4))

    for start, count in cut(3, tall - 3, 2):
        value = backward(d_all, back_two, start, count) * slope_all.get(start, count)
        d_one[start - 3 : start - 3 + count] = value.astype(BF)
        low, high = max(start, RIM), min(start + count, RIM + rows)
        moved_one[low - 2 : high - 2] = spread(cols, value[low - start : high - start])
    gradient(0, whole[:3], Rows((2, moved_one, rows + 4)))

    pltpu.make_async_copy(grads.at[core], keep, sems.at[0]).wait()
    pltpu.make_async_copy(grads.at[1 - core], send, sems.at[1]).wait()


class Shifted:
    def __init__(self, ref, by):
        self.ref, self.by = ref, by

    def __getitem__(self, key):
        return self.ref[key.start + self.by : key.stop + self.by]


def input_kernel(rows, cols, d_one, back_one, gin):
    field = Rows((RIM - 1, d_one, rows + 2))
    for start, count in cut(RIM, RIM + rows, 2):
        value = backward(field, back_one, start, count)
        gin[0, start - RIM : start - RIM + count] = value[:, :cols].astype(BF)


def place_kernel(parts, first, source, *refs):
    one, other, wide, sems = refs[-4:]
    size = wide.shape[0] // parts
    own_first = jnp.logical_not(is_odd("ha"))
    to_one = own_first if first else jnp.logical_not(own_first)
    for part in range(parts):
        at = pl.ds(part * size, size)
        wide[at, :] = source[at, :].astype(F32)

        @pl.when(to_one)
        def _():
            pltpu.make_async_copy(wide.at[at], one.at[at], sems.at[part]).start()

        @pl.when(jnp.logical_not(to_one))
        def _():
            pltpu.make_async_copy(wide.at[at], other.at[at], sems.at[part]).start()

    for part in range(parts):
        at = pl.ds(part * size, size)
        pltpu.make_async_copy(wide.at[at], one.at[at], sems.at[part]).wait()


def per_device(
    frames_in, cache_in, cache_mid, w_first, w_second,
    scale_first, shift_first, scale_second, shift_second, cotangent,
):
    _, rows, cols, chans = frames_in.shape
    devices = lax.axis_size("ha") * lax.axis_size("wa")
    factor = 1.0 / (rows * cols * devices) ** 0.5
    full, tall = cols + 2 * RIM, rows + 2 * RIM
    FULL[0] = full
    chips = devices // 2
    total = 27 * chans
    share = -(-total // (8 * chips)) * 8
    inner = pl.BlockSpec(memory_space=pltpu.VMEM)
    anywhere = pl.BlockSpec(memory_space=pl.ANY)

    def shaped(*shape, dtype=BF):
        return jax.ShapeDtypeStruct(shape, dtype)

    def call(kernel, name, out_shape, mebibytes, flops, args, sizes=True, **kwargs):
        def body(*refs):
            kernel(rows, cols, *refs) if sizes else kernel(*refs)

        count = len(out_shape)
        kwargs.setdefault("in_specs", [inner] * len(args))
        kwargs.setdefault("out_specs", (inner,) * count)
        return pl.pallas_call(
            body,
            out_shape=tuple(out_shape),
            cost_estimate=pl.CostEstimate(
                flops=int(flops), bytes_accessed=8 * 10**6, transcendentals=0
            ),
            compiler_params=pltpu.CompilerParams(vmem_limit_bytes=mebibytes * 2**20),
            name=name,
            **kwargs,
        )(*args)

    fields = (cache_in, frames_in, cache_mid, cotangent)
    rim_rows, rim_cols = shaped(6, RIM, cols, chans), shaped(6 * rows * RIM, chans)
    row_near, row_far, col_near, col_far = call(
        pack_kernel, "pack", (rim_rows, rim_rows, rim_cols, rim_cols), 53, 1e9, fields,
        in_specs=[anywhere] * 4,
        scratch_shapes=[pltpu.VMEM(v.shape, BF) for v in fields] + [pltpu.SemaphoreType.DMA((4,))],
    )
    ahead, back = shaped(9 * chans, 3 * chans), shaped(3 * chans, 3 * chans)
    ahead_one, ahead_two, back_one, back_two, affine = call(
        ready_kernel, "ready", (ahead, ahead, back, back, shaped(8, chans, dtype=F32)), 10, 2e9,
        (w_first, w_second, scale_first, shift_first, scale_second, shift_second), sizes=False,
    )
    (part_one,) = call(
        own_kernel, "own", (shaped(rows - 2, full, chans, dtype=F32),),
        12, 3e9, (cache_in, frames_in, ahead_one),
        scratch_shapes=[pltpu.VMEM((3, rows, full, chans), BF)],
    )
    col_near, col_far = trade("wa", col_near, col_far)
    row_near, part_one = lax.optimization_barrier((row_near, part_one))
    row_near, row_far = trade("ha", row_near, row_far)
    size = 6 * RIM * RIM
    corner_near, corner_far = trade(
        "ha",
        *call(
            corner_kernel, "corner", [shaped(2 * size, chans)] * 2, 4, 1e8, (col_near, col_far),
            sizes=False,
        ),
    )

    field, slope_mid, a_mid, d_mid, moved_mid = call(
        middle_kernel, "middle",
        (
            shaped(6, rows, full, chans),
            shaped(rows - 2, full, chans, dtype=F32),
            shaped(rows - 2, full, chans),
            shaped(rows - 4, full, chans),
            shaped(rows - 4, full, 3 * chans),
        ),
        16, 3e9, (*fields, col_near, col_far, part_one, ahead_one, ahead_two, affine),
    )
    keep, send, d_one = call(
        rim_kernel, "rim",
        (shaped(share * chips, chans), shaped(share * chips, chans), shaped(rows + 2, full, chans)),
        20, 5e9,
        (
            field, slope_mid, a_mid, d_mid, moved_mid, row_near, row_far, corner_near, corner_far,
            ahead_one, ahead_two, back_two, affine,
        ),
        out_specs=(anywhere, anywhere, inner),
        scratch_shapes=[
            pltpu.VMEM((6, RIM, full, chans), BF),
            pltpu.VMEM((6, RIM, full, chans), BF),
            pltpu.VMEM((8, full, chans), F32),
            pltpu.VMEM((8, full, chans), BF),
            pltpu.VMEM((8, full, chans), BF),
            pltpu.VMEM((8, full, 3 * chans), BF),
            pltpu.VMEM((rows + 4, full, 3 * chans), BF),
            pltpu.VMEM((2, share * chips, chans), BF),
            pltpu.SemaphoreType.DMA((2,)),
        ],
    )

    pairs, _ = swaps("ha")
    got = lax.ppermute(send, "ha", pairs)
    (grad_input,) = call(
        input_kernel, "input", (shaped(1, rows, cols, chans),), 8, 1e9, (d_one, back_one)
    )
    got, grad_input = lax.optimization_barrier((got, grad_input))
    chip_sum = (keep.astype(F32) + got.astype(F32)).astype(BF)
    cores = [[c for c in range(devices) if (c // lax.axis_size("wa")) % 2 == k] for k in range(2)]
    cores = [group[::-1] for group in cores]

    def spread_out(value):
        return lax.all_to_all(
            value.reshape(chips, share, chans), BOTH, 0, 0, axis_index_groups=cores, tiled=True
        )

    mine = (jnp.sum(spread_out(chip_sum).astype(F32), axis=0) * factor).astype(BF)
    one = spread_out(jnp.broadcast_to(mine[None], (chips, share, chans))).reshape(-1, chans)
    other = lax.ppermute(one, "ha", pairs)
    shape = (3, 3, 3, chans, chans)
    parts = 4

    def place(source, *given):
        return call(
            lambda *refs: place_kernel(parts, not given, *refs), "place",
            [shaped(total, chans, dtype=F32)] * 2, 6, 2e9, (source, *given), sizes=False,
            in_specs=[inner] + [anywhere] * len(given),
            out_specs=(anywhere, anywhere),
            scratch_shapes=[
                pltpu.VMEM((total, chans), F32), pltpu.SemaphoreType.DMA((parts,))
            ],
            input_output_aliases={1: 0, 2: 1} if given else {},
        )

    grad_first, grad_second = place(other, *place(one))
    return (grad_input, grad_first.reshape(shape), grad_second.reshape(shape))


def solution(mesh):
    tiled = P(None, "ha", "wa", None)
    return jax.shard_map(
        per_device,
        mesh=mesh,
        in_specs=(tiled, tiled, tiled, P(), P(), P(), P(), P(), P(), tiled),
        out_specs=(tiled, P(), P()),
        check_vma=False,
    )
```

```python
import jax
import jax.numpy as jnp
from jax import lax
from jax.experimental import pallas as pl
from jax.experimental.pallas import tpu as pltpu
from jax.sharding import PartitionSpec as P

BF = jnp.bfloat16
F32 = jnp.float32
RIM = 4
BOTH = ("ha", "wa")


def swaps(axis):
    count = lax.axis_size(axis)
    first = [(i, i ^ 1) for i in range(count)]
    second = [(i, i + 1 if i % 2 else i - 1) for i in range(1, count - 1)]
    return first, second


def trade(axis, near, far):
    first, second = swaps(axis)
    far = lax.ppermute(far, axis, second)
    return lax.ppermute(near, axis, first), far


def is_odd(axis):
    return lax.axis_index(axis) % 2 == 1


def slope(value):
    sig = jax.nn.sigmoid(value)
    return sig * (1.0 + value * (1.0 - sig))


def flat(value):
    return value.reshape(-1, value.shape[-1])


def turn(value, step):
    return pltpu.roll(value, step % value.shape[1], 1)


def join(block, near, far):
    high, _, lanes = block[0].shape
    odd = is_odd("wa")
    near, far = near.astype(F32), far.astype(F32)
    left = jnp.where(odd, near, far).reshape(high, 3, 2 * RIM, lanes)
    right = jnp.where(odd, far, near).reshape(high, 3, 2 * RIM, lanes)
    lower = lax.broadcasted_iota(jnp.int32, (high, 2 * RIM, lanes), 1) < RIM
    frames, rims = [], []
    for frame in range(6):
        one, other = right[:, frame // 2], left[:, frame // 2]
        if frame % 2 == 0:
            rim = jnp.where(lower, one, pltpu.roll(other, RIM, 1))
        else:
            rim = jnp.where(lower, pltpu.roll(one, RIM, 1), other)
        frames.append(jnp.concatenate([block[frame].astype(F32), rim], axis=1).astype(BF))
        rims.append(rim)
    return frames, rims


class Rows:
    def __init__(self, *pieces):
        self.pieces = pieces

    def get(self, start, count):
        out = []
        for first, ref, size in self.pieces:
            low, high = max(start, first), min(start + count, first + size)
            if low < high:
                out.append(ref[low - first : high - first])
        return out[0] if len(out) == 1 else jnp.concatenate(out, axis=0)


class Frame:
    def __init__(self, ref, index):
        self.ref, self.index = ref, index

    def __getitem__(self, key):
        return self.ref[self.index, key]


def forward(frames, weight, blocks):
    lhs = jnp.concatenate(
        [
            jnp.concatenate(
                [flat(frames[a].get(start - 1 + b, count)) for start, count in blocks], axis=0
            )
            for a in range(len(frames))
            for b in range(3)
        ],
        axis=1,
    )
    out = jnp.dot(lhs, weight, preferred_element_type=F32)
    return gather_columns(out, 1)


def rim_forward(rims, weight, start, count, cols):
    lhs = jnp.concatenate(
        [
            flat(rim[start - 1 + b - RIM : start - 1 + b - RIM + count])
            for rim in rims
            for b in range(3)
        ],
        axis=1,
    ).astype(BF)
    out = jnp.dot(lhs, weight, preferred_element_type=F32)
    lanes = out.shape[-1] // 3
    out = out.reshape(count, 2 * RIM, 3 * lanes)
    place = lax.broadcasted_iota(jnp.int32, (count, 2 * RIM, lanes), 1)
    last = 2 * RIM - 1
    from_left, from_right = turn(out[..., :lanes], 1), turn(out[..., 2 * lanes :], -1)
    here = (
        out[..., lanes : 2 * lanes]
        + jnp.where(place > 0, from_left, 0.0)
        + jnp.where(place < last, from_right, 0.0)
    )
    return jnp.concatenate(
        [
            jnp.where(place == 0, from_left, 0.0),
            jnp.zeros((count, cols - 4 * RIM, lanes), F32),
            jnp.where(place == last, from_right, 0.0),
            here,
        ],
        axis=1,
    )


def backward(field, weight, start, count):
    lhs = jnp.concatenate([flat(field.get(start + 1 - b, count)) for b in range(3)], axis=1)
    out = lax.dot_general(lhs, weight[...], (((1,), (1,)), ((), ())), preferred_element_type=F32)
    return gather_columns(out, -1)


def gather_columns(out, step):
    lanes = out.shape[-1] // 3
    out = out.reshape(-1, FULL[0], 3 * lanes)
    return (
        turn(out[..., :lanes], step)
        + out[..., lanes : 2 * lanes]
        + turn(out[..., 2 * lanes :], -step)
    )


FULL = [0]


def in_image(rows, cols, lanes, blocks):
    full = cols + 2 * RIM
    image_rows, image_cols = rows * lax.axis_size("ha"), cols * lax.axis_size("wa")
    col = lax.broadcasted_iota(jnp.int32, (1, full, lanes), 1)
    place = jnp.where(col < cols + RIM, col, col - full) + lax.axis_index("wa") * cols
    col_in = (place >= 0) & (place < image_cols)
    out = []
    for start, count in blocks:
        row = lax.broadcasted_iota(jnp.int32, (count, full, lanes), 0)
        row = row + (start - RIM) + lax.axis_index("ha") * rows
        out.append((row >= 0) & (row < image_rows) & col_in)
    return jnp.concatenate(out, axis=0) if len(out) > 1 else out[0]


def first_layer(rows, cols, conv, affine, blocks):
    lanes = affine.shape[-1]
    gain, bias = (affine[i : i + 1, :].reshape(1, 1, lanes) for i in (0, 1))
    m_one = conv * gain + bias
    sig = jax.nn.sigmoid(m_one)
    inside = in_image(rows, cols, lanes, blocks)
    a_one = jnp.where(inside, m_one * sig, 0.0).astype(BF)
    slope_one = jnp.where(inside, sig * (1.0 + m_one * (1.0 - sig)) * gain, 0.0)
    return a_one, slope_one


def second_layer(conv, cot, affine, blocks):
    lanes = affine.shape[-1]
    gain, bias = (affine[i : i + 1, :].reshape(1, 1, lanes) for i in (2, 3))
    m_two = conv * gain + bias
    pulled = [cot.get(start, count) for start, count in blocks]
    pulled = jnp.concatenate(pulled, axis=0) if len(pulled) > 1 else pulled[0]
    return pulled.astype(F32) * slope(m_two) * gain


def spread(cols, value):
    own = lax.broadcasted_iota(jnp.int32, (1,) + value.shape[1:], 1) < cols
    kept = jnp.where(own, value, 0.0)
    return jnp.concatenate([turn(kept, -1), kept, turn(kept, 1)], axis=2).astype(BF)


def cut(start, stop, parts):
    step = -(-(stop - start) // parts)
    return [(at, min(step, stop - at)) for at in range(start, stop, step)]


def pack_kernel(
    rows, cols, cache_in_at, frames_in_at, cache_mid_at, cot_at, row_near, row_far, col_near, col_far,
    cache_in, frames_in, cache_mid, cot, sems,
):
    copies = [
        pltpu.make_async_copy(source, target, sems.at[i])
        for i, (source, target) in enumerate(
            (
                (cache_in_at, cache_in),
                (frames_in_at, frames_in),
                (cache_mid_at, cache_mid),
                (cot_at, cot),
            )
        )
    ]
    odd_row, odd_col = is_odd("ha"), is_odd("wa")
    for copy in copies:
        copy.start()
    for copy in copies:
        copy.wait()
    sources = (
        (cache_in, 0), (cache_in, 1), (frames_in, 0), (cache_mid, 0), (cache_mid, 1), (cot, 0)
    )
    last = rows - RIM
    near_at, far_at = jnp.where(odd_row, 0, last), jnp.where(odd_row, last, 0)
    for frame, (ref, i) in enumerate(sources):
        row_near[frame] = ref[i, pl.ds(near_at, RIM)]
        row_far[frame] = ref[i, pl.ds(far_at, RIM)]
    lanes = col_near.shape[-1]
    lower = lax.broadcasted_iota(jnp.int32, (rows, 2 * RIM, lanes), 1) < RIM

    def edges(frame):
        ref, i = sources[frame]
        value = ref[i].astype(F32)
        return value[:, : 2 * RIM], pltpu.roll(value[:, cols - 2 * RIM :], RIM, 1)

    near, far = [], []
    for pair in range(3):
        (head, tail), (head_b, tail_b) = edges(2 * pair), edges(2 * pair + 1)
        heads = jnp.where(lower, head, pltpu.roll(head_b, RIM, 1))
        tails = jnp.where(lower, tail, pltpu.roll(tail_b, RIM, 1))
        near.append(jnp.where(odd_col, heads, tails))
        far.append(jnp.where(odd_col, tails, heads))
    col_near[...] = jnp.stack(near, axis=1).reshape(-1, lanes).astype(BF)
    col_far[...] = jnp.stack(far, axis=1).reshape(-1, lanes).astype(BF)


def corner_kernel(row_near, col_near, col_far, near, far):
    size = far.shape[0] // 2
    near[2 * size :] = flat(row_near[...])
    last = col_near.shape[0] - size
    odd = is_odd("ha")
    for target, start in (
        (near, jnp.where(odd, 0, last)),
        (far, jnp.where(odd, last, 0)),
    ):
        at = pl.ds(pl.multiple_of(start, 16), size)
        target[:size] = col_near[at]
        target[size : 2 * size] = col_far[at]


def ready_kernel(
    w_one, w_two, sc_one, sh_one, sc_two, sh_two, ahead_one, ahead_two, back_one, back_two, affine
):
    lanes = affine.shape[-1]
    for weight, ahead, back in ((w_one, ahead_one, back_one), (w_two, ahead_two, back_two)):
        for a in range(3):
            for b in range(3):
                for c in range(3):
                    at = (a * 3 + b) * lanes
                    ahead[at : at + lanes, c * lanes : (c + 1) * lanes] = weight[a, b, c]
        for b in range(3):
            for c in range(3):
                back[c * lanes : (c + 1) * lanes, b * lanes : (b + 1) * lanes] = weight[2, b, c]
    affine[...] = jnp.concatenate(
        [1.0 + sc_one[...], sh_one[...], 1.0 + sc_two[...], sh_two[...]] * 2, axis=0
    )


def own_kernel(rows, cols, cache_in, frames_in, ahead_one, part_one, field):
    block = [cache_in[0], cache_in[1], frames_in[0]]
    none = jnp.zeros((rows, 2 * RIM, block[0].shape[-1]), F32)
    for i, value in enumerate(block):
        field[i] = jnp.concatenate([value.astype(F32), none], axis=1).astype(BF)
    own = [Rows((RIM, Frame(field, i), rows)) for i in range(3)]
    first = RIM + 1
    for start, count in cut(first, RIM + rows - 1, 2):
        part_one[start - first : start - first + count] = forward(
            own, ahead_one[...], [(start, count)]
        )


def middle_kernel(
    rows, cols, cache_in, frames_in, cache_mid, cot, col_near, col_far, part_one,
    ahead_one, ahead_two, affine, field, slope_mid, a_mid, d_mid, moved_mid,
):
    block = [cache_in[0], cache_in[1], frames_in[0], cache_mid[0], cache_mid[1], cot[0]]
    frames, rims = join(block, col_near[...], col_far[...])
    for frame, value in enumerate(frames):
        field[frame] = value
    first = RIM + 1
    for start, count in cut(first, RIM + rows - 1, 2):
        at = slice(start - first, start - first + count)
        conv = part_one[at] + rim_forward(rims[:3], ahead_one[...], start, count, cols)
        a_mid[at], slope_mid[at] = first_layer(rows, cols, conv, affine, [(start, count)])
    frames = [Rows((RIM, Frame(field, i), rows)) for i in (3, 4)] + [Rows((first, a_mid, rows - 2))]
    cotangent = Rows((RIM, Frame(field, 5), rows))
    second = RIM + 2
    for start, count in cut(second, RIM + rows - 2, 2):
        at = slice(start - second, start - second + count)
        conv = forward(frames, ahead_two[...], [(start, count)])
        value = second_layer(conv, cotangent, affine, [(start, count)])
        d_mid[at] = value.astype(BF)
        moved_mid[at] = spread(cols, value)


def rim_kernel(
    rows, cols, field, slope_mid, a_mid, d_mid, moved_mid, row_far, beside, corner_far,
    ahead_one, ahead_two, back_two, affine, keep, send, d_one,
    top, bottom, slope_rim, a_rim, d_rim, moved_rim, moved_one, grads, sems,
):
    lanes = affine.shape[-1]
    tall = rows + 2 * RIM
    core = lax.axis_index("ha") % 2
    half = corner_far.shape[0] // 2

    def assemble(target, block, corner):
        parts, _ = join([block[i] for i in range(6)], corner[:half], corner[half : 2 * half])
        for frame, value in enumerate(parts):
            target[frame] = value

    row_near = beside[2 * half :].reshape(row_far.shape)

    @pl.when(is_odd("ha"))
    def _():
        assemble(top, row_near, beside)
        assemble(bottom, row_far, corner_far)

    @pl.when(jnp.logical_not(is_odd("ha")))
    def _():
        assemble(top, row_far, corner_far)
        assemble(bottom, row_near, beside)

    whole = [
        Rows(
            (0, Frame(top, i), RIM),
            (RIM, Frame(field, i), rows),
            (RIM + rows, Frame(bottom, i), RIM),
        )
        for i in range(6)
    ]

    def around(rim, mid, first, count):
        size = mid.shape[0]
        return Rows(
            (first, rim, count),
            (first + count, mid, size),
            (first + count + size, Shifted(rim, count), count),
        )

    used = 27 * lanes
    if grads.shape[1] > used:
        grads[:, used:, :] = jnp.zeros((2, grads.shape[1] - used, lanes), BF)
    edge = jnp.zeros((2,) + moved_rim.shape[1:], BF)
    moved_rim[0:2] = edge
    moved_rim[6:8] = edge
    moved_one[0:2] = edge
    moved_one[rows + 2 : rows + 4] = edge

    def gradient(which, frames, moved):
        rhs = jnp.concatenate([flat(moved.get(RIM - b, rows + 2)) for b in range(3)], axis=1)
        for a in range(3):
            lhs = flat(frames[a].get(RIM - 1, rows + 2))
            out = lax.dot_general(lhs, rhs, (((0,), (0,)), ((), ())), preferred_element_type=F32)
            for b in range(3):
                for c in range(3):
                    at = ((a * 3 + b) * 3 + c) * lanes
                    grads[which, at : at + lanes, :] = out[
                        :, (b * 3 + c) * lanes : (b * 3 + c + 1) * lanes
                    ].astype(BF)

        @pl.when(core == which)
        def _():
            pltpu.make_async_copy(grads.at[which], keep, sems.at[0]).start()

        @pl.when(core != which)
        def _():
            pltpu.make_async_copy(grads.at[which], send, sems.at[1]).start()

    blocks = [(1, 4), (tall - 5, 4)]
    conv = forward(whole[:3], ahead_one[...], blocks)
    a_value, slope_value = first_layer(rows, cols, conv, affine, blocks)
    a_rim[...] = a_value
    slope_rim[...] = slope_value
    a_all = around(a_rim, a_mid, 1, 4)
    slope_all = around(slope_rim, slope_mid, 1, 4)

    frames = whole[3:5] + [a_all]
    blocks = [(2, 4), (tall - 6, 4)]
    value = second_layer(forward(frames, ahead_two[...], blocks), whole[5], affine, blocks)
    d_rim[...] = value.astype(BF)
    moved_rim[2:6] = spread(cols, value[2:6])
    d_all = around(d_rim, d_mid, 2, 4)
    gradient(1, frames, around(moved_rim, moved_mid, 2, 4))

    for start, count in cut(3, tall - 3, 2):
        value = backward(d_all, back_two, start, count) * slope_all.get(start, count)
        d_one[start - 3 : start - 3 + count] = value.astype(BF)
        low, high = max(start, RIM), min(start + count, RIM + rows)
        moved_one[low - 2 : high - 2] = spread(cols, value[low - start : high - start])
    gradient(0, whole[:3], Rows((2, moved_one, rows + 4)))

    pltpu.make_async_copy(grads.at[core], keep, sems.at[0]).wait()
    pltpu.make_async_copy(grads.at[1 - core], send, sems.at[1]).wait()


class Shifted:
    def __init__(self, ref, by):
        self.ref, self.by = ref, by

    def __getitem__(self, key):
        return self.ref[key.start + self.by : key.stop + self.by]


def input_kernel(rows, cols, d_one, back_one, gin):
    field = Rows((RIM - 1, d_one, rows + 2))
    for start, count in cut(RIM, RIM + rows, 2):
        value = backward(field, back_one, start, count)
        gin[0, start - RIM : start - RIM + count] = value[:, :cols].astype(BF)


def place_kernel(parts, first, source, *refs):
    one, other, wide, sems = refs[-4:]
    size = wide.shape[0] // parts
    own_first = jnp.logical_not(is_odd("ha"))
    to_one = own_first if first else jnp.logical_not(own_first)
    for part in range(parts):
        at = pl.ds(part * size, size)
        wide[at, :] = source[at, :].astype(F32)

        @pl.when(to_one)
        def _():
            pltpu.make_async_copy(wide.at[at], one.at[at], sems.at[part]).start()

        @pl.when(jnp.logical_not(to_one))
        def _():
            pltpu.make_async_copy(wide.at[at], other.at[at], sems.at[part]).start()

    for part in range(parts):
        at = pl.ds(part * size, size)
        pltpu.make_async_copy(wide.at[at], one.at[at], sems.at[part]).wait()


def per_device(
    frames_in, cache_in, cache_mid, w_first, w_second,
    scale_first, shift_first, scale_second, shift_second, cotangent,
):
    _, rows, cols, chans = frames_in.shape
    devices = lax.axis_size("ha") * lax.axis_size("wa")
    factor = 1.0 / (rows * cols * devices) ** 0.5
    full, tall = cols + 2 * RIM, rows + 2 * RIM
    FULL[0] = full
    chips = devices // 2
    total = 27 * chans
    share = -(-total // (8 * chips)) * 8
    inner = pl.BlockSpec(memory_space=pltpu.VMEM)
    anywhere = pl.BlockSpec(memory_space=pl.ANY)

    def shaped(*shape, dtype=BF):
        return jax.ShapeDtypeStruct(shape, dtype)

    def call(kernel, name, out_shape, mebibytes, flops, args, sizes=True, **kwargs):
        def body(*refs):
            kernel(rows, cols, *refs) if sizes else kernel(*refs)

        count = len(out_shape)
        kwargs.setdefault("in_specs", [inner] * len(args))
        kwargs.setdefault("out_specs", (inner,) * count)
        return pl.pallas_call(
            body,
            out_shape=tuple(out_shape),
            cost_estimate=pl.CostEstimate(
                flops=int(flops), bytes_accessed=8 * 10**6, transcendentals=0
            ),
            compiler_params=pltpu.CompilerParams(vmem_limit_bytes=mebibytes * 2**20),
            name=name,
            **kwargs,
        )(*args)

    fields = (cache_in, frames_in, cache_mid, cotangent)
    rim_rows, rim_cols = shaped(6, RIM, cols, chans), shaped(6 * rows * RIM, chans)
    row_near, row_far, col_near, col_far = call(
        pack_kernel, "pack", (rim_rows, rim_rows, rim_cols, rim_cols), 53, 1e9, fields,
        in_specs=[anywhere] * 4,
        scratch_shapes=[pltpu.VMEM(v.shape, BF) for v in fields] + [pltpu.SemaphoreType.DMA((4,))],
    )
    ahead, back = shaped(9 * chans, 3 * chans), shaped(3 * chans, 3 * chans)
    ahead_one, ahead_two, back_one, back_two, affine = call(
        ready_kernel, "ready", (ahead, ahead, back, back, shaped(8, chans, dtype=F32)), 10, 2e9,
        (w_first, w_second, scale_first, shift_first, scale_second, shift_second), sizes=False,
    )
    (part_one,) = call(
        own_kernel, "own", (shaped(rows - 2, full, chans, dtype=F32),),
        12, 3e9, (cache_in, frames_in, ahead_one),
        scratch_shapes=[pltpu.VMEM((3, rows, full, chans), BF)],
    )
    col_near, col_far = trade("wa", col_near, col_far)
    row_far = lax.ppermute(row_far, "ha", swaps("ha")[1])
    row_near, part_one = lax.optimization_barrier((row_near, part_one))
    size = 6 * RIM * RIM
    beside, corner_far = trade(
        "ha",
        *call(
            corner_kernel, "corner",
            (shaped(2 * size + 6 * RIM * cols, chans), shaped(2 * size, chans)), 4, 1e8,
            (row_near, col_near, col_far), sizes=False,
        ),
    )
    part_one, row_far = lax.optimization_barrier((part_one, row_far))

    field, slope_mid, a_mid, d_mid, moved_mid = call(
        middle_kernel, "middle",
        (
            shaped(6, rows, full, chans),
            shaped(rows - 2, full, chans, dtype=F32),
            shaped(rows - 2, full, chans),
            shaped(rows - 4, full, chans),
            shaped(rows - 4, full, 3 * chans),
        ),
        16, 3e9, (*fields, col_near, col_far, part_one, ahead_one, ahead_two, affine),
    )
    keep, send, d_one = call(
        rim_kernel, "rim",
        (shaped(share * chips, chans), shaped(share * chips, chans), shaped(rows + 2, full, chans)),
        20, 5e9,
        (
            field, slope_mid, a_mid, d_mid, moved_mid, row_far, beside, corner_far,
            ahead_one, ahead_two, back_two, affine,
        ),
        out_specs=(anywhere, anywhere, inner),
        scratch_shapes=[
            pltpu.VMEM((6, RIM, full, chans), BF),
            pltpu.VMEM((6, RIM, full, chans), BF),
            pltpu.VMEM((8, full, chans), F32),
            pltpu.VMEM((8, full, chans), BF),
            pltpu.VMEM((8, full, chans), BF),
            pltpu.VMEM((8, full, 3 * chans), BF),
            pltpu.VMEM((rows + 4, full, 3 * chans), BF),
            pltpu.VMEM((2, share * chips, chans), BF),
            pltpu.SemaphoreType.DMA((2,)),
        ],
    )

    pairs, _ = swaps("ha")
    got = lax.ppermute(send, "ha", pairs)
    (grad_input,) = call(
        input_kernel, "input", (shaped(1, rows, cols, chans),), 8, 1e9, (d_one, back_one)
    )
    got, grad_input = lax.optimization_barrier((got, grad_input))
    chip_sum = (keep.astype(F32) + got.astype(F32)).astype(BF)
    cores = [[c for c in range(devices) if (c // lax.axis_size("wa")) % 2 == k] for k in range(2)]
    cores = [group[::-1] for group in cores]

    def spread_out(value):
        return lax.all_to_all(
            value.reshape(chips, share, chans), BOTH, 0, 0, axis_index_groups=cores, tiled=True
        )

    mine = (jnp.sum(spread_out(chip_sum).astype(F32), axis=0) * factor).astype(BF)
    one = spread_out(jnp.broadcast_to(mine[None], (chips, share, chans))).reshape(-1, chans)
    other = lax.ppermute(one, "ha", pairs)
    shape = (3, 3, 3, chans, chans)
    parts = 4

    def place(source, *given):
        return call(
            lambda *refs: place_kernel(parts, not given, *refs), "place",
            [shaped(total, chans, dtype=F32)] * 2, 6, 2e9, (source, *given), sizes=False,
            in_specs=[inner] + [anywhere] * len(given),
            out_specs=(anywhere, anywhere),
            scratch_shapes=[
                pltpu.VMEM((total, chans), F32), pltpu.SemaphoreType.DMA((parts,))
            ],
            input_output_aliases={1: 0, 2: 1} if given else {},
        )

    grad_first, grad_second = place(other, *place(one))
    return (grad_input, grad_first.reshape(shape), grad_second.reshape(shape))


def solution(mesh):
    tiled = P(None, "ha", "wa", None)
    return jax.shard_map(
        per_device,
        mesh=mesh,
        in_specs=(tiled, tiled, tiled, P(), P(), P(), P(), P(), P(), tiled),
        out_specs=(tiled, P(), P()),
        check_vma=False,
    )
```
